32 devices in a mesh: group: 2 (over y), gx: 4 (over z), gy: 2 (over x), gz: 2 (over core).
Axes of the slice: x: 2, y: 2, z: 4, core: 2. Of those that a mesh axis runs over, the one named last changes fastest.
Arguments:
- species: int32 [8, 2, 2, 216], P(('group', 'gx'), 'gy', 'gz'), parts along dimension 0, may hold values from 0 to 5
- counts: int32 [8, 2, 2], P(('group', 'gx'), 'gy', 'gz'), parts along dimension 0, may hold values from 27 to 216, as said below
- positions: float32 [8, 2, 2, 3, 216], P(('group', 'gx'), 'gy', 'gz'), parts along dimension 0, may hold values from 0 to 15, as said below
- ghost_rows: int32 [8, 2, 2, 152], P(('group', 'gx'), 'gy', 'gz'), parts along dimension 0, may hold values from 0 to 215, as said below
- neighbours: int32 [8, 2, 2, 26, 216], P(('group', 'gx'), 'gy', 'gz'), parts along dimension 0, may hold values from 0 to 727, as said below
- kvec: int32 [3, 4096], replicated, may hold values from -4 to 8, as said below
- embed: float32 [6, 64], replicated, may hold values from -6 to 6
- radial_one: float32 [8, 64], replicated, may hold values from -2 to 2
- radial_two: float32 [8, 64], replicated, may hold values from -2 to 2
- mix_one: float32 [64, 64], replicated, may hold values from -0.75 to 0.75
- mix_two: float32 [64, 64], replicated, may hold values from -0.75 to 0.75
- lr_filter: float32 [64, 4096], replicated, may hold values from -6 to 6
- read_weight: float32 [64, 64], replicated, may hold values from -0.75 to 0.75
- read_bias: float32 [64], replicated, may hold values from -3 to 3
- energy_weight: float32 [64], replicated, may hold values from -0.75 to 0.75
Outputs:
- energies: float32 [8, 2, 2, 216], P(('group', 'gx'), 'gy', 'gz'), parts along dimension 0
- forces: float32 [8, 2, 2, 3, 216], P(('group', 'gx'), 'gy', 'gz'), parts along dimension 0
The draws below stay inside these ranges and needn't reach their ends.
There are 2 independent parts, one for each index of `group`. The reference program is written for one: setup_inputs(seed, part) draws one part's arguments, and reference() takes and returns one part's arrays. A program takes and returns all parts, laid end to end along the dimension named above; an argument that names none is the same for every part. Nothing has to cross between parts.
Inputs may be any that keep to these rules, and one draw needn't show every extreme that they name: `counts`: every draw has a domain with 216 live slots and one with 27. `positions`: each slot of a domain sits at one site, each site holds one slot; each coordinate of an atom lies within 0.625 of its site's centre 2.5 * (s + 0.5). ghost_rows[x, y, z, g] is the slot at the g-th boundary site of the domain. `neighbours`: for a slot at site s, m runs over the 26 sites s + o with each o_d -1, 0 or 1, not all 0, in increasing order of (ox, oy, oz); a site inside the domain is named by its slot, one outside by 216 plus its extended-grid cell number. `kvec`: row 0 is 1 to 8; rows 1 and 2 are at most 4 and 4 in magnitude; each bound is reached.
All inputs are finite; a program needn't handle non-finite values.
Results may differ from the reference program's by a relative error of at most 0.0057.
Values may be sent and summed in bfloat16 or wider, within the bound.
No kernel may reach another device: no remote copies, remote signals or barrier semaphores. Data moves between devices by JAX's collectives and lax.ppermute only.
A program may use at most 128 MiB of HBM per device.

```python
import math
import jax
import jax.numpy as jnp
import numpy as np
from jax import lax

SIDE = 6
CHAN = 64
KVEC = 4096
NBASIS = 8
SPECIES = 6
NEIGH = 26
DOMX = 4
DOMY = 2
DOMZ = 2
ROWS = 216
ATOMS = 3456


def boundary_list_drawn(side):
    site_ids = np.arange(side ** 3).reshape(side, side, side)
    inner = np.zeros((side, side, side), dtype=bool)
    inner[1:side - 1, 1:side - 1, 1:side - 1] = True
    return site_ids[~inner].astype(np.int32)


def neighbour_offsets():
    steps = (-1, 0, 1)
    return np.array([(ox, oy, oz) for ox in steps for oy in steps for oz in steps if (ox, oy, oz) != (0, 0, 0)], np.int32)


def site_tables(key):
    domain_count = DOMX * DOMY * DOMZ
    slot_count = SIDE ** 3
    domain_keys = jax.random.split(jax.random.fold_in(key, 101), domain_count)
    site_of_slot = jax.vmap(lambda subkey: jax.random.permutation(subkey, slot_count))(domain_keys).astype(jnp.int32)
    slot_ids = jnp.arange(slot_count, dtype=jnp.int32)
    inverse = jax.vmap(lambda order: jnp.zeros(slot_count, jnp.int32).at[order].set(slot_ids))(site_of_slot)
    return (site_of_slot, inverse)


def draw_counts(key, part):
    key = jax.random.fold_in(key, 7)
    domain_count = DOMX * DOMY * DOMZ
    slot_count = SIDE ** 3
    subkeys = jax.random.split(key, 3)
    bucket = jax.random.randint(subkeys[0], (domain_count,), 0, 4)
    partial_fill = jax.random.randint(subkeys[1], (domain_count,), slot_count // 8, slot_count // 2 + 1)
    filled = jnp.where(bucket == 0, slot_count, partial_fill)
    full_domain = jax.random.randint(subkeys[2], (), 0, domain_count)
    filled = filled.at[full_domain].set(slot_count)
    filled = filled.at[(full_domain + 1) % domain_count].set(slot_count // 8)
    return filled.astype(jnp.int32).reshape(DOMX, DOMY, DOMZ)


def draw_positions(key, part):
    site_of_slot, inverse = site_tables(key)
    key = jax.random.fold_in(key, 3)
    coords = jnp.stack([site_of_slot // (SIDE * SIDE), site_of_slot // SIDE % SIDE, site_of_slot % SIDE], axis=1).astype(jnp.float32)
    jitter = jax.random.uniform(key, coords.shape, jnp.float32, -0.25, 0.25)
    return ((coords + 0.5 + jitter) * 2.5).reshape(DOMX, DOMY, DOMZ, 3, SIDE ** 3)


def draw_ghost_rows(key, part):
    site_of_slot, inverse = site_tables(key)
    boundary = jnp.asarray(boundary_list_drawn(SIDE))
    return inverse[:, boundary].astype(jnp.int32).reshape(DOMX, DOMY, DOMZ, -1)


def draw_neighbours(key, part):
    site_of_slot, inverse = site_tables(key)
    offsets = jnp.asarray(neighbour_offsets())
    coords = jnp.stack([site_of_slot // (SIDE * SIDE), site_of_slot // SIDE % SIDE, site_of_slot % SIDE], axis=-1)
    adjacent = coords[:, None, :, :] + offsets[None, :, None, :]
    inside = jnp.all((adjacent >= 0) & (adjacent < SIDE), axis=-1)
    flat_site = jnp.clip((adjacent[..., 0] * SIDE + adjacent[..., 1]) * SIDE + adjacent[..., 2], 0, SIDE ** 3 - 1)
    own_slot = jax.vmap(lambda table, wanted: table[wanted])(inverse, flat_site)
    ext_side = SIDE + 2
    ext_cell = SIDE ** 3 + ((adjacent[..., 0] + 1) * ext_side + adjacent[..., 1] + 1) * ext_side + adjacent[..., 2] + 1
    chosen = jnp.where(inside, own_slot, ext_cell).astype(jnp.int32)
    return chosen.reshape(DOMX, DOMY, DOMZ, 26, SIDE ** 3)


def draw_kvec(key, part):
    key = jax.random.fold_in(key, 13)
    subkeys = jax.random.split(key, 3)
    first_axis = jax.random.randint(subkeys[0], (KVEC,), 1, 2 * DOMX + 1)
    second_axis = jax.random.randint(subkeys[1], (KVEC,), -2 * DOMY, 2 * DOMY + 1)
    third_axis = jax.random.randint(subkeys[2], (KVEC,), -2 * DOMZ, 2 * DOMZ + 1)
    table = jnp.stack([first_axis, second_axis, third_axis]).astype(jnp.int32)
    table = table.at[0, 0].set(2 * DOMX).at[1, 1].set(-2 * DOMY).at[2, 2].set(-2 * DOMZ)
    return table


def touch_ends(result, own_key, least, top_value):
    longest = result.shape.index(max(result.shape))
    spots = []
    for shift in (0, 1):
        where = [jax.random.randint(jax.random.fold_in(own_key, axis), (), 0, length) for axis, length in enumerate(result.shape)]
        where[longest] = (where[longest] + shift) % result.shape[longest]
        spots.append(tuple(where))
    return result.at[spots[0]].set(least).at[spots[1]].set(top_value)


def normal_values(own_key, shape, width, reach, kind=jnp.bfloat16):
    return jnp.clip(width * jax.random.normal(own_key, shape, jnp.float32), -reach, reach).astype(kind)


def setup_inputs(seed: int = 0, part: int = 0) -> dict:
    seeds = jax.random.split(jax.random.key(seed), 16)
    part_splits = jax.random.split(jax.random.fold_in(seeds[15], part), 16)
    species = touch_ends(jax.random.randint(part_splits[0], (DOMX, DOMY, DOMZ, ROWS), 0, SPECIES), jax.random.fold_in(part_splits[0], 1), 0, SPECIES - 1).astype(jnp.int32)
    counts = draw_counts(jax.random.fold_in(jax.random.fold_in(seeds[15], part), 71), part)
    positions = draw_positions(jax.random.fold_in(jax.random.fold_in(seeds[15], part), 71), part)
    ghost_rows = draw_ghost_rows(jax.random.fold_in(jax.random.fold_in(seeds[15], part), 71), part)
    neighbours = draw_neighbours(jax.random.fold_in(jax.random.fold_in(seeds[15], part), 71), part)
    kvec = draw_kvec(jax.random.fold_in(seeds[15], 71), part)
    embed = normal_values(seeds[6], (SPECIES, CHAN), 1.0, 6.0, jnp.float32)
    radial_one = normal_values(seeds[7], (NBASIS, CHAN), NBASIS ** -0.5, 2.0, jnp.float32)
    radial_two = normal_values(seeds[8], (NBASIS, CHAN), NBASIS ** -0.5, 2.0, jnp.float32)
    mix_one = normal_values(seeds[9], (CHAN, CHAN), CHAN ** -0.5, 0.75, jnp.float32)
    mix_two = normal_values(seeds[10], (CHAN, CHAN), CHAN ** -0.5, 0.75, jnp.float32)
    lr_filter = normal_values(seeds[11], (CHAN, KVEC), 1.0, 6.0, jnp.float32)
    read_weight = normal_values(seeds[12], (CHAN, CHAN), CHAN ** -0.5, 0.75, jnp.float32)
    read_bias = normal_values(seeds[13], (CHAN,), 0.5, 3.0, jnp.float32)
    energy_weight = normal_values(seeds[14], (CHAN,), CHAN ** -0.5, 0.75, jnp.float32)
    return dict(species=species, counts=counts, positions=positions, ghost_rows=ghost_rows, neighbours=neighbours, kvec=kvec, embed=embed, radial_one=radial_one, radial_two=radial_two, mix_one=mix_one, mix_two=mix_two, lr_filter=lr_filter, read_weight=read_weight, read_bias=read_bias, energy_weight=energy_weight)


spacing = 2.5
cutoff = 5.0
two_pi = 6.283185307179586
highest = lax.Precision.HIGHEST

def boundary_list(side):
    site_ids = np.arange(side ** 3).reshape(side, side, side)
    inner = np.zeros((side, side, side), dtype=bool)
    inner[1:side - 1, 1:side - 1, 1:side - 1] = True
    return site_ids[~inner].astype(np.int32)

def radial_terms(distance):
    centres = cutoff * jnp.arange(NBASIS).astype(jnp.float32) / (NBASIS - 1)
    sharpness = (NBASIS / cutoff) ** 2
    gap_value = distance[None] - centres[:, None, None]
    gaussian = jnp.exp(-sharpness * gap_value * gap_value)
    envelope_base = jnp.maximum(1.0 - distance * distance / (cutoff * cutoff), 0.0)
    envelope = envelope_base * envelope_base
    envelope_slope = -4.0 * distance * envelope_base / (cutoff * cutoff)
    radial_value = gaussian * envelope[None]
    radial_slope = gaussian * (envelope_slope[None] - 2.0 * sharpness * gap_value * envelope[None])
    return (radial_value, radial_slope)

def embed_codes(type_code, embed):
    species_ids = jnp.arange(1, embed.shape[0] + 1, dtype=jnp.int32).astype(type_code.dtype)
    one_hot = (type_code[None, :] == species_ids[:, None]).astype(jnp.float32)
    return jnp.dot(embed.T, one_hot, precision=highest, preferred_element_type=jnp.float32)

def cell_shift():
    ext_side = SIDE + 2
    cells = jnp.arange(ext_side ** 3, dtype=jnp.int32)
    coords = jnp.stack([cells // (ext_side * ext_side), cells // ext_side % ext_side, cells % ext_side])
    domain_width = SIDE * spacing
    return jnp.where(coords == 0, -domain_width, jnp.where(coords == ext_side - 1, domain_width, 0.0)).astype(jnp.float32)

def pair_geometry(coords_own, pool_coords, pair_lists):
    separation = jnp.take(pool_coords, pair_lists, axis=1) - coords_own[:, None, :]
    distance = jnp.sqrt(lax.optimization_barrier(jnp.sum(separation * separation, axis=0)))
    return (separation, distance)

def message_forward(pool_values, pair_lists, radial_value, radial_weight):
    radial_filter = jnp.einsum('bc,bma->cma', radial_weight, radial_value, precision=highest)
    neighbour_value = jnp.take(pool_values, pair_lists, axis=1)
    return lax.optimization_barrier(jnp.sum(radial_filter * neighbour_value, axis=1))

def message_backward(grad_message, pool_values, pair_lists, radial_value, radial_slope, radial_weight, separation, distance, pool_size, with_features):
    neighbour_value = jnp.take(pool_values, pair_lists, axis=1)
    contracted = jnp.einsum('bc,cma->bma', radial_weight, grad_message[:, None, :] * neighbour_value, precision=highest)
    energy_slope = lax.optimization_barrier(jnp.sum(radial_slope * contracted, axis=0))
    pair_force = separation * (energy_slope / distance)[None]
    flat_index = pair_lists.reshape(-1)
    grad_pool = jnp.zeros((3, pool_size), jnp.float32).at[:, flat_index].add(pair_force.reshape(3, -1))
    grad_own = -lax.optimization_barrier(jnp.sum(pair_force, axis=1))
    if with_features:
        radial_filter = jnp.einsum('bc,bma->cma', radial_weight, radial_value, precision=highest)
        spread = (radial_filter * grad_message[:, None, :]).reshape(radial_filter.shape[0], -1)
        feature_pool = jnp.zeros((radial_filter.shape[0], pool_size), jnp.float32).at[:, flat_index].add(spread)
        return (grad_pool, grad_own, feature_pool)
    return (grad_pool, grad_own, grad_pool)

def phase_table(fraction, wave_numbers):
    phase_angle = two_pi * (fraction[0][:, None] * wave_numbers[0][None, :] + fraction[1][:, None] * wave_numbers[1][None, :] + fraction[2][:, None] * wave_numbers[2][None, :])
    return (jnp.cos(phase_angle).astype(jnp.bfloat16), jnp.sin(phase_angle).astype(jnp.bfloat16))

def read_long(cosine_low, sine_low, filtered):
    dims = (((1,), (1,)), ((), ()))
    return lax.dot_general(filtered[0], cosine_low, dims, preferred_element_type=jnp.float32) + lax.dot_general(filtered[1], sine_low, dims, preferred_element_type=jnp.float32)

def long_forces(cosine_low, sine_low, grad_low, rounded_one, filtered, back_filtered, wave_factors):
    dims = (((0,), (0,)), ((), ()))
    stacked_left = jnp.concatenate([grad_low, rounded_one], axis=0)
    real_part = lax.dot_general(stacked_left, jnp.concatenate([filtered[0], back_filtered[0]], axis=0), dims, preferred_element_type=jnp.float32)
    imag_part = lax.dot_general(stacked_left, jnp.concatenate([filtered[1], back_filtered[1]], axis=0), dims, preferred_element_type=jnp.float32)
    turning = cosine_low.astype(jnp.float32) * imag_part - sine_low.astype(jnp.float32) * real_part
    return lax.dot_general(wave_factors, turning, (((1,), (1,)), ((), ())), precision=highest, preferred_element_type=jnp.float32)

def domain_index(domain):
    return (domain // (DOMY * DOMZ), domain // DOMZ % DOMY, domain % DOMZ)

def whole_grid(per_domain, ghost_slots, boundary):
    features = per_domain.shape[1]

    def place_one(values, slot_rows):
        picked = jnp.take(values, slot_rows, axis=1)
        return jnp.zeros((features, SIDE ** 3), values.dtype).at[:, boundary].set(picked)
    domain_grids = jax.vmap(place_one)(per_domain, ghost_slots).reshape(DOMX, DOMY, DOMZ, features, SIDE, SIDE, SIDE)
    assembled = domain_grids.transpose(3, 0, 4, 1, 5, 2, 6).reshape(features, DOMX * SIDE, DOMY * SIDE, DOMZ * SIDE)
    return jnp.pad(assembled, ((0, 0), (1, 1), (1, 1), (1, 1)), mode='wrap')

def extended(padded, domain):
    index_x, index_y, index_z = domain_index(domain)
    anchor = (jnp.zeros((), jnp.int32), index_x * SIDE, index_y * SIDE, index_z * SIDE)
    piece = lax.dynamic_slice(padded, anchor, (padded.shape[0], SIDE + 2, SIDE + 2, SIDE + 2))
    return piece.reshape(padded.shape[0], -1)

def add_extended(running, grads, domain):
    index_x, index_y, index_z = domain_index(domain)
    anchor = (jnp.zeros((), jnp.int32), index_x * SIDE, index_y * SIDE, index_z * SIDE)
    extent = (running.shape[0], SIDE + 2, SIDE + 2, SIDE + 2)
    piece = lax.dynamic_slice(running, anchor, extent) + grads.reshape(extent)
    return lax.dynamic_update_slice(running, piece, anchor)

def unwrap(padded):
    for axis_number in (1, 2, 3):
        inner_size = padded.shape[axis_number] - 2
        low_slab = lax.slice_in_dim(padded, 0, 1, axis=axis_number)
        high_slab = lax.slice_in_dim(padded, inner_size + 1, inner_size + 2, axis=axis_number)
        inner = lax.slice_in_dim(padded, 1, inner_size + 1, axis=axis_number)
        first_layer = lax.slice_in_dim(inner, 0, 1, axis=axis_number) + high_slab
        last_layer = lax.slice_in_dim(inner, inner_size - 1, inner_size, axis=axis_number) + low_slab
        middle = lax.slice_in_dim(inner, 1, inner_size - 1, axis=axis_number)
        padded = jnp.concatenate([first_layer, middle, last_layer], axis=axis_number)
    return padded

def to_rows(padded_grad, ghost_slots, boundary):
    assembled = unwrap(padded_grad)
    features = assembled.shape[0]
    domain_grids = assembled.reshape(features, DOMX, SIDE, DOMY, SIDE, DOMZ, SIDE).transpose(1, 3, 5, 0, 2, 4, 6)
    domain_grids = domain_grids.reshape(DOMX * DOMY * DOMZ, features, SIDE ** 3)

    def place_one(site_grid, slot_rows):
        return jnp.zeros((features, SIDE ** 3), site_grid.dtype).at[:, slot_rows].add(site_grid[:, boundary])
    return jax.vmap(place_one)(domain_grids, ghost_slots)

def reference(species, counts, positions, ghost_rows, neighbours, kvec, embed, radial_one, radial_two, mix_one, mix_two, lr_filter, read_weight, read_bias, energy_weight):
    domain_count = DOMX * DOMY * DOMZ
    slot_count = SIDE ** 3
    pool_size = slot_count + (SIDE + 2) ** 3
    pair_scale = 1.0 / math.sqrt(NEIGH)
    wave_scale = 1.0 / math.sqrt(KVEC * ATOMS)
    domain_width = SIDE * spacing
    box_length = (DOMX * domain_width, DOMY * domain_width, DOMZ * domain_width)
    boundary = jnp.asarray(boundary_list(SIDE))
    domains = jnp.arange(domain_count, dtype=jnp.int32)
    species_flat = species.reshape(domain_count, slot_count)
    occupied = (jnp.arange(slot_count, dtype=jnp.int32)[None, :] < counts.reshape(domain_count, 1)).astype(jnp.float32)
    coords_own = positions.reshape(domain_count, 3, slot_count)
    ghost_slots = ghost_rows.reshape(domain_count, -1)
    pair_lists = neighbours.reshape(domain_count, NEIGH, slot_count)
    cell_offset = cell_shift()
    type_code = jnp.where(occupied > 0, species_flat + 1, 0)
    hidden_zero = jax.vmap(lambda codes: embed_codes(codes, embed))(species_flat + 1)
    masked_zero = hidden_zero * occupied[:, None, :]
    coords_grid = whole_grid(coords_own, ghost_slots, boundary)
    code_grid = whole_grid(type_code[:, None, :], ghost_slots, boundary)

    def geometry(domain):
        pool_coords = jnp.concatenate([coords_own[domain], extended(coords_grid, domain) + cell_offset], axis=1)
        separation, distance = pair_geometry(coords_own[domain], pool_coords, pair_lists[domain])
        radial_value, radial_slope = radial_terms(distance)
        return (separation, distance, radial_value, radial_slope)

    def pool_zero(domain):
        return jnp.concatenate([masked_zero[domain], embed_codes(extended(code_grid, domain)[0], embed)], axis=1)

    def layer_one(domain):
        separation, distance, radial_value, radial_slope = geometry(domain)
        message = message_forward(pool_zero(domain), pair_lists[domain], radial_value, radial_one)
        return hidden_zero[domain] + pair_scale * jnp.dot(mix_one.T, message, precision=highest, preferred_element_type=jnp.float32)
    hidden_one = lax.map(layer_one, domains)
    masked_one = hidden_one * occupied[:, None, :]
    rounded_one = masked_one.astype(jnp.bfloat16)
    masked_grid = whole_grid(masked_one, ghost_slots, boundary)
    wave_numbers = kvec.astype(jnp.float32)
    wave_factors = jnp.stack([two_pi * wave_numbers[axis_id] / box_length[axis_id] for axis_id in range(3)])

    def phases(domain):
        domain_pos = domain_index(domain)
        fraction = jnp.stack([(domain_pos[axis_id].astype(jnp.float32) * domain_width + coords_own[domain, axis_id]) / box_length[axis_id] for axis_id in range(3)])
        return phase_table(fraction, wave_numbers)

    def sum_structure(values):

        def add_one(running, domain):
            cosine_low, sine_low = phases(domain)
            term = jnp.stack([jnp.dot(values[domain], cosine_low, preferred_element_type=jnp.float32), jnp.dot(values[domain], sine_low, preferred_element_type=jnp.float32)])
            return (running + term, None)
        return lax.scan(add_one, jnp.zeros((2, CHAN, KVEC), jnp.float32), domains)[0]
    structure = sum_structure(rounded_one)
    filtered = (structure * lr_filter[None] * wave_scale).astype(jnp.bfloat16)

    def pool_one(domain):
        return jnp.concatenate([masked_one[domain], extended(masked_grid, domain)], axis=1)

    def forward_two(domain):
        cosine_low, sine_low = phases(domain)
        long_part = read_long(cosine_low, sine_low, filtered)
        separation, distance, radial_value, radial_slope = geometry(domain)
        message = message_forward(pool_one(domain), pair_lists[domain], radial_value, radial_two)
        hidden_two = hidden_one[domain] + pair_scale * jnp.dot(mix_two.T, message, precision=highest, preferred_element_type=jnp.float32) + long_part
        activation = jnp.dot(read_weight.T, hidden_two, precision=highest, preferred_element_type=jnp.float32) + read_bias[:, None]
        gating = jax.nn.sigmoid(activation)
        energy = occupied[domain] * lax.optimization_barrier(jnp.sum(activation * gating * energy_weight[:, None], axis=0))
        grad_act = occupied[domain][None] * energy_weight[:, None] * gating * (1.0 + activation * (1.0 - gating))
        grad_two = jnp.dot(read_weight, grad_act, precision=highest, preferred_element_type=jnp.float32)
        return (energy, grad_two)
    energies, grad_two = lax.map(forward_two, domains)
    grad_low = grad_two.astype(jnp.bfloat16)
    grad_structure = sum_structure(grad_low)
    back_filtered = (grad_structure * lr_filter[None] * wave_scale).astype(jnp.bfloat16)
    padded_shape = (CHAN + 3, DOMX * SIDE + 2, DOMY * SIDE + 2, DOMZ * SIDE + 2)

    def backward_two(running, domain):
        cosine_low, sine_low = phases(domain)
        grad_long = occupied[domain][None] * read_long(cosine_low, sine_low, back_filtered)
        force_long = long_forces(cosine_low, sine_low, grad_low[domain], rounded_one[domain], filtered, back_filtered, wave_factors)
        separation, distance, radial_value, radial_slope = geometry(domain)
        grad_message = pair_scale * jnp.dot(mix_two, grad_two[domain], precision=highest, preferred_element_type=jnp.float32)
        grad_pool, grad_own, feature_pool = message_backward(grad_message, pool_one(domain), pair_lists[domain], radial_value, radial_slope, radial_two, separation, distance, pool_size, True)
        combined = jnp.concatenate([feature_pool, grad_pool], axis=0)
        running = add_extended(running, combined[:, slot_count:], domain)
        return (running, (grad_long, force_long, grad_own, combined[:, :slot_count]))
    padded_two, (grad_long, force_long, grad_own_two, own_two) = lax.scan(backward_two, jnp.zeros(padded_shape, jnp.float32), domains)
    returned_two = to_rows(padded_two, ghost_slots, boundary)
    grad_one = grad_two + grad_long + occupied[:, None, :] * (own_two[:, :CHAN] + returned_two[:, :CHAN])

    def backward_one(running, domain):
        separation, distance, radial_value, radial_slope = geometry(domain)
        grad_message = pair_scale * jnp.dot(mix_one, grad_one[domain], precision=highest, preferred_element_type=jnp.float32)
        grad_pool, grad_own, unused = message_backward(grad_message, pool_zero(domain), pair_lists[domain], radial_value, radial_slope, radial_one, separation, distance, pool_size, False)
        running = add_extended(running, grad_pool[:, slot_count:], domain)
        return (running, grad_own + grad_pool[:, :slot_count])
    padded_one, layer_one_grad = lax.scan(backward_one, jnp.zeros((3,) + padded_shape[1:], jnp.float32), domains)
    returned_one = to_rows(padded_one, ghost_slots, boundary)
    total_grad = layer_one_grad + returned_one + force_long + grad_own_two + own_two[:, CHAN:] + returned_two[:, CHAN:]
    forces = -total_grad
    return (energies.reshape(DOMX, DOMY, DOMZ, slot_count), forces.reshape(DOMX, DOMY, DOMZ, 3, slot_count))
```

```python
import math

import jax
import jax.numpy as jnp
import numpy as np
from jax import lax
from jax.experimental import pallas as pl
from jax.experimental.pallas import tpu as pltpu
from jax.sharding import PartitionSpec as P

SIDE = 6
KVEC = 4096
NBASIS = 8
NEIGH = 26


spacing = 2.5
cutoff = 5.0
two_pi = 6.283185307179586
highest = lax.Precision.HIGHEST


def passed_along(block, axis, distance):
    devices = range(lax.axis_size(axis))
    route = [((i - distance) % len(devices), i) for i in devices]
    return lax.ppermute(block, axis, route)


def extended(block, sides, width):
    for axis, dim in sides:
        count = lax.axis_size(axis)
        forward = [(i, i + 1) for i in range(count - 1)]
        forward.append((count - 1, 0))
        backward = [(target, source) for source, target in forward]
        low = lax.ppermute(
            lax.slice_in_dim(block, block.shape[dim] - width, None, axis=dim), axis, forward
        )
        high = lax.ppermute(lax.slice_in_dim(block, 0, width, axis=dim), axis, backward)
        block = jnp.concatenate([low, block, high], axis=dim)
    return block


def rows_per_block():
    return SIDE * SIDE


def boundary_list(side):
    site_ids = np.arange(side**3).reshape(side, side, side)
    inner = np.zeros((side, side, side), dtype=bool)
    inner[1 : side - 1, 1 : side - 1, 1 : side - 1] = True
    return site_ids[~inner].astype(np.int32)


def radial_terms(distance):
    centres = cutoff * jnp.arange(NBASIS).astype(jnp.float32) / (NBASIS - 1)
    sharpness = (NBASIS / cutoff) ** 2
    gap_value = distance[None] - centres[:, None, None]
    gaussian = jnp.exp(-sharpness * gap_value * gap_value)
    envelope_base = jnp.maximum(1.0 - distance * distance / (cutoff * cutoff), 0.0)
    envelope = envelope_base * envelope_base
    envelope_slope = -4.0 * distance * envelope_base / (cutoff * cutoff)
    radial_value = gaussian * envelope[None]
    radial_slope = gaussian * (envelope_slope[None] - 2.0 * sharpness * gap_value * envelope[None])
    return (radial_value, radial_slope)


def embed_codes(type_code, embed):
    species_ids = jnp.arange(1, embed.shape[0] + 1, dtype=jnp.int32).astype(type_code.dtype)
    one_hot = (type_code[None, :] == species_ids[:, None]).astype(jnp.float32)
    return jnp.dot(embed.T, one_hot, precision=highest, preferred_element_type=jnp.float32)


def cell_shift():
    ext_side = SIDE + 2
    cells = jnp.arange(ext_side**3, dtype=jnp.int32)
    coords = jnp.stack(
        [cells // (ext_side * ext_side), cells // ext_side % ext_side, cells % ext_side]
    )
    domain_width = SIDE * spacing
    return jnp.where(
        coords == 0, -domain_width, jnp.where(coords == ext_side - 1, domain_width, 0.0)
    ).astype(jnp.float32)


def pair_geometry(coords_own, pool_coords, pair_lists):
    separation = jnp.take(pool_coords, pair_lists, axis=1) - coords_own[:, None, :]
    distance = jnp.sqrt(jnp.sum(separation * separation, axis=0))
    return (separation, distance)


def message_forward(pool_values, pair_lists, radial_value, radial_weight):
    radial_filter = jnp.einsum("bc,bma->cma", radial_weight, radial_value, precision=highest)
    neighbour_value = jnp.take(pool_values, pair_lists, axis=1)
    return jnp.sum(radial_filter * neighbour_value, axis=1)


def message_backward(
    grad_message,
    pool_values,
    pair_lists,
    radial_value,
    radial_slope,
    radial_weight,
    separation,
    distance,
    pool_size,
    with_features,
):
    neighbour_value = jnp.take(pool_values, pair_lists, axis=1)
    contracted = jnp.einsum(
        "bc,cma->bma", radial_weight, grad_message[:, None, :] * neighbour_value, precision=highest
    )
    energy_slope = jnp.sum(radial_slope * contracted, axis=0)
    pair_force = separation * (energy_slope / distance)[None]
    flat_index = pair_lists.reshape(-1)
    grad_pool = (
        jnp.zeros((3, pool_size), jnp.float32).at[:, flat_index].add(pair_force.reshape(3, -1))
    )
    grad_own = -jnp.sum(pair_force, axis=1)
    if with_features:
        radial_filter = jnp.einsum("bc,bma->cma", radial_weight, radial_value, precision=highest)
        spread = (radial_filter * grad_message[:, None, :]).reshape(radial_filter.shape[0], -1)
        feature_pool = (
            jnp.zeros((radial_filter.shape[0], pool_size), jnp.float32)
            .at[:, flat_index]
            .add(spread)
        )
        return (grad_pool, grad_own, feature_pool)
    return (grad_pool, grad_own, grad_pool)


def phase_table(fraction, wave_numbers):
    phase_angle = two_pi * (
        fraction[0][:, None] * wave_numbers[0][None, :]
        + fraction[1][:, None] * wave_numbers[1][None, :]
        + fraction[2][:, None] * wave_numbers[2][None, :]
    )
    return (jnp.cos(phase_angle).astype(jnp.bfloat16), jnp.sin(phase_angle).astype(jnp.bfloat16))


def read_long(cosine_low, sine_low, filtered):
    dims = (((1,), (1,)), ((), ()))
    return lax.dot_general(
        filtered[0], cosine_low, dims, preferred_element_type=jnp.float32
    ) + lax.dot_general(filtered[1], sine_low, dims, preferred_element_type=jnp.float32)


def block_live(step_index, live_count):
    block_rows = rows_per_block()
    per_member = SIDE**3 // block_rows
    first_row = (step_index % per_member * block_rows).astype(jnp.float32)
    return first_row < live_count[step_index // per_member]


def lr_struct(fraction, row_values, live_count, wave_numbers):
    block_rows = rows_per_block()
    blocks = fraction.shape[1] // block_rows

    def step(step_index, running):

        def work(running):
            offset = step_index * block_rows
            frac_block = lax.dynamic_slice_in_dim(fraction, offset, block_rows, 1)
            feature_block = lax.dynamic_slice_in_dim(row_values, offset, block_rows, 1)
            cosine_low, sine_low = phase_table(frac_block, wave_numbers)
            term = jnp.stack(
                [
                    jnp.dot(feature_block, cosine_low, preferred_element_type=jnp.float32),
                    jnp.dot(feature_block, sine_low, preferred_element_type=jnp.float32),
                ]
            )
            return running + term

        return lax.cond(
            block_live(step_index, live_count), work, lambda unchanged: unchanged, running
        )

    initial = jnp.zeros((2, row_values.shape[0], wave_numbers.shape[1]), jnp.float32)
    return lax.fori_loop(0, blocks, step, initial)


def lr_read(fraction, live_count, wave_numbers, filtered):
    block_rows = rows_per_block()
    blocks = fraction.shape[1] // block_rows

    def step(step_index, result):

        def work(result):
            offset = step_index * block_rows
            cosine_low, sine_low = phase_table(
                lax.dynamic_slice_in_dim(fraction, offset, block_rows, 1), wave_numbers
            )
            return lax.dynamic_update_slice_in_dim(
                result, read_long(cosine_low, sine_low, filtered), offset, 1
            )

        return lax.cond(
            block_live(step_index, live_count), work, lambda unchanged: unchanged, result
        )

    initial = jnp.zeros((filtered.shape[1], fraction.shape[1]), jnp.float32)
    return lax.fori_loop(0, blocks, step, initial)


def lr_back(
    fraction,
    rounded_rows,
    grad_rows,
    occupied_rows,
    live_count,
    wave_numbers,
    wave_factors,
    filtered,
    back_filtered,
):
    block_rows = rows_per_block()
    blocks = fraction.shape[1] // block_rows
    dims = (((0,), (0,)), ((), ()))
    right_real = jnp.concatenate([filtered[0], back_filtered[0]], axis=0)
    right_imag = jnp.concatenate([filtered[1], back_filtered[1]], axis=0)

    def step(step_index, carried):

        def work(carried):
            grad_long, force_long = carried
            offset = step_index * block_rows
            cosine_low, sine_low = phase_table(
                lax.dynamic_slice_in_dim(fraction, offset, block_rows, 1), wave_numbers
            )
            mask_block = lax.dynamic_slice_in_dim(occupied_rows, offset, block_rows, 0)
            grad_block = mask_block[None] * read_long(cosine_low, sine_low, back_filtered)
            stacked_left = jnp.concatenate(
                [
                    lax.dynamic_slice_in_dim(grad_rows, offset, block_rows, 1),
                    lax.dynamic_slice_in_dim(rounded_rows, offset, block_rows, 1),
                ],
                axis=0,
            )
            real_part = lax.dot_general(
                stacked_left, right_real, dims, preferred_element_type=jnp.float32
            )
            imag_part = lax.dot_general(
                stacked_left, right_imag, dims, preferred_element_type=jnp.float32
            )
            turning = (
                cosine_low.astype(jnp.float32) * imag_part
                - sine_low.astype(jnp.float32) * real_part
            )
            force_block = lax.dot_general(
                wave_factors,
                turning,
                (((1,), (1,)), ((), ())),
                precision=highest,
                preferred_element_type=jnp.float32,
            )
            return (
                lax.dynamic_update_slice_in_dim(grad_long, grad_block, offset, 1),
                lax.dynamic_update_slice_in_dim(force_long, force_block, offset, 1),
            )

        return lax.cond(
            block_live(step_index, live_count), work, lambda unchanged: unchanged, carried
        )

    initial = (
        jnp.zeros((rounded_rows.shape[0], fraction.shape[1]), jnp.float32),
        jnp.zeros((3, fraction.shape[1]), jnp.float32),
    )
    return lax.fori_loop(0, blocks, step, initial)


def boundary_grid(values, ghost_slots, boundary):
    picked = jnp.take(values, ghost_slots, axis=1)
    site_grid = jnp.zeros((values.shape[0], SIDE**3), values.dtype).at[:, boundary].set(picked)
    return site_grid.reshape(values.shape[0], SIDE, SIDE, SIDE)


def fold_slab(site_grid, axis_number, from_left, from_right):
    inner_size = site_grid.shape[axis_number] - 2
    inner = lax.slice_in_dim(site_grid, 1, inner_size + 1, axis=axis_number)
    first_layer = lax.slice_in_dim(inner, 0, 1, axis=axis_number) + from_left
    last_layer = lax.slice_in_dim(inner, inner_size - 1, inner_size, axis=axis_number) + from_right
    middle = lax.slice_in_dim(inner, 1, inner_size - 1, axis=axis_number)
    return jnp.concatenate([first_layer, middle, last_layer], axis=axis_number)


def return_halo(site_grid):
    edge = site_grid.shape[3] - 1
    received = [
        passed_along(
            lax.slice_in_dim(site_grid, slab_start, slab_start + 1, axis=3), "gz", direction
        )
        for direction, slab_start in ((1, edge), (-1, 0))
    ]
    site_grid = fold_slab(site_grid, 3, received[0], received[1])
    edge = site_grid.shape[2] - 1
    received = [
        passed_along(
            lax.slice_in_dim(site_grid, slab_start, slab_start + 1, axis=2), "gy", direction
        )
        for direction, slab_start in ((1, edge), (-1, 0))
    ]
    site_grid = fold_slab(site_grid, 2, received[0], received[1])
    edge = site_grid.shape[1] - 1
    received = [
        passed_along(
            lax.slice_in_dim(site_grid, slab_start, slab_start + 1, axis=1), "gx", direction
        )
        for direction, slab_start in ((1, edge), (-1, 0))
    ]
    return fold_slab(site_grid, 1, received[0], received[1])


def ghost_to_rows(site_grid, ghost_slots, boundary):
    features = site_grid.shape[0]
    picked = site_grid.reshape(features, -1)[:, boundary]
    return jnp.zeros((features, SIDE**3), site_grid.dtype).at[:, ghost_slots].add(picked)


def local(
    species,
    counts,
    positions,
    ghost_rows,
    neighbours,
    kvec,
    embed,
    radial_one,
    radial_two,
    mix_one,
    mix_two,
    lr_filter,
    read_weight,
    read_bias,
    energy_weight,
):
    slot_count = SIDE**3
    ext_side = SIDE + 2
    pool_size = slot_count + ext_side**3
    pair_scale = 1.0 / math.sqrt(NEIGH)
    domain_width = SIDE * spacing
    mesh_sizes = (lax.axis_size("gx"), lax.axis_size("gy"), lax.axis_size("gz"))
    box_length = tuple((count_along * domain_width for count_along in mesh_sizes))
    wave_scale = 1.0 / math.sqrt(
        KVEC * (slot_count * mesh_sizes[0] * mesh_sizes[1] * mesh_sizes[2])
    )
    species_flat = species.reshape(slot_count)
    live_total = counts.reshape(())
    coords_own = positions.reshape(3, slot_count)
    ghost_slots = ghost_rows.reshape(-1)
    pair_lists = neighbours.reshape(NEIGH, slot_count)
    boundary = jnp.asarray(boundary_list(SIDE))
    cell_offset = cell_shift()
    occupied = (jnp.arange(slot_count, dtype=jnp.int32) < live_total).astype(jnp.float32)
    type_code = jnp.where(occupied > 0, species_flat + 1, 0).astype(jnp.float32)
    hidden_zero = embed_codes(species_flat + 1, embed)
    masked_zero = hidden_zero * occupied[None]
    packet = boundary_grid(
        jnp.concatenate([coords_own, type_code[None]], axis=0), ghost_slots, boundary
    )
    ext_atoms = extended(packet, (("gx", 1), ("gy", 2), ("gz", 3)), 1).reshape(4, -1)
    pool_coords = jnp.concatenate([coords_own, ext_atoms[:3] + cell_offset], axis=1)
    pool_zero = jnp.concatenate([masked_zero, embed_codes(ext_atoms[3], embed)], axis=1)
    separation, distance = pair_geometry(coords_own, pool_coords, pair_lists)
    radial_value, radial_slope = radial_terms(distance)
    message = message_forward(pool_zero, pair_lists, radial_value, radial_one)
    hidden_one = hidden_zero + pair_scale * jnp.dot(
        mix_one.T, message, precision=highest, preferred_element_type=jnp.float32
    )
    masked_one = hidden_one * occupied[None]
    rounded_one = masked_one.astype(jnp.bfloat16)
    domain_pos = (lax.axis_index("gx"), lax.axis_index("gy"), lax.axis_index("gz"))
    fraction = jnp.stack(
        [
            (domain_pos[axis_id].astype(jnp.float32) * domain_width + coords_own[axis_id])
            / box_length[axis_id]
            for axis_id in range(3)
        ]
    )
    wave_numbers = kvec.astype(jnp.float32)
    wave_factors = jnp.stack(
        [two_pi * wave_numbers[axis_id] / box_length[axis_id] for axis_id in range(3)]
    )
    own_count = jnp.sum(occupied)[None]
    share_size = KVEC // (mesh_sizes[0] * mesh_sizes[1] * mesh_sizes[2])
    share_start = lax.axis_index(("gx", "gy", "gz")) * share_size
    filter_share = lax.dynamic_slice_in_dim(lr_filter, share_start, share_size, 1)
    struct_part = lax.psum_scatter(
        lr_struct(fraction, rounded_one, own_count, wave_numbers),
        ("gx", "gy", "gz"),
        scatter_dimension=2,
        tiled=True,
    )
    filtered = lax.all_gather(
        (struct_part * filter_share[None] * wave_scale).astype(jnp.bfloat16),
        ("gx", "gy", "gz"),
        axis=2,
        tiled=True,
    )
    long_part = lr_read(fraction, own_count, wave_numbers, filtered)
    masked_ext = extended(
        boundary_grid(masked_one, ghost_slots, boundary).astype(jnp.bfloat16),
        (("gx", 1), ("gy", 2), ("gz", 3)),
        1,
    ).astype(jnp.float32)
    pool_one = jnp.concatenate([masked_one, masked_ext.reshape(masked_one.shape[0], -1)], axis=1)
    message_two = message_forward(pool_one, pair_lists, radial_value, radial_two)
    hidden_two = (
        hidden_one
        + pair_scale
        * jnp.dot(mix_two.T, message_two, precision=highest, preferred_element_type=jnp.float32)
        + long_part
    )
    activation = (
        jnp.dot(read_weight.T, hidden_two, precision=highest, preferred_element_type=jnp.float32)
        + read_bias[:, None]
    )
    gating = jax.nn.sigmoid(activation)
    energies = occupied * jnp.sum(activation * gating * energy_weight[:, None], axis=0)
    grad_act = (
        occupied[None] * energy_weight[:, None] * gating * (1.0 + activation * (1.0 - gating))
    )
    grad_two = jnp.dot(read_weight, grad_act, precision=highest, preferred_element_type=jnp.float32)
    grad_low = grad_two.astype(jnp.bfloat16)
    grad_part = lax.psum_scatter(
        lr_struct(fraction, grad_low, own_count, wave_numbers),
        ("gx", "gy", "gz"),
        scatter_dimension=2,
        tiled=True,
    )
    back_filtered = lax.all_gather(
        (grad_part * filter_share[None] * wave_scale).astype(jnp.bfloat16),
        ("gx", "gy", "gz"),
        axis=2,
        tiled=True,
    )
    grad_long, force_long = lr_back(
        fraction,
        rounded_one,
        grad_low,
        occupied,
        own_count,
        wave_numbers,
        wave_factors,
        filtered,
        back_filtered,
    )
    grad_message = pair_scale * jnp.dot(
        mix_two, grad_two, precision=highest, preferred_element_type=jnp.float32
    )
    grad_pool, grad_own_two, feature_pool = message_backward(
        grad_message,
        pool_one,
        pair_lists,
        radial_value,
        radial_slope,
        radial_two,
        separation,
        distance,
        pool_size,
        True,
    )
    combined = jnp.concatenate([feature_pool, grad_pool], axis=0)
    features = combined.shape[0]
    returned_two = ghost_to_rows(
        return_halo(combined[:, slot_count:].reshape(features, ext_side, ext_side, ext_side)),
        ghost_slots,
        boundary,
    )
    own_two = combined[:, :slot_count]
    channels = masked_one.shape[0]
    grad_one = (
        grad_two + grad_long + occupied[None] * (own_two[:channels] + returned_two[:channels])
    )
    grad_message_one = pair_scale * jnp.dot(
        mix_one, grad_one, precision=highest, preferred_element_type=jnp.float32
    )
    grad_pool_one, grad_own_one, unused = message_backward(
        grad_message_one,
        pool_zero,
        pair_lists,
        radial_value,
        radial_slope,
        radial_one,
        separation,
        distance,
        pool_size,
        False,
    )
    layer_one_grad = grad_own_one + grad_pool_one[:, :slot_count]
    returned_one = ghost_to_rows(
        return_halo(grad_pool_one[:, slot_count:].reshape(3, ext_side, ext_side, ext_side)),
        ghost_slots,
        boundary,
    )
    total_grad = (
        layer_one_grad
        + returned_one
        + force_long
        + grad_own_two
        + own_two[channels:]
        + returned_two[channels:]
    )
    forces = -total_grad
    return (energies.reshape(1, 1, 1, slot_count), forces.reshape(1, 1, 1, 3, slot_count))


offsets = tuple(
    (ox, oy, oz)
    for ox in (0, 1)
    for oy in (-1, 0, 1)
    for oz in (-1, 0, 1)
    if (ox, oy, oz) > (0, 0, 0)
)
half = len(offsets)
slots = SIDE**3
ext = SIDE + 2
cells = ext**3
chan = 64
grid_dims = (4, 2, 2)
domains = 16
planes = 8
rows_all = slots * planes
waves = 648
table = 2 * waves
pad = 256
gamma = (NBASIS / cutoff) ** 2
step = cutoff / (NBASIS - 1)
nt = (((1,), (1,)), ((), ()))
nn = (((1,), (0,)), ((), ()))
f32 = jnp.float32
bf16 = jnp.bfloat16


def dot(left, right, dims=nn, precision=None):
    return lax.dot_general(left, right, dims, precision=precision, preferred_element_type=f32)


def split(value):
    high = value.astype(bf16)
    return high, (value - high.astype(f32)).astype(bf16)


def dot_split(left, high, low):
    left_high, left_low = split(left)
    return dot(left_high, high) + dot(left_low, high) + dot(left_high, low)


def site_of(coords):
    where = (coords * (1.0 / spacing)).astype(jnp.int32)
    return (where[0:1] * SIDE + where[1:2]) * SIDE + where[2:3]


def iota(shape, dim):
    return lax.broadcasted_iota(jnp.int32, shape, dim)


def place_kernel(count_ref, pos_ref, species_ref, out_ref):
    coords = pos_ref[...]
    live = iota((1, slots), 1) < count_ref[0]
    code = jnp.where(live, species_ref[...] + 1, 0).astype(f32)
    data = jnp.concatenate([coords, code], axis=0)
    hot = (iota((slots, slots), 0) == site_of(coords)).astype(f32)
    out_ref[...] = dot(data, hot, nt, highest)


def twice(block):
    zero = jnp.zeros_like(block)
    return jnp.concatenate(
        [jnp.concatenate([block, zero], axis=1), jnp.concatenate([zero, block], axis=1)], axis=0
    )


def weights_kernel(
    kvec_ref,
    filter_ref,
    embed_ref,
    one_ref,
    two_ref,
    mix_one_ref,
    mix_two_ref,
    read_ref,
    gain_ref,
    radial_ref,
    embed_out,
    mix_ref,
    act_ref,
    grad_ref,
    back_ref,
    pair_ref,
):
    pair_scale = 1.0 / math.sqrt(NEIGH)
    wave_scale = 1.0 / math.sqrt(KVEC * slots * domains)
    waves_in = kvec_ref[...]

    def folded(row):
        return jnp.where(row > 0, 2 * row - 1, -2 * row)

    index = (folded(waves_in[1:2]) * 9 + folded(waves_in[2:3])) * 8 + waves_in[0:1] - 1
    filter_high, filter_low = split(filter_ref[...] * wave_scale)
    parts = jnp.concatenate([filter_high, filter_low], axis=0)
    gain = jnp.zeros((waves, 2 * chan), f32)
    width = 1024
    for start in range(0, KVEC, width):
        hot = (iota((waves, width), 0) == index[:, start : start + width]).astype(f32).astype(bf16)
        gain = gain + dot(hot, parts[:, start : start + width], nt)
    gain = (gain[:, :chan] + gain[:, chan:]).reshape(waves // 8, 8, chan)
    gain_ref[...] = jnp.concatenate([gain, gain], axis=1).reshape(table, chan)

    centre = step * iota((NBASIS, 1), 0).astype(f32)
    fall = jnp.exp(-gamma * centre * centre)
    rows = iota((pad, pad), 0)
    columns = iota((pad, pad), 1)
    kept = (rows // 128) == (columns % 128 // chan)

    def spread(block):
        return jnp.broadcast_to(block[:, None, :], (NBASIS, 16, chan)).reshape(128, chan)

    def wide(left, right):
        left, right = spread(left), spread(right)
        line = jnp.concatenate([left, left, right, right], axis=1)
        return jnp.concatenate([line, line], axis=0)

    radial = wide(one_ref[...] * fall, two_ref[...] * fall)
    for offset in range(half):
        radial_ref[offset] = jnp.where(kept & (rows % 16 == offset), radial, 0.0).astype(bf16)
    table_rows = jnp.concatenate([embed_ref[...], jnp.zeros((2, chan), f32)], axis=0)
    high = table_rows.astype(bf16).astype(f32)
    species_rows = kept & (rows % 16 == half)
    embeds = jnp.where(species_rows, wide(high, table_rows - high), 0.0).astype(bf16)
    lives = jnp.where(species_rows[:, :128], 1.0, 0.0).astype(bf16)
    embed_out[...] = jnp.concatenate([embeds, lives], axis=1)

    def put(ref, value):
        value_high, value_low = split(value)
        ref[0] = value_high
        ref[1] = value_low

    mix_two = mix_two_ref[...]
    read = read_ref[...]
    both = dot(mix_two, read, nn, highest) * pair_scale
    put(mix_ref, twice(mix_one_ref[...] * pair_scale))
    put(act_ref, jnp.concatenate([twice(read), twice(both)], axis=0))
    put(grad_ref, jnp.concatenate([twice(read.T), twice(both.T)], axis=1))
    put(back_ref, mix_one_ref[...].T * pair_scale)
    pairs = jnp.concatenate([two_ref[...], two_ref[...], one_ref[...], one_ref[...]], axis=1)
    pairs_high = pairs.astype(bf16).astype(f32)
    pair_ref[...] = jnp.concatenate([pairs_high, pairs - pairs_high], axis=0).astype(bf16)


def turn(fraction):
    rest = fraction - jnp.floor(fraction + 0.5)
    angle = rest * (0.5 * two_pi)
    square = angle * angle
    sine = angle * (
        1.0
        + square
        * (
            -1.0 / 6
            + square
            * (
                1.0 / 120
                + square * (-1.0 / 5040 + square * (1.0 / 362880 - square * (1.0 / 39916800)))
            )
        )
    )
    cosine = 1.0 + square * (
        -0.5
        + square
        * (
            1.0 / 24
            + square
            * (
                -1.0 / 720
                + square
                * (1.0 / 40320 + square * (-1.0 / 3628800 + square * (1.0 / 479001600)))
            )
        )
    )
    return 1.0 - 2.0 * sine * sine, 2.0 * sine * cosine


def fan(base, step_pairs):
    real, imag = base
    out = [(real, imag)]
    for cosine, sine in step_pairs:
        a, b, c, d = real * cosine, imag * sine, real * sine, imag * cosine
        out.append((a - b, c + d))
        out.append((a + b, d - c))
    return out


def wave_tile(coords, store):
    frac = [coords[axis] / (grid_dims[axis] * SIDE * spacing) for axis in range(3)]
    row = iota((8, 128), 0)
    base = turn(frac[0] * (row + 1).astype(f32))
    rest = turn(jnp.where(row < 4, frac[1], frac[2]) * (row % 4 + 1).astype(f32))

    def line(index):
        return tuple(jnp.broadcast_to(part[index : index + 1], (8, 128)) for part in rest)

    y_lines = [line(index) for index in range(4)]
    z_lines = [line(index + 4) for index in range(4)]
    index = 0
    for level in fan(base, y_lines):
        for real, imag in fan(level, z_lines):
            store(index, jnp.concatenate([real, imag], axis=0).astype(bf16))
            index += 1


def swap_lanes(value):
    return pltpu.roll(value, chan, value.ndim - 1)


def swap_planes(value):
    up = pltpu.roll(value, 1, 1)
    down = pltpu.roll(value, planes - 1, 1)
    return jnp.where(iota(value.shape, 1) % 2 == 0, down, up)


def as_three(value):
    return value.reshape((-1,) + value.shape[-2:])


def fill_ghosts(ref):
    inner = slice(1, SIDE + 1)
    for ghost, source, shift in ((0, SIDE, 2), (SIDE + 1, 1, planes - 2)):
        value = ref[source, inner, inner]
        ref[ghost, inner, inner] = pltpu.roll(as_three(value), shift, 1).reshape(value.shape)
    for ghost, source in ((0, SIDE), (SIDE + 1, 1)):
        value = ref[:, source, inner]
        ref[:, ghost, inner] = swap_planes(as_three(value)).reshape(value.shape)
    for ghost, source in ((0, SIDE), (SIDE + 1, 1)):
        value = ref[:, :, source]
        ref[:, :, ghost] = swap_lanes(as_three(value)).reshape(value.shape)


def fold_ghosts(ref):
    inner = slice(1, SIDE + 1)
    for ghost, target in ((SIDE + 1, 1), (0, SIDE)):
        value = ref[:, :, ghost]
        ref[:, :, target] = ref[:, :, target] + swap_lanes(as_three(value)).reshape(value.shape)
    for ghost, target in ((SIDE + 1, 1), (0, SIDE)):
        value = ref[:, ghost, inner]
        ref[:, target, inner] = ref[:, target, inner] + swap_planes(as_three(value)).reshape(
            value.shape
        )
    for ghost, target, shift in ((SIDE + 1, 1, 2), (0, SIDE, planes - 2)):
        value = ref[ghost, inner, inner]
        ref[target, inner, inner] = ref[target, inner, inner] + pltpu.roll(
            as_three(value), shift, 1
        ).reshape(value.shape)


def inner_rows(ref):
    inner = slice(1, SIDE + 1)
    return ref[inner, inner, inner].reshape(rows_all, 128)


def set_inner(ref, value):
    inner = slice(1, SIDE + 1)
    ref[inner, inner, inner] = value.reshape(SIDE, SIDE, SIDE, planes, 128)


def convolve(filters, layer, source, target):
    target[...] = jnp.zeros(target.shape, f32)
    lanes = slice(layer * 128, layer * 128 + 128)
    groups = {}
    for number, (ox, oy, oz) in enumerate(offsets):
        groups.setdefault((ox, oy), []).append((number, oz))

    def body(line, carry):
        x = line // SIDE
        y = line % SIDE
        own = [source[x + 1, y + 1, z + 1] for z in range(SIDE)]
        own_sum = [jnp.zeros((planes, 128), f32)] * SIDE
        for (ox, oy), members in groups.items():
            there = [source[x + 1 + ox, y + 1 + oy, z] for z in range(ext)]
            sums = [None] * ext
            for z in range(SIDE):
                for number, oz in members:
                    first = pl.multiple_of((line * SIDE + z) * planes, planes)
                    weight = filters[number, pl.ds(first, planes), lanes]
                    own_sum[z] = own_sum[z] + weight * there[z + 1 + oz]
                    term = weight * own[z]
                    spot = z + 1 + oz
                    sums[spot] = term if sums[spot] is None else sums[spot] + term
            for z in range(ext):
                if sums[z] is not None:
                    target[x + 1 + ox, y + 1 + oy, z] = target[x + 1 + ox, y + 1 + oy, z] + sums[z]
        for z in range(SIDE):
            target[x + 1, y + 1, z + 1] = target[x + 1, y + 1, z + 1] + own_sum[z]
        return carry

    lax.fori_loop(0, SIDE * SIDE, body, 0)
    fold_ghosts(target)


def box_kernel(
    place_ref,
    all_ref,
    pos_ref,
    gain_ref,
    radial_ref,
    embed_ref,
    mix_ref,
    act_ref,
    grad_ref,
    back_ref,
    pair_ref,
    bias_ref,
    energy_ref,
    out_ref,
    sep_ref,
    sites_ref,
    basis_ref,
    filters_ref,
    waves_ref,
    ring_ref,
    zero_ref,
    one_ref,
    two_ref,
    sum_ref,
    packed_ref,
    shift_ref,
    own_ref,
):
    home = [place_ref[axis] for axis in range(3)]
    sites_ref[...] = jnp.zeros((4 * domains, pad), f32)
    for number in range(domains):
        spot = [
            lax.rem(home[axis] + part, grid_dims[axis])
            for axis, part in enumerate((number // 4, number // 2 % 2, number % 2))
        ]
        sites_ref[number * 4 : number * 4 + 4, 0:slots] = all_ref[
            (spot[0] * 2 + spot[1]) * 2 + spot[2]
        ]
    sites = sites_ref[:, 0:slots]

    lane = iota((1, cells), 1)
    coords = [lane // (ext * ext), lane // ext % ext, lane % ext]
    wrapped = [(value + SIDE - 1) % SIDE for value in coords]
    wrapped_site = (wrapped[0] * SIDE + wrapped[1]) * SIDE + wrapped[2]
    inside = coords[0] >= 0
    for value in coords:
        inside = inside & (value > 0) & (value < ext - 1)
    hot_all = iota((slots, cells), 0) == wrapped_site
    grown = dot(sites, hot_all.astype(f32), nn, highest)
    picks = (hot_all & inside).astype(f32)

    back16 = jnp.concatenate([grown[48:], grown[:48]], axis=0)
    ahead16 = jnp.concatenate([grown[16:], grown[:16]], axis=0)
    grown = jnp.where(coords[0] == 0, back16, jnp.where(coords[0] == ext - 1, ahead16, grown))
    swapped = jnp.concatenate(
        [grown[8 * (part ^ 1) : 8 * (part ^ 1) + 8] for part in range(8)], axis=0
    )
    grown = jnp.where((coords[1] == 0) | (coords[1] == ext - 1), swapped, grown)
    swapped = pltpu.roll(grown.reshape(8, 8, cells), 4, 1).reshape(64, cells)
    grown = jnp.where((coords[2] == 0) | (coords[2] == ext - 1), swapped, grown)
    component = iota((64, cells), 0) % 4
    domain_width = SIDE * spacing
    for axis in range(3):
        moved = jnp.where(
            coords[axis] == 0,
            -domain_width,
            jnp.where(coords[axis] == ext - 1, domain_width, 0.0),
        )
        grown = grown + jnp.where(component == axis, moved, 0.0)
    own_ext = grown[0:4]
    tiles = cells // 128

    def put_sep(number, value):
        for tile in range(tiles):
            sep_ref[tile, pl.ds(number, 64, stride=16), :] = value[:, tile * 128 : tile * 128 + 128]

    def get_sep(window):
        return jnp.concatenate([sep_ref[tile, window, :] for tile in range(tiles)], axis=1)

    for number, (ox, oy, oz) in enumerate(offsets):
        distance = (ox * ext + oy) * ext + oz
        put_sep(number, pltpu.roll(grown, cells - distance, 1) - grown)
    for number in range(half, 16):
        put_sep(number, grown)

    picks_low = picks.astype(bf16)
    row16 = iota((16, cells), 0)

    def basis_of(domain):
        first = pl.multiple_of(domain * 64, 64)
        sx, sy, sz, codes = [get_sep(pl.ds(first + 16 * part, 16)) for part in range(4)]
        square = sx * sx + sy * sy + sz * sz
        near = jnp.minimum(jnp.sqrt(square), cutoff)
        base = jnp.maximum(1.0 - square * (1.0 / (cutoff * cutoff)), 0.0)
        value = jnp.exp(-gamma * jnp.minimum(square, cutoff * cutoff)) * base * base
        ratio = jnp.exp((2.0 * gamma * step) * near)
        out = []
        for number in range(NBASIS):
            hit = jnp.where(codes == number + 1.0, 1.0, 0.0)
            out.append(jnp.where(row16 == half, hit, value))
            value = value * ratio
        return jnp.concatenate(out, axis=0).astype(bf16)

    def basis_step(plane, carry):
        both = jnp.concatenate([basis_of(2 * plane), basis_of(2 * plane + 1)], axis=0)
        picked = dot(picks_low, both, nt)
        for tile in range(2):
            basis_ref[tile, pl.ds(plane, slots, stride=planes), :] = picked[
                :, tile * 128 : tile * 128 + 128
            ]
        return carry

    lax.fori_loop(0, planes, basis_step, 0)

    def wave_step(plane, carry):
        for part in range(2):
            for tile in range(2):
                lanes = slice(tile * 128, tile * 128 + 128)
                block = sites_ref[pl.ds(pl.multiple_of(plane * 8, 8), 8), lanes]
                coords_here = [block[part * 4 + axis : part * 4 + axis + 1] for axis in range(3)]
                coords_here[0] = coords_here[0] + (plane // 2).astype(f32) * domain_width
                coords_here[1] = coords_here[1] + (plane % 2).astype(f32) * domain_width
                coords_here[2] = coords_here[2] + part * domain_width
                start = pl.multiple_of(plane * pad + tile * 128, 128)

                def store(index, value):
                    waves_ref[part, index * 16 : index * 16 + 16, pl.ds(start, 128)] = value

                wave_tile(coords_here, store)
        return carry

    lax.fori_loop(0, planes, wave_step, 0)
    for tile in range(cells // 128):
        lanes = slice(tile * 128, tile * 128 + 128)

        def store(index, value):
            ring_ref[index * 16 : index * 16 + 16, lanes] = value

        wave_tile([own_ext[axis : axis + 1, lanes] for axis in range(3)], store)

    basis_low = jnp.concatenate([basis_ref[0], basis_ref[1]], axis=1).astype(bf16)
    for number in range(half):
        filters_ref[number] = dot(basis_low, radial_ref[number])
    start_values = dot(basis_low, embed_ref[...])
    rows_ref = basis_ref.at[0]
    live_ref = basis_ref.at[1]
    live_ref[...] = start_values[:, 256:384]
    set_inner(zero_ref, start_values[:, :128] + start_values[:, 128:256])
    fill_ghosts(zero_ref)
    convolve(filters_ref, 0, zero_ref, sum_ref)
    first_rows = inner_rows(zero_ref) + live_ref[...] * dot_split(
        inner_rows(sum_ref), mix_ref[0], mix_ref[1]
    )
    set_inner(one_ref, first_rows)
    rows_ref[...] = first_rows
    fill_ghosts(one_ref)

    def pack_rows():
        for plane in range(planes):
            value = rows_ref[pl.ds(plane, slots, stride=planes), :]
            packed_ref[plane * pad : plane * pad + pad, :] = jnp.concatenate(
                [value, jnp.zeros((pad - slots, 128), f32)], axis=0
            ).astype(bf16)

    def structure():
        low = dot(waves_ref[0], packed_ref[...])
        high = dot(waves_ref[1], packed_ref[...])
        return (low[:, :chan] + high[:, chan:]) * gain_ref[...]

    pack_rows()
    own_ref[...] = jnp.zeros(own_ref.shape, f32)
    own_ref[0, 0:slots] = rows_ref[pl.ds(0, slots, stride=planes), :]
    filtered = structure()
    filtered_rows = filtered.T.astype(bf16)
    long_rows = jnp.concatenate(
        [dot(filtered_rows, waves_ref[0]), dot(filtered_rows, waves_ref[1])], axis=0
    )
    for plane in range(planes):
        turned = long_rows[:, plane * pad : plane * pad + pad].T
        rows_ref[pl.ds(plane, slots, stride=planes), :] = turned[:slots]
    convolve(filters_ref, 1, one_ref, sum_ref)
    joined = jnp.concatenate([inner_rows(one_ref) + rows_ref[...], inner_rows(sum_ref)], axis=1)
    act = dot_split(joined, act_ref[0], act_ref[1]) + bias_ref[...]
    sig = 1.0 / (1.0 + jnp.exp(-act))
    weighted = live_ref[...] * energy_ref[...] * sig
    rows_ref[...] = weighted * act
    own_energy = rows_ref[pl.ds(0, slots, stride=planes), :]
    first_half = jnp.where(iota((8, 128), 1) < chan, 1.0, 0.0)
    site_energy = dot(first_half, own_energy, nt, highest)[0:1]
    grads = dot_split(weighted * (1.0 + act * (1.0 - sig)), grad_ref[0], grad_ref[1])
    rows_ref[...] = grads[:, :128]
    set_inner(two_ref, grads[:, 128:])
    fill_ghosts(two_ref)
    pack_rows()
    own_ref[1, 0:slots] = rows_ref[pl.ds(0, slots, stride=planes), :]
    back = structure()
    back_rows = back.T.astype(bf16)
    flat = (cells * planes, 128)
    own_cells = pl.ds(0, cells, stride=planes)
    one_cells = one_ref.reshape(flat)[own_cells, :][:, :chan]
    two_cells = two_ref.reshape(flat)[own_cells, :][:, :chan]
    zero_cells = zero_ref.reshape(flat)[own_cells, :][:, :chan]
    convolve(filters_ref, 1, two_ref, sum_ref)
    set_inner(sum_ref, rows_ref[...] + live_ref[...] * inner_rows(sum_ref))
    fill_ghosts(sum_ref)
    sum_cells = sum_ref.reshape(flat)[own_cells, :][:, :chan]
    live_cells = jnp.where(own_ext[3:4] > 0, 1.0, 0.0)
    ring_long = (dot(back_rows, ring_ref[...]) * live_cells).T
    grad_cells = dot_split(sum_cells + ring_long, back_ref[0], back_ref[1])

    def crossed(value):
        value = value.reshape(waves // 8, 2, 8, chan)
        value = jnp.concatenate([value[:, 1:2], -value[:, 0:1]], axis=1).reshape(table, chan)
        return jnp.concatenate([value, jnp.zeros((table, chan), f32)], axis=1).astype(bf16)

    response = dot(crossed(filtered), own_ref[1].astype(bf16), nt) + dot(
        crossed(back), own_ref[0].astype(bf16), nt
    )
    turning_high, turning_low = split(waves_ref[0, :, 0:pad].astype(f32) * response)
    spot = iota((8, table), 1)
    wave = spot // 16 * 8 + spot % 8

    def signed(index):
        return jnp.where(index % 2 == 1, (index + 1) // 2, -(index // 2))

    row = iota((8, table), 0)
    number = jnp.where(
        row == 0,
        wave % 8 + 1,
        jnp.where(row == 1, signed(wave // 72), jnp.where(row == 2, signed(wave // 8 % 9), 0)),
    )
    number = number.astype(f32).astype(bf16)
    scale_row = iota((8, 1), 0)
    scales = jnp.where(
        scale_row == 0,
        two_pi / (grid_dims[0] * domain_width),
        two_pi / (grid_dims[1] * domain_width),
    )
    long_force = (dot(number, turning_high) + dot(number, turning_low))[:, :slots] * scales

    left = [
        jnp.concatenate([two_cells, one_cells], axis=1),
        jnp.concatenate([grad_cells, zero_cells], axis=1),
    ]
    right = jnp.concatenate(
        [
            jnp.concatenate([one_cells, two_cells], axis=1),
            jnp.concatenate([zero_cells, grad_cells], axis=1),
        ],
        axis=1,
    )
    shift_ref[0:cells] = right
    shift_ref[cells:] = jnp.zeros((shift_ref.shape[0] - cells, 256), f32)
    left = jnp.concatenate(left, axis=1)
    centre = step * iota((8, cells), 0).astype(f32)
    sep = [get_sep(slice(16 * part, 16 * part + 16)) for part in range(3)]
    square = sep[0] * sep[0] + sep[1] * sep[1] + sep[2] * sep[2]
    length = jnp.sqrt(square)
    inverse = 1.0 / length
    base = jnp.maximum(1.0 - square * (1.0 / (cutoff * cutoff)), 0.0)
    inward = length * base * (-4.0 / (cutoff * cutoff))
    outward = (-2.0 * gamma) * base * base
    totals = [jnp.zeros((1, cells), f32)] * 3
    for number, (ox, oy, oz) in enumerate(offsets):
        distance = (ox * ext + oy) * ext + oz
        products = (left * shift_ref[distance : distance + cells]).astype(bf16)
        shares = dot(pair_ref[...], products, nt)
        shares = shares[:8] + shares[8:]
        row = slice(number, number + 1)
        gap = length[row] - centre
        slope = jnp.exp(-gamma * gap * gap) * (inward[row] + gap * outward[row])
        strength = jnp.sum(slope * shares, axis=0, keepdims=True) * inverse[row]
        for part in range(3):
            force = sep[part][row] * strength
            totals[part] = totals[part] + pltpu.roll(force, distance, 1) - force
    total = jnp.concatenate(totals + [jnp.zeros((5, cells), f32)], axis=0)
    site_total = dot(total, picks, nt, highest)
    lines = jnp.concatenate([-(site_total[0:3] + long_force[0:3]), site_energy], axis=0)
    lines = jnp.concatenate([lines, jnp.zeros((4, slots), f32)], axis=0)
    hot = (iota((slots, slots), 0) == site_of(pos_ref[...])).astype(f32)
    out_ref[...] = dot(lines, hot, nn, highest)


def kernel_params():
    return pltpu.CompilerParams(vmem_limit_bytes=63 * 1024 * 1024)


def whole_box(
    species,
    counts,
    positions,
    ghost_rows,
    neighbours,
    kvec,
    embed,
    radial_one,
    radial_two,
    mix_one,
    mix_two,
    lr_filter,
    read_weight,
    read_bias,
    energy_weight,
):
    axes = ("gx", "gy", "gz")
    coords = positions.reshape(3, slots)
    vmem = pl.BlockSpec(memory_space=pltpu.VMEM)
    smem = pl.BlockSpec(memory_space=pltpu.SMEM)
    placed = pl.pallas_call(
        place_kernel,
        out_shape=jax.ShapeDtypeStruct((4, slots), f32),
        in_specs=[smem, vmem, vmem],
        out_specs=vmem,
    )(counts.reshape(1), coords, species.reshape(1, slots))
    shared = lax.all_to_all(
        jnp.broadcast_to(placed[None], (domains, 4, slots)), axes, 0, 0, tiled=True
    )
    prepared = pl.pallas_call(
        weights_kernel,
        out_shape=(
            jax.ShapeDtypeStruct((table, chan), f32),
            jax.ShapeDtypeStruct((half, pad, pad), bf16),
            jax.ShapeDtypeStruct((pad, 384), bf16),
            jax.ShapeDtypeStruct((2, 128, 128), bf16),
            jax.ShapeDtypeStruct((2, 256, 128), bf16),
            jax.ShapeDtypeStruct((2, 128, 256), bf16),
            jax.ShapeDtypeStruct((2, chan, chan), bf16),
            jax.ShapeDtypeStruct((16, 256), bf16),
        ),
        in_specs=[vmem] * 8,
        out_specs=(vmem,) * 8,
        compiler_params=kernel_params(),
    )(kvec, lr_filter, embed, radial_one, radial_two, mix_one, mix_two, read_weight)
    place = jnp.stack([lax.axis_index(axis) for axis in axes]).astype(jnp.int32)
    result = box_call(
        place, shared, coords, prepared, read_bias.reshape(1, chan), energy_weight.reshape(1, chan)
    )
    return (result[3].reshape(1, 1, 1, slots), result[:3].reshape(1, 1, 1, 3, slots))


def box_call(place, shared, coords, prepared, bias, energy, interpret=False):
    vmem = pl.BlockSpec(memory_space=pltpu.VMEM)
    smem = pl.BlockSpec(memory_space=pltpu.SMEM)
    grid_shape = (ext, ext, ext, planes, 128)
    return pl.pallas_call(
        box_kernel,
        out_shape=jax.ShapeDtypeStruct((8, slots), f32),
        in_specs=[smem] + [vmem] * 12,
        out_specs=vmem,
        scratch_shapes=[
            pltpu.VMEM((cells // 128, 64 * 16, 128), f32),
            pltpu.VMEM((64, pad), f32),
            pltpu.VMEM((2, rows_all, 128), f32),
            pltpu.VMEM((half, rows_all, pad), f32),
            pltpu.VMEM((2, table, planes * pad), bf16),
            pltpu.VMEM((table, cells), bf16),
            pltpu.VMEM(grid_shape, f32),
            pltpu.VMEM(grid_shape, f32),
            pltpu.VMEM(grid_shape, f32),
            pltpu.VMEM(grid_shape, f32),
            pltpu.VMEM((planes * pad, 128), bf16),
            pltpu.VMEM((cells + 80, 256), f32),
            pltpu.VMEM((2, pad, 128), f32),
        ],
        compiler_params=kernel_params(),
        interpret=interpret,
    )(
        place,
        shared,
        coords,
        *prepared,
        jnp.concatenate([bias, bias], axis=1),
        jnp.concatenate([energy, energy], axis=1),
    )


def solution(mesh):
    in_specs = (
        P(("group", "gx"), "gy", "gz", None),
        P(("group", "gx"), "gy", "gz"),
        P(("group", "gx"), "gy", "gz", None, None),
        P(("group", "gx"), "gy", "gz", None),
        P(("group", "gx"), "gy", "gz", None, None),
        P(),
        P(),
        P(),
        P(),
        P(),
        P(),
        P(),
        P(),
        P(),
        P(),
    )
    out_specs = (P(("group", "gx"), "gy", "gz", None), P(("group", "gx"), "gy", "gz", None, None))
    sizes = tuple(mesh.shape[axis] for axis in ("gx", "gy", "gz"))
    plan = whole_box if sizes == grid_dims else local
    return jax.shard_map(plan, mesh=mesh, in_specs=in_specs, out_specs=out_specs, check_vma=False)
```

```python
import math

import jax
import jax.numpy as jnp
import numpy as np
from jax import lax
from jax.experimental import pallas as pl
from jax.experimental.pallas import tpu as pltpu
from jax.sharding import PartitionSpec as P

SIDE = 6
KVEC = 4096
NBASIS = 8
NEIGH = 26


spacing = 2.5
cutoff = 5.0
two_pi = 6.283185307179586
highest = lax.Precision.HIGHEST


def passed_along(block, axis, distance):
    devices = range(lax.axis_size(axis))
    route = [((i - distance) % len(devices), i) for i in devices]
    return lax.ppermute(block, axis, route)


def extended(block, sides, width):
    for axis, dim in sides:
        count = lax.axis_size(axis)
        forward = [(i, i + 1) for i in range(count - 1)]
        forward.append((count - 1, 0))
        backward = [(target, source) for source, target in forward]
        low = lax.ppermute(
            lax.slice_in_dim(block, block.shape[dim] - width, None, axis=dim), axis, forward
        )
        high = lax.ppermute(lax.slice_in_dim(block, 0, width, axis=dim), axis, backward)
        block = jnp.concatenate([low, block, high], axis=dim)
    return block


def rows_per_block():
    return SIDE * SIDE


def boundary_list(side):
    site_ids = np.arange(side**3).reshape(side, side, side)
    inner = np.zeros((side, side, side), dtype=bool)
    inner[1 : side - 1, 1 : side - 1, 1 : side - 1] = True
    return site_ids[~inner].astype(np.int32)


def radial_terms(distance):
    centres = cutoff * jnp.arange(NBASIS).astype(jnp.float32) / (NBASIS - 1)
    sharpness = (NBASIS / cutoff) ** 2
    gap_value = distance[None] - centres[:, None, None]
    gaussian = jnp.exp(-sharpness * gap_value * gap_value)
    envelope_base = jnp.maximum(1.0 - distance * distance / (cutoff * cutoff), 0.0)
    envelope = envelope_base * envelope_base
    envelope_slope = -4.0 * distance * envelope_base / (cutoff * cutoff)
    radial_value = gaussian * envelope[None]
    radial_slope = gaussian * (envelope_slope[None] - 2.0 * sharpness * gap_value * envelope[None])
    return (radial_value, radial_slope)


def embed_codes(type_code, embed):
    species_ids = jnp.arange(1, embed.shape[0] + 1, dtype=jnp.int32).astype(type_code.dtype)
    one_hot = (type_code[None, :] == species_ids[:, None]).astype(jnp.float32)
    return jnp.dot(embed.T, one_hot, precision=highest, preferred_element_type=jnp.float32)


def cell_shift():
    ext_side = SIDE + 2
    cells = jnp.arange(ext_side**3, dtype=jnp.int32)
    coords = jnp.stack(
        [cells // (ext_side * ext_side), cells // ext_side % ext_side, cells % ext_side]
    )
    domain_width = SIDE * spacing
    return jnp.where(
        coords == 0, -domain_width, jnp.where(coords == ext_side - 1, domain_width, 0.0)
    ).astype(jnp.float32)


def pair_geometry(coords_own, pool_coords, pair_lists):
    separation = jnp.take(pool_coords, pair_lists, axis=1) - coords_own[:, None, :]
    distance = jnp.sqrt(jnp.sum(separation * separation, axis=0))
    return (separation, distance)


def message_forward(pool_values, pair_lists, radial_value, radial_weight):
    radial_filter = jnp.einsum("bc,bma->cma", radial_weight, radial_value, precision=highest)
    neighbour_value = jnp.take(pool_values, pair_lists, axis=1)
    return jnp.sum(radial_filter * neighbour_value, axis=1)


def message_backward(
    grad_message,
    pool_values,
    pair_lists,
    radial_value,
    radial_slope,
    radial_weight,
    separation,
    distance,
    pool_size,
    with_features,
):
    neighbour_value = jnp.take(pool_values, pair_lists, axis=1)
    contracted = jnp.einsum(
        "bc,cma->bma", radial_weight, grad_message[:, None, :] * neighbour_value, precision=highest
    )
    energy_slope = jnp.sum(radial_slope * contracted, axis=0)
    pair_force = separation * (energy_slope / distance)[None]
    flat_index = pair_lists.reshape(-1)
    grad_pool = (
        jnp.zeros((3, pool_size), jnp.float32).at[:, flat_index].add(pair_force.reshape(3, -1))
    )
    grad_own = -jnp.sum(pair_force, axis=1)
    if with_features:
        radial_filter = jnp.einsum("bc,bma->cma", radial_weight, radial_value, precision=highest)
        spread = (radial_filter * grad_message[:, None, :]).reshape(radial_filter.shape[0], -1)
        feature_pool = (
            jnp.zeros((radial_filter.shape[0], pool_size), jnp.float32)
            .at[:, flat_index]
            .add(spread)
        )
        return (grad_pool, grad_own, feature_pool)
    return (grad_pool, grad_own, grad_pool)


def phase_table(fraction, wave_numbers):
    phase_angle = two_pi * (
        fraction[0][:, None] * wave_numbers[0][None, :]
        + fraction[1][:, None] * wave_numbers[1][None, :]
        + fraction[2][:, None] * wave_numbers[2][None, :]
    )
    return (jnp.cos(phase_angle).astype(jnp.bfloat16), jnp.sin(phase_angle).astype(jnp.bfloat16))


def read_long(cosine_low, sine_low, filtered):
    dims = (((1,), (1,)), ((), ()))
    return lax.dot_general(
        filtered[0], cosine_low, dims, preferred_element_type=jnp.float32
    ) + lax.dot_general(filtered[1], sine_low, dims, preferred_element_type=jnp.float32)


def block_live(step_index, live_count):
    block_rows = rows_per_block()
    per_member = SIDE**3 // block_rows
    first_row = (step_index % per_member * block_rows).astype(jnp.float32)
    return first_row < live_count[step_index // per_member]


def lr_struct(fraction, row_values, live_count, wave_numbers):
    block_rows = rows_per_block()
    blocks = fraction.shape[1] // block_rows

    def step(step_index, running):

        def work(running):
            offset = step_index * block_rows
            frac_block = lax.dynamic_slice_in_dim(fraction, offset, block_rows, 1)
            feature_block = lax.dynamic_slice_in_dim(row_values, offset, block_rows, 1)
            cosine_low, sine_low = phase_table(frac_block, wave_numbers)
            term = jnp.stack(
                [
                    jnp.dot(feature_block, cosine_low, preferred_element_type=jnp.float32),
                    jnp.dot(feature_block, sine_low, preferred_element_type=jnp.float32),
                ]
            )
            return running + term

        return lax.cond(
            block_live(step_index, live_count), work, lambda unchanged: unchanged, running
        )

    initial = jnp.zeros((2, row_values.shape[0], wave_numbers.shape[1]), jnp.float32)
    return lax.fori_loop(0, blocks, step, initial)


def lr_read(fraction, live_count, wave_numbers, filtered):
    block_rows = rows_per_block()
    blocks = fraction.shape[1] // block_rows

    def step(step_index, result):

        def work(result):
            offset = step_index * block_rows
            cosine_low, sine_low = phase_table(
                lax.dynamic_slice_in_dim(fraction, offset, block_rows, 1), wave_numbers
            )
            return lax.dynamic_update_slice_in_dim(
                result, read_long(cosine_low, sine_low, filtered), offset, 1
            )

        return lax.cond(
            block_live(step_index, live_count), work, lambda unchanged: unchanged, result
        )

    initial = jnp.zeros((filtered.shape[1], fraction.shape[1]), jnp.float32)
    return lax.fori_loop(0, blocks, step, initial)


def lr_back(
    fraction,
    rounded_rows,
    grad_rows,
    occupied_rows,
    live_count,
    wave_numbers,
    wave_factors,
    filtered,
    back_filtered,
):
    block_rows = rows_per_block()
    blocks = fraction.shape[1] // block_rows
    dims = (((0,), (0,)), ((), ()))
    right_real = jnp.concatenate([filtered[0], back_filtered[0]], axis=0)
    right_imag = jnp.concatenate([filtered[1], back_filtered[1]], axis=0)

    def step(step_index, carried):

        def work(carried):
            grad_long, force_long = carried
            offset = step_index * block_rows
            cosine_low, sine_low = phase_table(
                lax.dynamic_slice_in_dim(fraction, offset, block_rows, 1), wave_numbers
            )
            mask_block = lax.dynamic_slice_in_dim(occupied_rows, offset, block_rows, 0)
            grad_block = mask_block[None] * read_long(cosine_low, sine_low, back_filtered)
            stacked_left = jnp.concatenate(
                [
                    lax.dynamic_slice_in_dim(grad_rows, offset, block_rows, 1),
                    lax.dynamic_slice_in_dim(rounded_rows, offset, block_rows, 1),
                ],
                axis=0,
            )
            real_part = lax.dot_general(
                stacked_left, right_real, dims, preferred_element_type=jnp.float32
            )
            imag_part = lax.dot_general(
                stacked_left, right_imag, dims, preferred_element_type=jnp.float32
            )
            turning = (
                cosine_low.astype(jnp.float32) * imag_part
                - sine_low.astype(jnp.float32) * real_part
            )
            force_block = lax.dot_general(
                wave_factors,
                turning,
                (((1,), (1,)), ((), ())),
                precision=highest,
                preferred_element_type=jnp.float32,
            )
            return (
                lax.dynamic_update_slice_in_dim(grad_long, grad_block, offset, 1),
                lax.dynamic_update_slice_in_dim(force_long, force_block, offset, 1),
            )

        return lax.cond(
            block_live(step_index, live_count), work, lambda unchanged: unchanged, carried
        )

    initial = (
        jnp.zeros((rounded_rows.shape[0], fraction.shape[1]), jnp.float32),
        jnp.zeros((3, fraction.shape[1]), jnp.float32),
    )
    return lax.fori_loop(0, blocks, step, initial)


def boundary_grid(values, ghost_slots, boundary):
    picked = jnp.take(values, ghost_slots, axis=1)
    site_grid = jnp.zeros((values.shape[0], SIDE**3), values.dtype).at[:, boundary].set(picked)
    return site_grid.reshape(values.shape[0], SIDE, SIDE, SIDE)


def fold_slab(site_grid, axis_number, from_left, from_right):
    inner_size = site_grid.shape[axis_number] - 2
    inner = lax.slice_in_dim(site_grid, 1, inner_size + 1, axis=axis_number)
    first_layer = lax.slice_in_dim(inner, 0, 1, axis=axis_number) + from_left
    last_layer = lax.slice_in_dim(inner, inner_size - 1, inner_size, axis=axis_number) + from_right
    middle = lax.slice_in_dim(inner, 1, inner_size - 1, axis=axis_number)
    return jnp.concatenate([first_layer, middle, last_layer], axis=axis_number)


def return_halo(site_grid):
    edge = site_grid.shape[3] - 1
    received = [
        passed_along(
            lax.slice_in_dim(site_grid, slab_start, slab_start + 1, axis=3), "gz", direction
        )
        for direction, slab_start in ((1, edge), (-1, 0))
    ]
    site_grid = fold_slab(site_grid, 3, received[0], received[1])
    edge = site_grid.shape[2] - 1
    received = [
        passed_along(
            lax.slice_in_dim(site_grid, slab_start, slab_start + 1, axis=2), "gy", direction
        )
        for direction, slab_start in ((1, edge), (-1, 0))
    ]
    site_grid = fold_slab(site_grid, 2, received[0], received[1])
    edge = site_grid.shape[1] - 1
    received = [
        passed_along(
            lax.slice_in_dim(site_grid, slab_start, slab_start + 1, axis=1), "gx", direction
        )
        for direction, slab_start in ((1, edge), (-1, 0))
    ]
    return fold_slab(site_grid, 1, received[0], received[1])


def ghost_to_rows(site_grid, ghost_slots, boundary):
    features = site_grid.shape[0]
    picked = site_grid.reshape(features, -1)[:, boundary]
    return jnp.zeros((features, SIDE**3), site_grid.dtype).at[:, ghost_slots].add(picked)


def local(
    species,
    counts,
    positions,
    ghost_rows,
    neighbours,
    kvec,
    embed,
    radial_one,
    radial_two,
    mix_one,
    mix_two,
    lr_filter,
    read_weight,
    read_bias,
    energy_weight,
):
    slot_count = SIDE**3
    ext_side = SIDE + 2
    pool_size = slot_count + ext_side**3
    pair_scale = 1.0 / math.sqrt(NEIGH)
    domain_width = SIDE * spacing
    mesh_sizes = (lax.axis_size("gx"), lax.axis_size("gy"), lax.axis_size("gz"))
    box_length = tuple((count_along * domain_width for count_along in mesh_sizes))
    wave_scale = 1.0 / math.sqrt(
        KVEC * (slot_count * mesh_sizes[0] * mesh_sizes[1] * mesh_sizes[2])
    )
    species_flat = species.reshape(slot_count)
    live_total = counts.reshape(())
    coords_own = positions.reshape(3, slot_count)
    ghost_slots = ghost_rows.reshape(-1)
    pair_lists = neighbours.reshape(NEIGH, slot_count)
    boundary = jnp.asarray(boundary_list(SIDE))
    cell_offset = cell_shift()
    occupied = (jnp.arange(slot_count, dtype=jnp.int32) < live_total).astype(jnp.float32)
    type_code = jnp.where(occupied > 0, species_flat + 1, 0).astype(jnp.float32)
    hidden_zero = embed_codes(species_flat + 1, embed)
    masked_zero = hidden_zero * occupied[None]
    packet = boundary_grid(
        jnp.concatenate([coords_own, type_code[None]], axis=0), ghost_slots, boundary
    )
    ext_atoms = extended(packet, (("gx", 1), ("gy", 2), ("gz", 3)), 1).reshape(4, -1)
    pool_coords = jnp.concatenate([coords_own, ext_atoms[:3] + cell_offset], axis=1)
    pool_zero = jnp.concatenate([masked_zero, embed_codes(ext_atoms[3], embed)], axis=1)
    separation, distance = pair_geometry(coords_own, pool_coords, pair_lists)
    radial_value, radial_slope = radial_terms(distance)
    message = message_forward(pool_zero, pair_lists, radial_value, radial_one)
    hidden_one = hidden_zero + pair_scale * jnp.dot(
        mix_one.T, message, precision=highest, preferred_element_type=jnp.float32
    )
    masked_one = hidden_one * occupied[None]
    rounded_one = masked_one.astype(jnp.bfloat16)
    domain_pos = (lax.axis_index("gx"), lax.axis_index("gy"), lax.axis_index("gz"))
    fraction = jnp.stack(
        [
            (domain_pos[axis_id].astype(jnp.float32) * domain_width + coords_own[axis_id])
            / box_length[axis_id]
            for axis_id in range(3)
        ]
    )
    wave_numbers = kvec.astype(jnp.float32)
    wave_factors = jnp.stack(
        [two_pi * wave_numbers[axis_id] / box_length[axis_id] for axis_id in range(3)]
    )
    own_count = jnp.sum(occupied)[None]
    share_size = KVEC // (mesh_sizes[0] * mesh_sizes[1] * mesh_sizes[2])
    share_start = lax.axis_index(("gx", "gy", "gz")) * share_size
    filter_share = lax.dynamic_slice_in_dim(lr_filter, share_start, share_size, 1)
    struct_part = lax.psum_scatter(
        lr_struct(fraction, rounded_one, own_count, wave_numbers),
        ("gx", "gy", "gz"),
        scatter_dimension=2,
        tiled=True,
    )
    filtered = lax.all_gather(
        (struct_part * filter_share[None] * wave_scale).astype(jnp.bfloat16),
        ("gx", "gy", "gz"),
        axis=2,
        tiled=True,
    )
    long_part = lr_read(fraction, own_count, wave_numbers, filtered)
    masked_ext = extended(
        boundary_grid(masked_one, ghost_slots, boundary).astype(jnp.bfloat16),
        (("gx", 1), ("gy", 2), ("gz", 3)),
        1,
    ).astype(jnp.float32)
    pool_one = jnp.concatenate([masked_one, masked_ext.reshape(masked_one.shape[0], -1)], axis=1)
    message_two = message_forward(pool_one, pair_lists, radial_value, radial_two)
    hidden_two = (
        hidden_one
        + pair_scale
        * jnp.dot(mix_two.T, message_two, precision=highest, preferred_element_type=jnp.float32)
        + long_part
    )
    activation = (
        jnp.dot(read_weight.T, hidden_two, precision=highest, preferred_element_type=jnp.float32)
        + read_bias[:, None]
    )
    gating = jax.nn.sigmoid(activation)
    energies = occupied * jnp.sum(activation * gating * energy_weight[:, None], axis=0)
    grad_act = (
        occupied[None] * energy_weight[:, None] * gating * (1.0 + activation * (1.0 - gating))
    )
    grad_two = jnp.dot(read_weight, grad_act, precision=highest, preferred_element_type=jnp.float32)
    grad_low = grad_two.astype(jnp.bfloat16)
    grad_part = lax.psum_scatter(
        lr_struct(fraction, grad_low, own_count, wave_numbers),
        ("gx", "gy", "gz"),
        scatter_dimension=2,
        tiled=True,
    )
    back_filtered = lax.all_gather(
        (grad_part * filter_share[None] * wave_scale).astype(jnp.bfloat16),
        ("gx", "gy", "gz"),
        axis=2,
        tiled=True,
    )
    grad_long, force_long = lr_back(
        fraction,
        rounded_one,
        grad_low,
        occupied,
        own_count,
        wave_numbers,
        wave_factors,
        filtered,
        back_filtered,
    )
    grad_message = pair_scale * jnp.dot(
        mix_two, grad_two, precision=highest, preferred_element_type=jnp.float32
    )
    grad_pool, grad_own_two, feature_pool = message_backward(
        grad_message,
        pool_one,
        pair_lists,
        radial_value,
        radial_slope,
        radial_two,
        separation,
        distance,
        pool_size,
        True,
    )
    combined = jnp.concatenate([feature_pool, grad_pool], axis=0)
    features = combined.shape[0]
    returned_two = ghost_to_rows(
        return_halo(combined[:, slot_count:].reshape(features, ext_side, ext_side, ext_side)),
        ghost_slots,
        boundary,
    )
    own_two = combined[:, :slot_count]
    channels = masked_one.shape[0]
    grad_one = (
        grad_two + grad_long + occupied[None] * (own_two[:channels] + returned_two[:channels])
    )
    grad_message_one = pair_scale * jnp.dot(
        mix_one, grad_one, precision=highest, preferred_element_type=jnp.float32
    )
    grad_pool_one, grad_own_one, unused = message_backward(
        grad_message_one,
        pool_zero,
        pair_lists,
        radial_value,
        radial_slope,
        radial_one,
        separation,
        distance,
        pool_size,
        False,
    )
    layer_one_grad = grad_own_one + grad_pool_one[:, :slot_count]
    returned_one = ghost_to_rows(
        return_halo(grad_pool_one[:, slot_count:].reshape(3, ext_side, ext_side, ext_side)),
        ghost_slots,
        boundary,
    )
    total_grad = (
        layer_one_grad
        + returned_one
        + force_long
        + grad_own_two
        + own_two[channels:]
        + returned_two[channels:]
    )
    forces = -total_grad
    return (energies.reshape(1, 1, 1, slot_count), forces.reshape(1, 1, 1, 3, slot_count))


offsets = tuple(
    (ox, oy, oz)
    for ox in (0, 1)
    for oy in (-1, 0, 1)
    for oz in (-1, 0, 1)
    if (ox, oy, oz) > (0, 0, 0)
)
half = len(offsets)
slots = SIDE**3
ext = SIDE + 2
cells = ext**3
inner_lanes = SIDE * ext * ext
chan = 64
grid_dims = (4, 2, 2)
domains = 16
planes = 8
rows_all = slots * planes
waves = 648
table = 2 * waves
pad = 256
gamma = (NBASIS / cutoff) ** 2
step = cutoff / (NBASIS - 1)
nt = (((1,), (1,)), ((), ()))
nn = (((1,), (0,)), ((), ()))
f32 = jnp.float32
bf16 = jnp.bfloat16


def dot(left, right, dims=nn, precision=None):
    return lax.dot_general(left, right, dims, precision=precision, preferred_element_type=f32)


def split(value):
    high = value.astype(bf16)
    return high, (value - high.astype(f32)).astype(bf16)


def dot_split(left, high, low):
    left_high, left_low = split(left)
    return dot(left_high, high) + dot(left_low, high) + dot(left_high, low)


def exact(left, hot, dims=nn):
    high = left.astype(bf16).astype(f32)
    rest = left - high
    middle = rest.astype(bf16).astype(f32)
    count = left.shape[0]
    stacked = jnp.concatenate([high, middle, rest - middle], axis=0).astype(bf16)
    parts = dot(stacked, hot, dims)
    return parts[:count] + parts[count : 2 * count] + parts[2 * count :]


def coords_of(ref):
    return jnp.concatenate([ref[0, 0, axis] for axis in range(3)], axis=0)


def site_of(coords):
    where = (coords * (1.0 / spacing)).astype(jnp.int32)
    return (where[0:1] * SIDE + where[1:2]) * SIDE + where[2:3]


def iota(shape, dim):
    return lax.broadcasted_iota(jnp.int32, shape, dim)


def place_kernel(count_ref, pos_ref, species_ref, out_ref):
    coords = coords_of(pos_ref)
    live = iota((1, slots), 1) < count_ref[0, 0, 0]
    code = jnp.where(live, species_ref[0, 0] + 1, 0).astype(f32)
    data = jnp.concatenate([coords, code, jnp.zeros((4, slots), f32)], axis=0)
    hot = (iota((slots, slots), 0) == site_of(coords)).astype(f32).astype(bf16)
    placed = exact(data, hot, nt)[0:4]
    for number in range(domains):
        out_ref[number] = placed


def twice(block):
    zero = jnp.zeros_like(block)
    return jnp.concatenate(
        [jnp.concatenate([block, zero], axis=1), jnp.concatenate([zero, block], axis=1)], axis=0
    )


def weights_kernel(
    kvec_ref,
    filter_ref,
    embed_ref,
    one_ref,
    two_ref,
    mix_one_ref,
    mix_two_ref,
    read_ref,
    bias_ref,
    energy_ref,
    gain_ref,
    radial_ref,
    embed_out,
    mix_ref,
    act_ref,
    grad_ref,
    back_ref,
    pair_ref,
    lines_ref,
):
    pair_scale = 1.0 / math.sqrt(NEIGH)
    wave_scale = 1.0 / math.sqrt(KVEC * slots * domains)
    waves_in = kvec_ref[...]

    def folded(row):
        return jnp.where(row > 0, 2 * row - 1, -2 * row)

    index = (folded(waves_in[1:2]) * 9 + folded(waves_in[2:3])) * 8 + waves_in[0:1] - 1
    filter_high, filter_low = split(filter_ref[...] * wave_scale)
    parts = jnp.concatenate([filter_high, filter_low], axis=0)
    gain = jnp.zeros((waves, 2 * chan), f32)
    width = 1024
    for start in range(0, KVEC, width):
        hot = (iota((waves, width), 0) == index[:, start : start + width]).astype(f32).astype(bf16)
        gain = gain + dot(hot, parts[:, start : start + width], nt)
    gain = (gain[:, :chan] + gain[:, chan:]).reshape(waves // 8, 8, chan)
    gain_ref[...] = jnp.concatenate([gain, gain], axis=1).reshape(table, chan)

    centre = step * iota((NBASIS, 1), 0).astype(f32)
    fall = jnp.exp(-gamma * centre * centre)
    rows = iota((pad, pad), 0)
    columns = iota((pad, pad), 1)
    kept = (rows // 128) == (columns % 128 // chan)

    def spread(block):
        return jnp.broadcast_to(block[:, None, :], (NBASIS, 16, chan)).reshape(128, chan)

    def wide(left, right):
        left, right = spread(left), spread(right)
        line = jnp.concatenate([left, left, right, right], axis=1)
        return jnp.concatenate([line, line], axis=0)

    radial = wide(one_ref[...] * fall, two_ref[...] * fall)
    for offset in range(half):
        radial_ref[offset] = jnp.where(kept & (rows % 16 == offset), radial, 0.0).astype(bf16)
    table_rows = jnp.concatenate([embed_ref[...], jnp.zeros((2, chan), f32)], axis=0)
    high = table_rows.astype(bf16).astype(f32)
    species_rows = kept & (rows % 16 == half)
    embeds = jnp.where(species_rows, wide(high, table_rows - high), 0.0).astype(bf16)
    lives = jnp.where(species_rows[:, :128], 1.0, 0.0).astype(bf16)
    embed_out[...] = jnp.concatenate([embeds, lives], axis=1)

    def put(ref, value):
        value_high, value_low = split(value)
        ref[0] = value_high
        ref[1] = value_low

    bias = bias_ref[...]
    energy = energy_ref[...]
    lines_ref[0:1] = jnp.concatenate([bias, bias], axis=1)
    lines_ref[1:2] = jnp.concatenate([energy, energy], axis=1)
    mix_two = mix_two_ref[...]
    read = read_ref[...]
    both = dot(mix_two, read, nn, highest) * pair_scale
    put(mix_ref, twice(mix_one_ref[...] * pair_scale))
    put(act_ref, jnp.concatenate([twice(read), twice(both)], axis=0))
    put(grad_ref, jnp.concatenate([twice(read.T), twice(both.T)], axis=1))
    put(back_ref, mix_one_ref[...].T * pair_scale)
    pairs = jnp.concatenate([two_ref[...], two_ref[...], one_ref[...], one_ref[...]], axis=1)
    pairs = jnp.broadcast_to(pairs[:, None, :], (NBASIS, 16, 256)).reshape(128, 256).T
    for offset in range(half):
        pair_ref[offset] = jnp.where(columns[:, :128] % 16 == offset, pairs, 0.0).astype(bf16)


def turn(fraction):
    rest = fraction - jnp.floor(fraction + 0.5)
    angle = rest * (0.5 * two_pi)
    square = angle * angle
    sine = angle * (
        1.0
        + square
        * (
            -1.0 / 6
            + square
            * (
                1.0 / 120
                + square * (-1.0 / 5040 + square * (1.0 / 362880 - square * (1.0 / 39916800)))
            )
        )
    )
    cosine = 1.0 + square * (
        -0.5
        + square
        * (
            1.0 / 24
            + square
            * (
                -1.0 / 720
                + square
                * (1.0 / 40320 + square * (-1.0 / 3628800 + square * (1.0 / 479001600)))
            )
        )
    )
    return 1.0 - 2.0 * sine * sine, 2.0 * sine * cosine


def fan(base, step_pairs):
    real, imag = base
    out = [(real, imag)]
    for cosine, sine in step_pairs:
        a, b, c, d = real * cosine, imag * sine, real * sine, imag * cosine
        out.append((a - b, c + d))
        out.append((a + b, d - c))
    return out


def wave_tile(coords, store):
    frac = [coords[axis] / (grid_dims[axis] * SIDE * spacing) for axis in range(3)]
    row = iota((8, 128), 0)
    base = turn(frac[0] * (row + 1).astype(f32))
    rest = turn(jnp.where(row < 4, frac[1], frac[2]) * (row % 4 + 1).astype(f32))

    def line(index):
        return tuple(jnp.broadcast_to(part[index : index + 1], (8, 128)) for part in rest)

    y_lines = [line(index) for index in range(4)]
    z_lines = [line(index + 4) for index in range(4)]
    index = 0
    for level in fan(base, y_lines):
        for real, imag in fan(level, z_lines):
            store(index, jnp.concatenate([real, imag], axis=0).astype(bf16))
            index += 1


def swap_lanes(value):
    return pltpu.roll(value, chan, value.ndim - 1)


def swap_planes(value):
    up = pltpu.roll(value, 1, 1)
    down = pltpu.roll(value, planes - 1, 1)
    return jnp.where(iota(value.shape, 1) % 2 == 0, down, up)


def as_three(value):
    return value.reshape((-1,) + value.shape[-2:])


def fill_ghosts(ref):
    inner = slice(1, SIDE + 1)
    for ghost, source, shift in ((0, SIDE, 2), (SIDE + 1, 1, planes - 2)):
        value = ref[source, inner, inner]
        ref[ghost, inner, inner] = pltpu.roll(as_three(value), shift, 1).reshape(value.shape)
    for ghost, source in ((0, SIDE), (SIDE + 1, 1)):
        value = ref[:, source, inner]
        ref[:, ghost, inner] = swap_planes(as_three(value)).reshape(value.shape)
    for ghost, source in ((0, SIDE), (SIDE + 1, 1)):
        value = ref[:, :, source]
        ref[:, :, ghost] = swap_lanes(as_three(value)).reshape(value.shape)


def fold_ghosts(ref):
    inner = slice(1, SIDE + 1)
    for ghost, target in ((SIDE + 1, 1), (0, SIDE)):
        value = ref[:, :, ghost]
        ref[:, :, target] = ref[:, :, target] + swap_lanes(as_three(value)).reshape(value.shape)
    for ghost, target in ((SIDE + 1, 1), (0, SIDE)):
        value = ref[:, ghost, inner]
        ref[:, target, inner] = ref[:, target, inner] + swap_planes(as_three(value)).reshape(
            value.shape
        )
    for ghost, target, shift in ((SIDE + 1, 1, 2), (0, SIDE, planes - 2)):
        value = ref[ghost, inner, inner]
        ref[target, inner, inner] = ref[target, inner, inner] + pltpu.roll(
            as_three(value), shift, 1
        ).reshape(value.shape)


def inner_rows(ref):
    inner = slice(1, SIDE + 1)
    return ref[inner, inner, inner].reshape(rows_all, 128)


def set_inner(ref, value):
    inner = slice(1, SIDE + 1)
    ref[inner, inner, inner] = value.reshape(SIDE, SIDE, SIDE, planes, 128)


def convolve(filters, layer, source, target, beside=None):
    target[...] = jnp.zeros(target.shape, f32)
    lanes = slice(layer * 128, layer * 128 + 128)
    groups = {}
    for number, (ox, oy, oz) in enumerate(offsets):
        groups.setdefault((ox, oy), []).append((number, oz))

    def one_line(line):
        x = line // SIDE
        y = line % SIDE
        own = [source[x + 1, y + 1, z + 1] for z in range(SIDE)]
        own_sum = [jnp.zeros((planes, 128), f32)] * SIDE
        for (ox, oy), members in groups.items():
            there = [source[x + 1 + ox, y + 1 + oy, z] for z in range(ext)]
            sums = [None] * ext
            for z in range(SIDE):
                for number, oz in members:
                    first = pl.multiple_of((line * SIDE + z) * planes, planes)
                    weight = filters[number, pl.ds(first, planes), lanes]
                    own_sum[z] = own_sum[z] + weight * there[z + 1 + oz]
                    term = weight * own[z]
                    spot = z + 1 + oz
                    sums[spot] = term if sums[spot] is None else sums[spot] + term
            for z in range(ext):
                if sums[z] is not None:
                    target[x + 1 + ox, y + 1 + oy, z] = target[x + 1 + ox, y + 1 + oy, z] + sums[z]
        for z in range(SIDE):
            target[x + 1, y + 1, z + 1] = target[x + 1, y + 1, z + 1] + own_sum[z]

    def body(number, carry):
        if beside is not None:
            beside(number)
        for part in range(3):
            one_line(number * 3 + part)
        return carry

    lax.fori_loop(0, SIDE * SIDE // 3, body, 0)
    fold_ghosts(target)


def box_kernel(
    place_ref,
    all_ref,
    pos_ref,
    gain_ref,
    radial_ref,
    embed_ref,
    mix_ref,
    act_ref,
    grad_ref,
    back_ref,
    pair_ref,
    lines_ref,
    energy_out,
    force_out,
    sep_ref,
    sites_ref,
    basis_ref,
    filters_ref,
    waves_ref,
    ring_ref,
    zero_ref,
    one_ref,
    sum_ref,
    packed_ref,
    own_ref,
    flat_ref,
    low_ref,
    parts_ref,
    saved_ref,
):
    home = [place_ref[axis] for axis in range(3)]
    sites_ref[...] = jnp.zeros((4 * domains, pad), f32)
    domain_width = SIDE * spacing
    offset_row = iota((4, slots), 0)
    for number in range(domains):
        spot = [
            lax.rem(home[axis] + part, grid_dims[axis])
            for axis, part in enumerate((number // 4, number // 2 % 2, number % 2))
        ]
        block = all_ref[(spot[0] * 2 + spot[1]) * 2 + spot[2]]
        sites_ref[number * 4 : number * 4 + 4, 0:slots] = block
        shifts = [part * domain_width for part in (number // 4, number // 2 % 2, number % 2)]
        moved = jnp.where(
            offset_row == 0, shifts[0], jnp.where(offset_row == 1, shifts[1], shifts[2])
        )
        start = (number % 2 * planes + number // 2) * slots
        flat_ref[0:4, start : start + slots] = block + moved
    sites = sites_ref[:, 0:slots]

    lane = iota((1, cells), 1)
    coords = [(lane // (ext * ext) + 1) % ext, lane // ext % ext, lane % ext]
    wrapped = [(value + SIDE - 1) % SIDE for value in coords]
    wrapped_site = (wrapped[0] * SIDE + wrapped[1]) * SIDE + wrapped[2]
    inside = coords[0] >= 0
    for value in coords:
        inside = inside & (value > 0) & (value < ext - 1)
    hot_all = iota((slots, cells), 0) == wrapped_site
    grown = exact(sites, hot_all.astype(f32).astype(bf16))
    picks = (hot_all & inside)[:, :inner_lanes].astype(f32).astype(bf16)

    back16 = jnp.concatenate([grown[48:], grown[:48]], axis=0)
    ahead16 = jnp.concatenate([grown[16:], grown[:16]], axis=0)
    grown = jnp.where(coords[0] == 0, back16, jnp.where(coords[0] == ext - 1, ahead16, grown))
    swapped = jnp.concatenate(
        [grown[8 * (part ^ 1) : 8 * (part ^ 1) + 8] for part in range(8)], axis=0
    )
    grown = jnp.where((coords[1] == 0) | (coords[1] == ext - 1), swapped, grown)
    swapped = pltpu.roll(grown.reshape(8, 8, cells), 4, 1).reshape(64, cells)
    grown = jnp.where((coords[2] == 0) | (coords[2] == ext - 1), swapped, grown)
    component = iota((64, cells), 0) % 4
    for axis in range(3):
        moved = jnp.where(
            coords[axis] == 0,
            -domain_width,
            jnp.where(coords[axis] == ext - 1, domain_width, 0.0),
        )
        grown = grown + jnp.where(component == axis, moved, 0.0)
    own_ext = grown[0:4]
    tiles = cells // 128

    def put_sep(number, value):
        for tile in range(tiles):
            sep_ref[tile, pl.ds(number, 64, stride=16), :] = value[:, tile * 128 : tile * 128 + 128]

    def get_sep(window, count=tiles):
        return jnp.concatenate([sep_ref[tile, window, :] for tile in range(count)], axis=1)

    for number, (ox, oy, oz) in enumerate(offsets):
        distance = (ox * ext + oy) * ext + oz
        put_sep(number, pltpu.roll(grown, cells - distance, 1) - grown)
    for number in range(half, 16):
        put_sep(number, grown)

    row16 = iota((16, inner_lanes), 0)

    def basis_of(domain):
        first = pl.multiple_of(domain * 64, 64)
        sx, sy, sz, codes = [get_sep(pl.ds(first + 16 * part, 16), inner_lanes // 128) for part in range(4)]
        square = sx * sx + sy * sy + sz * sz
        near = jnp.minimum(jnp.sqrt(square), cutoff)
        base = jnp.maximum(1.0 - square * (1.0 / (cutoff * cutoff)), 0.0)
        value = jnp.exp(-gamma * jnp.minimum(square, cutoff * cutoff)) * base * base
        ratio = jnp.exp((2.0 * gamma * step) * near)
        out = []
        for number in range(NBASIS):
            hit = jnp.where(codes == number + 1.0, 1.0, 0.0)
            out.append(jnp.where(row16 == half, hit, value))
            value = value * ratio
        return jnp.concatenate(out, axis=0).astype(bf16)

    def basis_step(plane, carry):
        both = jnp.concatenate([basis_of(2 * plane), basis_of(2 * plane + 1)], axis=0)
        picked = dot(picks, both, nt)
        for tile in range(2):
            basis_ref[tile, pl.ds(plane, slots, stride=planes), :] = picked[
                :, tile * 128 : tile * 128 + 128
            ]
        return carry

    lax.fori_loop(0, planes, basis_step, 0)

    basis_low = jnp.concatenate([basis_ref[0], basis_ref[1]], axis=1).astype(bf16)
    low_ref[...] = basis_low

    def flat_tile(start):
        block = flat_ref[:, pl.ds(start, 128)]

        def store(index, value):
            waves_ref[index * 16 : index * 16 + 16, pl.ds(start, 128)] = value

        wave_tile([block[axis : axis + 1] for axis in range(3)], store)

    def wave_step(number, carry):
        filters_ref[number] = dot(low_ref[...], radial_ref[number])
        for part in range(2):
            flat_tile(pl.multiple_of(number * 256 + part * 128, 128))
        return carry

    lax.fori_loop(0, half, wave_step, 0)
    flat_tile(half * 256)
    for tile in range(cells // 128):
        lanes = slice(tile * 128, tile * 128 + 128)

        def store(index, value):
            ring_ref[index * 16 : index * 16 + 16, lanes] = value

        wave_tile([own_ext[axis : axis + 1, lanes] for axis in range(3)], store)

    start_values = dot(basis_low, embed_ref[...])
    rows_ref = basis_ref.at[0]
    live_ref = basis_ref.at[1]
    live_ref[...] = start_values[:, 256:384]
    set_inner(zero_ref, start_values[:, :128] + start_values[:, 128:256])
    fill_ghosts(zero_ref)
    convolve(filters_ref, 0, zero_ref, sum_ref)
    flat = (cells * planes, 128)
    own_cells = pl.ds(0, cells, stride=planes)

    def cells_of(ref):
        value = ref.reshape(flat)[own_cells, :]
        return jnp.concatenate([value[ext * ext :], value[: ext * ext]], axis=0)[:, :chan]

    saved_ref[0] = cells_of(zero_ref)
    first_rows = inner_rows(zero_ref) + live_ref[...] * dot_split(
        inner_rows(sum_ref), mix_ref[0], mix_ref[1]
    )
    set_inner(one_ref, first_rows)
    rows_ref[...] = first_rows
    fill_ghosts(one_ref)
    saved_ref[1] = cells_of(one_ref)
    two_ref = zero_ref

    def pack_rows():
        for plane in range(planes):
            value = rows_ref[pl.ds(plane, slots, stride=planes), :]
            packed_ref[plane * slots : plane * slots + slots] = value
            packed_ref[rows_all + plane * slots : rows_all + plane * slots + slots] = pltpu.roll(
                value, chan, 1
            )
        tail = 12 * pad
        parts_ref[...] = dot(waves_ref[:, tail:], packed_ref[tail:].astype(bf16))

    def structure_step(number):
        start = pl.multiple_of(number * pad, pad)
        parts_ref[...] = parts_ref[...] + dot(
            waves_ref[:, pl.ds(start, pad)], packed_ref[pl.ds(start, pad), :].astype(bf16)
        )

    def structure():
        return parts_ref[:, :chan] * gain_ref[...]

    pack_rows()
    own_ref[...] = jnp.zeros(own_ref.shape, f32)
    own_ref[0, 0:slots] = rows_ref[pl.ds(0, slots, stride=planes), :]
    convolve(filters_ref, 1, one_ref, sum_ref, structure_step)
    filtered = structure()
    long_rows = dot(filtered.T.astype(bf16), waves_ref[...]).T
    for plane in range(planes):
        first = long_rows[plane * slots : plane * slots + slots]
        second = long_rows[rows_all + plane * slots : rows_all + plane * slots + slots]
        rows_ref[pl.ds(plane, slots, stride=planes), :] = jnp.concatenate([first, second], axis=1)
    joined = jnp.concatenate([inner_rows(one_ref) + rows_ref[...], inner_rows(sum_ref)], axis=1)
    act = dot_split(joined, act_ref[0], act_ref[1]) + lines_ref[0:1]
    sig = 1.0 / (1.0 + jnp.exp(-act))
    weighted = live_ref[...] * lines_ref[1:2] * sig
    rows_ref[...] = weighted * act
    own_energy = rows_ref[pl.ds(0, slots, stride=planes), :]
    first_half = jnp.where(iota((8, 128), 1) < chan, 1.0, 0.0)
    energy_high, energy_low = split(own_energy)
    first_half = first_half.astype(bf16)
    site_energy = (dot(first_half, energy_high, nt) + dot(first_half, energy_low, nt))[0:1]
    grads = dot_split(weighted * (1.0 + act * (1.0 - sig)), grad_ref[0], grad_ref[1])
    rows_ref[...] = grads[:, :128]
    set_inner(two_ref, grads[:, 128:])
    fill_ghosts(two_ref)
    pack_rows()
    own_ref[1, 0:slots] = rows_ref[pl.ds(0, slots, stride=planes), :]
    two_cells = cells_of(two_ref)
    convolve(filters_ref, 1, two_ref, sum_ref, structure_step)
    back = structure()
    back_rows = back.T.astype(bf16)
    set_inner(sum_ref, rows_ref[...] + live_ref[...] * inner_rows(sum_ref))
    fill_ghosts(sum_ref)
    sum_cells = cells_of(sum_ref)
    live_cells = jnp.where(own_ext[3:4] > 0, 1.0, 0.0)
    ring_long = (dot(back_rows, ring_ref[...]) * live_cells).T
    grad_cells = dot_split(sum_cells + ring_long, back_ref[0], back_ref[1])

    def crossed(value):
        value = value.reshape(waves // 8, 2, 8, chan)
        value = jnp.concatenate([value[:, 1:2], -value[:, 0:1]], axis=1).reshape(table, chan)
        return jnp.concatenate([value, jnp.zeros((table, chan), f32)], axis=1).astype(bf16)

    response = dot(crossed(filtered), own_ref[1].astype(bf16), nt) + dot(
        crossed(back), own_ref[0].astype(bf16), nt
    )
    turning_high, turning_low = split(waves_ref[:, 0:pad].astype(f32) * response)
    spot = iota((8, table), 1)
    wave = spot // 16 * 8 + spot % 8

    def signed(index):
        return jnp.where(index % 2 == 1, (index + 1) // 2, -(index // 2))

    row = iota((8, table), 0)
    number = jnp.where(
        row == 0,
        wave % 8 + 1,
        jnp.where(row == 1, signed(wave // 72), jnp.where(row == 2, signed(wave // 8 % 9), 0)),
    )
    number = number.astype(f32).astype(bf16)
    scale_row = iota((8, 1), 0)
    scales = jnp.where(
        scale_row == 0,
        two_pi / (grid_dims[0] * domain_width),
        two_pi / (grid_dims[1] * domain_width),
    )
    long_force = (dot(number, turning_high) + dot(number, turning_low))[:, :slots] * scales

    zero_cells = saved_ref[0]
    one_cells = saved_ref[1]
    left = [
        jnp.concatenate([two_cells, one_cells], axis=1),
        jnp.concatenate([grad_cells, zero_cells], axis=1),
    ]
    right = jnp.concatenate(
        [
            jnp.concatenate([one_cells, two_cells], axis=1),
            jnp.concatenate([zero_cells, grad_cells], axis=1),
        ],
        axis=1,
    )
    left = jnp.concatenate(left, axis=1)
    reach = ext * ext + 2 * ext
    for shift in range(3):
        moved = right if shift == 1 else pltpu.roll(right, (1 - shift) % cells, 0)
        filters_ref[shift, 0:cells] = moved
        filters_ref[shift, cells : cells + reach] = moved[:reach]
    shares = jnp.zeros((cells, 128), f32)
    for number, (ox, oy, oz) in enumerate(offsets):
        distance = (ox * ext + oy) * ext
        products = left * filters_ref[oz + 1, distance : distance + cells]
        shares = shares + dot(products.astype(bf16), pair_ref[number])
    shares = shares.T
    sep = [get_sep(slice(16 * part, 16 * part + 16)) for part in range(3)]
    square = sep[0] * sep[0] + sep[1] * sep[1] + sep[2] * sep[2]
    length = jnp.sqrt(square)
    base = jnp.maximum(1.0 - square * (1.0 / (cutoff * cutoff)), 0.0)
    inward = length * base * (-4.0 / (cutoff * cutoff))
    outward = (-2.0 * gamma) * base * base
    strength = jnp.zeros((16, cells), f32)
    for number in range(NBASIS):
        gap = length - step * number
        slope = jnp.exp(-gamma * gap * gap) * (inward + gap * outward)
        strength = strength + slope * shares[16 * number : 16 * number + 16]
    strength = strength / length
    totals = []
    for part in range(3):
        force = jnp.where(iota((16, cells), 0) < half, sep[part] * strength, 0.0)
        total = -jnp.sum(force, axis=0, keepdims=True)
        for number, (ox, oy, oz) in enumerate(offsets):
            distance = (ox * ext + oy) * ext + oz
            total = total + pltpu.roll(force[number : number + 1], distance, 1)
        totals.append(total)
    total = jnp.concatenate(totals + [jnp.zeros((5, cells), f32)], axis=0)
    site_total = exact(total[:, :inner_lanes], picks, nt)
    lines = jnp.concatenate([-(site_total[0:3] + long_force[0:3]), site_energy], axis=0)
    lines = jnp.concatenate([lines, jnp.zeros((4, slots), f32)], axis=0)
    hot = (iota((slots, slots), 0) == site_of(coords_of(pos_ref))).astype(f32).astype(bf16)
    lines = exact(lines, hot)
    for axis in range(3):
        force_out[0, 0, axis] = lines[axis : axis + 1]
    energy_out[0, 0] = lines[3:4]


def kernel_params():
    return pltpu.CompilerParams(vmem_limit_bytes=63 * 1024 * 1024)


def whole_box(
    species,
    counts,
    positions,
    ghost_rows,
    neighbours,
    kvec,
    embed,
    radial_one,
    radial_two,
    mix_one,
    mix_two,
    lr_filter,
    read_weight,
    read_bias,
    energy_weight,
):
    axes = ("gx", "gy", "gz")
    vmem = pl.BlockSpec(memory_space=pltpu.VMEM)
    smem = pl.BlockSpec(memory_space=pltpu.SMEM)
    placed = pl.pallas_call(
        place_kernel,
        out_shape=jax.ShapeDtypeStruct((domains, 4, slots), f32),
        in_specs=[smem, vmem, vmem],
        out_specs=vmem,
    )(counts, positions.transpose(0, 1, 3, 2, 4), species)
    shared = lax.all_to_all(placed, axes, 0, 0, tiled=True)
    prepared = pl.pallas_call(
        weights_kernel,
        out_shape=(
            jax.ShapeDtypeStruct((table, chan), f32),
            jax.ShapeDtypeStruct((half, pad, pad), bf16),
            jax.ShapeDtypeStruct((pad, 384), bf16),
            jax.ShapeDtypeStruct((2, 128, 128), bf16),
            jax.ShapeDtypeStruct((2, 256, 128), bf16),
            jax.ShapeDtypeStruct((2, 128, 256), bf16),
            jax.ShapeDtypeStruct((2, chan, chan), bf16),
            jax.ShapeDtypeStruct((half, 256, 128), bf16),
            jax.ShapeDtypeStruct((8, 128), f32),
        ),
        in_specs=[vmem] * 10,
        out_specs=(vmem,) * 9,
        compiler_params=kernel_params(),
    )(
        kvec,
        lr_filter,
        embed,
        radial_one,
        radial_two,
        mix_one,
        mix_two,
        read_weight,
        read_bias.reshape(1, chan),
        energy_weight.reshape(1, chan),
    )
    place = jnp.stack([lax.axis_index(axis) for axis in axes]).astype(jnp.int32)
    energies, forces = box_call(place, shared, positions.transpose(0, 1, 3, 2, 4), prepared)
    return (energies, forces.transpose(0, 1, 3, 2, 4))


def box_call(place, shared, coords, prepared):
    vmem = pl.BlockSpec(memory_space=pltpu.VMEM)
    smem = pl.BlockSpec(memory_space=pltpu.SMEM)
    grid_shape = (ext, ext, ext, planes, 128)
    return pl.pallas_call(
        box_kernel,
        out_shape=(
            jax.ShapeDtypeStruct((1, 1, 1, slots), f32),
            jax.ShapeDtypeStruct((1, 1, 3, 1, slots), f32),
        ),
        in_specs=[smem] + [vmem] * 11,
        out_specs=(vmem, vmem),
        scratch_shapes=[
            pltpu.VMEM((cells // 128, 64 * 16, 128), f32),
            pltpu.VMEM((64, pad), f32),
            pltpu.VMEM((2, rows_all, 128), f32),
            pltpu.VMEM((half, rows_all, pad), f32),
            pltpu.VMEM((table, domains * slots), bf16),
            pltpu.VMEM((table, cells), bf16),
            pltpu.VMEM(grid_shape, f32),
            pltpu.VMEM(grid_shape, f32),
            pltpu.VMEM(grid_shape, f32),
            pltpu.VMEM((domains * slots, 128), f32),
            pltpu.VMEM((2, pad, 128), f32),
            pltpu.VMEM((8, domains * slots), f32),
            pltpu.VMEM((rows_all, pad), bf16),
            pltpu.VMEM((table, 128), f32),
            pltpu.VMEM((2, cells, chan), f32),
        ],
        compiler_params=kernel_params(),
    )(place, shared, coords, *prepared)


def solution(mesh):
    in_specs = (
        P(("group", "gx"), "gy", "gz", None),
        P(("group", "gx"), "gy", "gz"),
        P(("group", "gx"), "gy", "gz", None, None),
        P(("group", "gx"), "gy", "gz", None),
        P(("group", "gx"), "gy", "gz", None, None),
        P(),
        P(),
        P(),
        P(),
        P(),
        P(),
        P(),
        P(),
        P(),
        P(),
    )
    out_specs = (P(("group", "gx"), "gy", "gz", None), P(("group", "gx"), "gy", "gz", None, None))
    sizes = tuple(mesh.shape[axis] for axis in ("gx", "gy", "gz"))
    plan = whole_box if sizes == grid_dims else local
    return jax.shard_map(plan, mesh=mesh, in_specs=in_specs, out_specs=out_specs, check_vma=False)
```

```python
import math

import jax
import jax.numpy as jnp
import numpy as np
from jax import lax
from jax.experimental import pallas as pl
from jax.experimental.pallas import tpu as pltpu
from jax.sharding import PartitionSpec as P

SIDE = 6
KVEC = 4096
NBASIS = 8
NEIGH = 26


spacing = 2.5
cutoff = 5.0
two_pi = 6.283185307179586
highest = lax.Precision.HIGHEST


def passed_along(block, axis, distance):
    devices = range(lax.axis_size(axis))
    route = [((i - distance) % len(devices), i) for i in devices]
    return lax.ppermute(block, axis, route)


def extended(block, sides, width):
    for axis, dim in sides:
        count = lax.axis_size(axis)
        forward = [(i, i + 1) for i in range(count - 1)]
        forward.append((count - 1, 0))
        backward = [(target, source) for source, target in forward]
        low = lax.ppermute(
            lax.slice_in_dim(block, block.shape[dim] - width, None, axis=dim), axis, forward
        )
        high = lax.ppermute(lax.slice_in_dim(block, 0, width, axis=dim), axis, backward)
        block = jnp.concatenate([low, block, high], axis=dim)
    return block


def rows_per_block():
    return SIDE * SIDE


def boundary_list(side):
    site_ids = np.arange(side**3).reshape(side, side, side)
    inner = np.zeros((side, side, side), dtype=bool)
    inner[1 : side - 1, 1 : side - 1, 1 : side - 1] = True
    return site_ids[~inner].astype(np.int32)


def radial_terms(distance):
    centres = cutoff * jnp.arange(NBASIS).astype(jnp.float32) / (NBASIS - 1)
    sharpness = (NBASIS / cutoff) ** 2
    gap_value = distance[None] - centres[:, None, None]
    gaussian = jnp.exp(-sharpness * gap_value * gap_value)
    envelope_base = jnp.maximum(1.0 - distance * distance / (cutoff * cutoff), 0.0)
    envelope = envelope_base * envelope_base
    envelope_slope = -4.0 * distance * envelope_base / (cutoff * cutoff)
    radial_value = gaussian * envelope[None]
    radial_slope = gaussian * (envelope_slope[None] - 2.0 * sharpness * gap_value * envelope[None])
    return (radial_value, radial_slope)


def embed_codes(type_code, embed):
    species_ids = jnp.arange(1, embed.shape[0] + 1, dtype=jnp.int32).astype(type_code.dtype)
    one_hot = (type_code[None, :] == species_ids[:, None]).astype(jnp.float32)
    return jnp.dot(embed.T, one_hot, precision=highest, preferred_element_type=jnp.float32)


def cell_shift():
    ext_side = SIDE + 2
    cells = jnp.arange(ext_side**3, dtype=jnp.int32)
    coords = jnp.stack(
        [cells // (ext_side * ext_side), cells // ext_side % ext_side, cells % ext_side]
    )
    domain_width = SIDE * spacing
    return jnp.where(
        coords == 0, -domain_width, jnp.where(coords == ext_side - 1, domain_width, 0.0)
    ).astype(jnp.float32)


def pair_geometry(coords_own, pool_coords, pair_lists):
    separation = jnp.take(pool_coords, pair_lists, axis=1) - coords_own[:, None, :]
    distance = jnp.sqrt(jnp.sum(separation * separation, axis=0))
    return (separation, distance)


def message_forward(pool_values, pair_lists, radial_value, radial_weight):
    radial_filter = jnp.einsum("bc,bma->cma", radial_weight, radial_value, precision=highest)
    neighbour_value = jnp.take(pool_values, pair_lists, axis=1)
    return jnp.sum(radial_filter * neighbour_value, axis=1)


def message_backward(
    grad_message,
    pool_values,
    pair_lists,
    radial_value,
    radial_slope,
    radial_weight,
    separation,
    distance,
    pool_size,
    with_features,
):
    neighbour_value = jnp.take(pool_values, pair_lists, axis=1)
    contracted = jnp.einsum(
        "bc,cma->bma", radial_weight, grad_message[:, None, :] * neighbour_value, precision=highest
    )
    energy_slope = jnp.sum(radial_slope * contracted, axis=0)
    pair_force = separation * (energy_slope / distance)[None]
    flat_index = pair_lists.reshape(-1)
    grad_pool = (
        jnp.zeros((3, pool_size), jnp.float32).at[:, flat_index].add(pair_force.reshape(3, -1))
    )
    grad_own = -jnp.sum(pair_force, axis=1)
    if with_features:
        radial_filter = jnp.einsum("bc,bma->cma", radial_weight, radial_value, precision=highest)
        spread = (radial_filter * grad_message[:, None, :]).reshape(radial_filter.shape[0], -1)
        feature_pool = (
            jnp.zeros((radial_filter.shape[0], pool_size), jnp.float32)
            .at[:, flat_index]
            .add(spread)
        )
        return (grad_pool, grad_own, feature_pool)
    return (grad_pool, grad_own, grad_pool)


def phase_table(fraction, wave_numbers):
    phase_angle = two_pi * (
        fraction[0][:, None] * wave_numbers[0][None, :]
        + fraction[1][:, None] * wave_numbers[1][None, :]
        + fraction[2][:, None] * wave_numbers[2][None, :]
    )
    return (jnp.cos(phase_angle).astype(jnp.bfloat16), jnp.sin(phase_angle).astype(jnp.bfloat16))


def read_long(cosine_low, sine_low, filtered):
    dims = (((1,), (1,)), ((), ()))
    return lax.dot_general(
        filtered[0], cosine_low, dims, preferred_element_type=jnp.float32
    ) + lax.dot_general(filtered[1], sine_low, dims, preferred_element_type=jnp.float32)


def block_live(step_index, live_count):
    block_rows = rows_per_block()
    per_member = SIDE**3 // block_rows
    first_row = (step_index % per_member * block_rows).astype(jnp.float32)
    return first_row < live_count[step_index // per_member]


def lr_struct(fraction, row_values, live_count, wave_numbers):
    block_rows = rows_per_block()
    blocks = fraction.shape[1] // block_rows

    def step(step_index, running):

        def work(running):
            offset = step_index * block_rows
            frac_block = lax.dynamic_slice_in_dim(fraction, offset, block_rows, 1)
            feature_block = lax.dynamic_slice_in_dim(row_values, offset, block_rows, 1)
            cosine_low, sine_low = phase_table(frac_block, wave_numbers)
            term = jnp.stack(
                [
                    jnp.dot(feature_block, cosine_low, preferred_element_type=jnp.float32),
                    jnp.dot(feature_block, sine_low, preferred_element_type=jnp.float32),
                ]
            )
            return running + term

        return lax.cond(
            block_live(step_index, live_count), work, lambda unchanged: unchanged, running
        )

    initial = jnp.zeros((2, row_values.shape[0], wave_numbers.shape[1]), jnp.float32)
    return lax.fori_loop(0, blocks, step, initial)


def lr_read(fraction, live_count, wave_numbers, filtered):
    block_rows = rows_per_block()
    blocks = fraction.shape[1] // block_rows

    def step(step_index, result):

        def work(result):
            offset = step_index * block_rows
            cosine_low, sine_low = phase_table(
                lax.dynamic_slice_in_dim(fraction, offset, block_rows, 1), wave_numbers
            )
            return lax.dynamic_update_slice_in_dim(
                result, read_long(cosine_low, sine_low, filtered), offset, 1
            )

        return lax.cond(
            block_live(step_index, live_count), work, lambda unchanged: unchanged, result
        )

    initial = jnp.zeros((filtered.shape[1], fraction.shape[1]), jnp.float32)
    return lax.fori_loop(0, blocks, step, initial)


def lr_back(
    fraction,
    rounded_rows,
    grad_rows,
    occupied_rows,
    live_count,
    wave_numbers,
    wave_factors,
    filtered,
    back_filtered,
):
    block_rows = rows_per_block()
    blocks = fraction.shape[1] // block_rows
    dims = (((0,), (0,)), ((), ()))
    right_real = jnp.concatenate([filtered[0], back_filtered[0]], axis=0)
    right_imag = jnp.concatenate([filtered[1], back_filtered[1]], axis=0)

    def step(step_index, carried):

        def work(carried):
            grad_long, force_long = carried
            offset = step_index * block_rows
            cosine_low, sine_low = phase_table(
                lax.dynamic_slice_in_dim(fraction, offset, block_rows, 1), wave_numbers
            )
            mask_block = lax.dynamic_slice_in_dim(occupied_rows, offset, block_rows, 0)
            grad_block = mask_block[None] * read_long(cosine_low, sine_low, back_filtered)
            stacked_left = jnp.concatenate(
                [
                    lax.dynamic_slice_in_dim(grad_rows, offset, block_rows, 1),
                    lax.dynamic_slice_in_dim(rounded_rows, offset, block_rows, 1),
                ],
                axis=0,
            )
            real_part = lax.dot_general(
                stacked_left, right_real, dims, preferred_element_type=jnp.float32
            )
            imag_part = lax.dot_general(
                stacked_left, right_imag, dims, preferred_element_type=jnp.float32
            )
            turning = (
                cosine_low.astype(jnp.float32) * imag_part
                - sine_low.astype(jnp.float32) * real_part
            )
            force_block = lax.dot_general(
                wave_factors,
                turning,
                (((1,), (1,)), ((), ())),
                precision=highest,
                preferred_element_type=jnp.float32,
            )
            return (
                lax.dynamic_update_slice_in_dim(grad_long, grad_block, offset, 1),
                lax.dynamic_update_slice_in_dim(force_long, force_block, offset, 1),
            )

        return lax.cond(
            block_live(step_index, live_count), work, lambda unchanged: unchanged, carried
        )

    initial = (
        jnp.zeros((rounded_rows.shape[0], fraction.shape[1]), jnp.float32),
        jnp.zeros((3, fraction.shape[1]), jnp.float32),
    )
    return lax.fori_loop(0, blocks, step, initial)


def boundary_grid(values, ghost_slots, boundary):
    picked = jnp.take(values, ghost_slots, axis=1)
    site_grid = jnp.zeros((values.shape[0], SIDE**3), values.dtype).at[:, boundary].set(picked)
    return site_grid.reshape(values.shape[0], SIDE, SIDE, SIDE)


def fold_slab(site_grid, axis_number, from_left, from_right):
    inner_size = site_grid.shape[axis_number] - 2
    inner = lax.slice_in_dim(site_grid, 1, inner_size + 1, axis=axis_number)
    first_layer = lax.slice_in_dim(inner, 0, 1, axis=axis_number) + from_left
    last_layer = lax.slice_in_dim(inner, inner_size - 1, inner_size, axis=axis_number) + from_right
    middle = lax.slice_in_dim(inner, 1, inner_size - 1, axis=axis_number)
    return jnp.concatenate([first_layer, middle, last_layer], axis=axis_number)


def return_halo(site_grid):
    edge = site_grid.shape[3] - 1
    received = [
        passed_along(
            lax.slice_in_dim(site_grid, slab_start, slab_start + 1, axis=3), "gz", direction
        )
        for direction, slab_start in ((1, edge), (-1, 0))
    ]
    site_grid = fold_slab(site_grid, 3, received[0], received[1])
    edge = site_grid.shape[2] - 1
    received = [
        passed_along(
            lax.slice_in_dim(site_grid, slab_start, slab_start + 1, axis=2), "gy", direction
        )
        for direction, slab_start in ((1, edge), (-1, 0))
    ]
    site_grid = fold_slab(site_grid, 2, received[0], received[1])
    edge = site_grid.shape[1] - 1
    received = [
        passed_along(
            lax.slice_in_dim(site_grid, slab_start, slab_start + 1, axis=1), "gx", direction
        )
        for direction, slab_start in ((1, edge), (-1, 0))
    ]
    return fold_slab(site_grid, 1, received[0], received[1])


def ghost_to_rows(site_grid, ghost_slots, boundary):
    features = site_grid.shape[0]
    picked = site_grid.reshape(features, -1)[:, boundary]
    return jnp.zeros((features, SIDE**3), site_grid.dtype).at[:, ghost_slots].add(picked)


def local(
    species,
    counts,
    positions,
    ghost_rows,
    neighbours,
    kvec,
    embed,
    radial_one,
    radial_two,
    mix_one,
    mix_two,
    lr_filter,
    read_weight,
    read_bias,
    energy_weight,
):
    slot_count = SIDE**3
    ext_side = SIDE + 2
    pool_size = slot_count + ext_side**3
    pair_scale = 1.0 / math.sqrt(NEIGH)
    domain_width = SIDE * spacing
    mesh_sizes = (lax.axis_size("gx"), lax.axis_size("gy"), lax.axis_size("gz"))
    box_length = tuple((count_along * domain_width for count_along in mesh_sizes))
    wave_scale = 1.0 / math.sqrt(
        KVEC * (slot_count * mesh_sizes[0] * mesh_sizes[1] * mesh_sizes[2])
    )
    species_flat = species.reshape(slot_count)
    live_total = counts.reshape(())
    coords_own = positions.reshape(3, slot_count)
    ghost_slots = ghost_rows.reshape(-1)
    pair_lists = neighbours.reshape(NEIGH, slot_count)
    boundary = jnp.asarray(boundary_list(SIDE))
    cell_offset = cell_shift()
    occupied = (jnp.arange(slot_count, dtype=jnp.int32) < live_total).astype(jnp.float32)
    type_code = jnp.where(occupied > 0, species_flat + 1, 0).astype(jnp.float32)
    hidden_zero = embed_codes(species_flat + 1, embed)
    masked_zero = hidden_zero * occupied[None]
    packet = boundary_grid(
        jnp.concatenate([coords_own, type_code[None]], axis=0), ghost_slots, boundary
    )
    ext_atoms = extended(packet, (("gx", 1), ("gy", 2), ("gz", 3)), 1).reshape(4, -1)
    pool_coords = jnp.concatenate([coords_own, ext_atoms[:3] + cell_offset], axis=1)
    pool_zero = jnp.concatenate([masked_zero, embed_codes(ext_atoms[3], embed)], axis=1)
    separation, distance = pair_geometry(coords_own, pool_coords, pair_lists)
    radial_value, radial_slope = radial_terms(distance)
    message = message_forward(pool_zero, pair_lists, radial_value, radial_one)
    hidden_one = hidden_zero + pair_scale * jnp.dot(
        mix_one.T, message, precision=highest, preferred_element_type=jnp.float32
    )
    masked_one = hidden_one * occupied[None]
    rounded_one = masked_one.astype(jnp.bfloat16)
    domain_pos = (lax.axis_index("gx"), lax.axis_index("gy"), lax.axis_index("gz"))
    fraction = jnp.stack(
        [
            (domain_pos[axis_id].astype(jnp.float32) * domain_width + coords_own[axis_id])
            / box_length[axis_id]
            for axis_id in range(3)
        ]
    )
    wave_numbers = kvec.astype(jnp.float32)
    wave_factors = jnp.stack(
        [two_pi * wave_numbers[axis_id] / box_length[axis_id] for axis_id in range(3)]
    )
    own_count = jnp.sum(occupied)[None]
    share_size = KVEC // (mesh_sizes[0] * mesh_sizes[1] * mesh_sizes[2])
    share_start = lax.axis_index(("gx", "gy", "gz")) * share_size
    filter_share = lax.dynamic_slice_in_dim(lr_filter, share_start, share_size, 1)
    struct_part = lax.psum_scatter(
        lr_struct(fraction, rounded_one, own_count, wave_numbers),
        ("gx", "gy", "gz"),
        scatter_dimension=2,
        tiled=True,
    )
    filtered = lax.all_gather(
        (struct_part * filter_share[None] * wave_scale).astype(jnp.bfloat16),
        ("gx", "gy", "gz"),
        axis=2,
        tiled=True,
    )
    long_part = lr_read(fraction, own_count, wave_numbers, filtered)
    masked_ext = extended(
        boundary_grid(masked_one, ghost_slots, boundary).astype(jnp.bfloat16),
        (("gx", 1), ("gy", 2), ("gz", 3)),
        1,
    ).astype(jnp.float32)
    pool_one = jnp.concatenate([masked_one, masked_ext.reshape(masked_one.shape[0], -1)], axis=1)
    message_two = message_forward(pool_one, pair_lists, radial_value, radial_two)
    hidden_two = (
        hidden_one
        + pair_scale
        * jnp.dot(mix_two.T, message_two, precision=highest, preferred_element_type=jnp.float32)
        + long_part
    )
    activation = (
        jnp.dot(read_weight.T, hidden_two, precision=highest, preferred_element_type=jnp.float32)
        + read_bias[:, None]
    )
    gating = jax.nn.sigmoid(activation)
    energies = occupied * jnp.sum(activation * gating * energy_weight[:, None], axis=0)
    grad_act = (
        occupied[None] * energy_weight[:, None] * gating * (1.0 + activation * (1.0 - gating))
    )
    grad_two = jnp.dot(read_weight, grad_act, precision=highest, preferred_element_type=jnp.float32)
    grad_low = grad_two.astype(jnp.bfloat16)
    grad_part = lax.psum_scatter(
        lr_struct(fraction, grad_low, own_count, wave_numbers),
        ("gx", "gy", "gz"),
        scatter_dimension=2,
        tiled=True,
    )
    back_filtered = lax.all_gather(
        (grad_part * filter_share[None] * wave_scale).astype(jnp.bfloat16),
        ("gx", "gy", "gz"),
        axis=2,
        tiled=True,
    )
    grad_long, force_long = lr_back(
        fraction,
        rounded_one,
        grad_low,
        occupied,
        own_count,
        wave_numbers,
        wave_factors,
        filtered,
        back_filtered,
    )
    grad_message = pair_scale * jnp.dot(
        mix_two, grad_two, precision=highest, preferred_element_type=jnp.float32
    )
    grad_pool, grad_own_two, feature_pool = message_backward(
        grad_message,
        pool_one,
        pair_lists,
        radial_value,
        radial_slope,
        radial_two,
        separation,
        distance,
        pool_size,
        True,
    )
    combined = jnp.concatenate([feature_pool, grad_pool], axis=0)
    features = combined.shape[0]
    returned_two = ghost_to_rows(
        return_halo(combined[:, slot_count:].reshape(features, ext_side, ext_side, ext_side)),
        ghost_slots,
        boundary,
    )
    own_two = combined[:, :slot_count]
    channels = masked_one.shape[0]
    grad_one = (
        grad_two + grad_long + occupied[None] * (own_two[:channels] + returned_two[:channels])
    )
    grad_message_one = pair_scale * jnp.dot(
        mix_one, grad_one, precision=highest, preferred_element_type=jnp.float32
    )
    grad_pool_one, grad_own_one, unused = message_backward(
        grad_message_one,
        pool_zero,
        pair_lists,
        radial_value,
        radial_slope,
        radial_one,
        separation,
        distance,
        pool_size,
        False,
    )
    layer_one_grad = grad_own_one + grad_pool_one[:, :slot_count]
    returned_one = ghost_to_rows(
        return_halo(grad_pool_one[:, slot_count:].reshape(3, ext_side, ext_side, ext_side)),
        ghost_slots,
        boundary,
    )
    total_grad = (
        layer_one_grad
        + returned_one
        + force_long
        + grad_own_two
        + own_two[channels:]
        + returned_two[channels:]
    )
    forces = -total_grad
    return (energies.reshape(1, 1, 1, slot_count), forces.reshape(1, 1, 1, 3, slot_count))


offsets = tuple(
    (ox, oy, oz)
    for ox in (0, 1)
    for oy in (-1, 0, 1)
    for oz in (-1, 0, 1)
    if (ox, oy, oz) > (0, 0, 0)
)
half = len(offsets)
slots = SIDE**3
ext = SIDE + 2
cells = ext**3
inner_lanes = SIDE * ext * ext
reach = ext * ext + 2 * ext
chan = 64
grid_dims = (4, 2, 2)
domains = 16
planes = 8
rows_all = slots * planes
waves = 648
table = 2 * waves
pad = 256
span = -(-rows_all // 128) * 128
gamma = (NBASIS / cutoff) ** 2
step = cutoff / (NBASIS - 1)
nt = (((1,), (1,)), ((), ()))
nn = (((1,), (0,)), ((), ()))
f32 = jnp.float32
bf16 = jnp.bfloat16


def dot(left, right, dims=nn, precision=None):
    return lax.dot_general(left, right, dims, precision=precision, preferred_element_type=f32)


def split(value):
    high = value.astype(bf16)
    return high, (value - high.astype(f32)).astype(bf16)


def dot_split(left, high, low):
    left_high, left_low = split(left)
    return dot(left_high, high) + dot(left_low, high) + dot(left_high, low)


def exact(left, hot, dims=nn):
    high = left.astype(bf16).astype(f32)
    rest = left - high
    middle = rest.astype(bf16).astype(f32)
    count = left.shape[0]
    stacked = jnp.concatenate([high, middle, rest - middle], axis=0).astype(bf16)
    parts = dot(stacked, hot, dims)
    return parts[:count] + parts[count : 2 * count] + parts[2 * count :]


def coords_of(ref):
    return jnp.concatenate([ref[0, 0, axis] for axis in range(3)], axis=0)


def site_of(coords):
    where = (coords * (1.0 / spacing)).astype(jnp.int32)
    return (where[0:1] * SIDE + where[1:2]) * SIDE + where[2:3]


def iota(shape, dim):
    return lax.broadcasted_iota(jnp.int32, shape, dim)


def place_kernel(count_ref, pos_ref, species_ref, out_ref):
    coords = coords_of(pos_ref)
    live = iota((1, slots), 1) < count_ref[0, 0, 0]
    code = jnp.where(live, species_ref[0, 0] + 1, 0).astype(f32)
    data = jnp.concatenate([coords, code, jnp.zeros((4, slots), f32)], axis=0)
    hot = (iota((slots, slots), 0) == site_of(coords)).astype(f32).astype(bf16)
    placed = exact(data, hot, nt)[0:4]
    for number in range(domains):
        out_ref[number] = placed


def twice(block):
    zero = jnp.zeros_like(block)
    return jnp.concatenate(
        [jnp.concatenate([block, zero], axis=1), jnp.concatenate([zero, block], axis=1)], axis=0
    )


def gain_kernel(kvec_ref, filter_ref, gain_ref):
    wave_scale = 1.0 / math.sqrt(KVEC * slots * domains)
    waves_in = kvec_ref[...]

    def folded(row):
        return jnp.where(row > 0, 2 * row - 1, -2 * row)

    index = (folded(waves_in[1:2]) * 9 + folded(waves_in[2:3])) * 8 + waves_in[0:1] - 1
    filter_high, filter_low = split(filter_ref[...] * wave_scale)
    parts = jnp.concatenate([filter_high, filter_low], axis=0)
    gain = jnp.zeros((waves, 2 * chan), f32)
    width = 1024
    for start in range(0, KVEC, width):
        hot = (iota((waves, width), 0) == index[:, start : start + width]).astype(f32).astype(bf16)
        gain = gain + dot(hot, parts[:, start : start + width], nt)
    gain = (gain[:, :chan] + gain[:, chan:]).reshape(waves // 8, 8, chan)
    gain_ref[...] = jnp.concatenate([gain, gain], axis=1).reshape(table, chan).T


def turn(fraction):
    rest = fraction - jnp.floor(fraction + 0.5)
    angle = rest * (0.5 * two_pi)
    square = angle * angle
    sine = angle * (
        1.0
        + square
        * (
            -1.0 / 6
            + square
            * (
                1.0 / 120
                + square * (-1.0 / 5040 + square * (1.0 / 362880 - square * (1.0 / 39916800)))
            )
        )
    )
    cosine = 1.0 + square * (
        -0.5
        + square
        * (
            1.0 / 24
            + square
            * (
                -1.0 / 720
                + square
                * (1.0 / 40320 + square * (-1.0 / 3628800 + square * (1.0 / 479001600)))
            )
        )
    )
    return 1.0 - 2.0 * sine * sine, 2.0 * sine * cosine


def fan(base, step_pairs):
    real, imag = base
    out = [(real, imag)]
    for cosine, sine in step_pairs:
        a, b, c, d = real * cosine, imag * sine, real * sine, imag * cosine
        out.append((a - b, c + d))
        out.append((a + b, d - c))
    return out


def wave_tile(coords, store):
    frac = [coords[axis] / (grid_dims[axis] * SIDE * spacing) for axis in range(3)]
    row = iota((8, 128), 0)
    base = turn(frac[0] * (row + 1).astype(f32))
    rest = turn(jnp.where(row < 4, frac[1], frac[2]) * (row % 4 + 1).astype(f32))

    def line(index):
        return tuple(jnp.broadcast_to(part[index : index + 1], (8, 128)) for part in rest)

    y_lines = [line(index) for index in range(4)]
    z_lines = [line(index + 4) for index in range(4)]
    index = 0
    for level in fan(base, y_lines):
        for real, imag in fan(level, z_lines):
            store(index, jnp.concatenate([real, imag], axis=0).astype(bf16))
            index += 1
        yield index


def swap_lanes(value):
    return pltpu.roll(value, chan, value.ndim - 1)


def swap_planes(value):
    up = pltpu.roll(value, 1, 1)
    down = pltpu.roll(value, planes - 1, 1)
    return jnp.where(iota(value.shape, 1) % 2 == 0, down, up)


def as_three(value):
    return value.reshape((-1,) + value.shape[-2:])


def fill_ghosts(ref):
    inner = slice(1, SIDE + 1)
    for ghost, source, shift in ((0, SIDE, 2), (SIDE + 1, 1, planes - 2)):
        value = ref[source, inner, inner]
        ref[ghost, inner, inner] = pltpu.roll(as_three(value), shift, 1).reshape(value.shape)
    for ghost, source in ((0, SIDE), (SIDE + 1, 1)):
        value = ref[:, source, inner]
        ref[:, ghost, inner] = swap_planes(as_three(value)).reshape(value.shape)
    for ghost, source in ((0, SIDE), (SIDE + 1, 1)):
        value = ref[:, :, source]
        ref[:, :, ghost] = swap_lanes(as_three(value)).reshape(value.shape)


def fold_ghosts(ref):
    inner = slice(1, SIDE + 1)
    for ghost, target in ((SIDE + 1, 1), (0, SIDE)):
        value = ref[:, :, ghost]
        ref[:, :, target] = ref[:, :, target] + swap_lanes(as_three(value)).reshape(value.shape)
    for ghost, target in ((SIDE + 1, 1), (0, SIDE)):
        value = ref[:, ghost, inner]
        ref[:, target, inner] = ref[:, target, inner] + swap_planes(as_three(value)).reshape(
            value.shape
        )
    for ghost, target, shift in ((SIDE + 1, 1, 2), (0, SIDE, planes - 2)):
        value = ref[ghost, inner, inner]
        ref[target, inner, inner] = ref[target, inner, inner] + pltpu.roll(
            as_three(value), shift, 1
        ).reshape(value.shape)


def inner_rows(ref, level):
    inner = slice(1, SIDE + 1)
    return ref[level + 1, inner, inner].reshape(rows_all // SIDE, 128)


def set_level(ref, level, value):
    inner = slice(1, SIDE + 1)
    ref[level + 1, inner, inner] = value.reshape(SIDE, SIDE, planes, 128)


def level_rows(level):
    return slice(level * (rows_all // SIDE), (level + 1) * (rows_all // SIDE))


def set_inner(ref, value):
    inner = slice(1, SIDE + 1)
    ref[inner, inner, inner] = value.reshape(SIDE, SIDE, SIDE, planes, 128)


def convolve(filters, layer, source, target, beside=None):
    target[...] = jnp.zeros(target.shape, f32)
    lanes = slice(layer * 128, layer * 128 + 128)
    groups = {}
    for number, (ox, oy, oz) in enumerate(offsets):
        groups.setdefault((ox, oy), []).append((number, oz))

    def one_line(line):
        x = line // SIDE
        y = line % SIDE
        own = [source[x + 1, y + 1, z + 1] for z in range(SIDE)]
        own_sum = [jnp.zeros((planes, 128), f32)] * SIDE
        for (ox, oy), members in groups.items():
            there = [source[x + 1 + ox, y + 1 + oy, z] for z in range(ext)]
            sums = [None] * ext
            first = pl.multiple_of(line * (SIDE * planes), SIDE * planes)
            weights = [
                filters[number, pl.ds(first, SIDE * planes), lanes].astype(f32)
                for number, _ in members
            ]
            for z in range(SIDE):
                for block, (_, oz) in zip(weights, members):
                    weight = block[z * planes : z * planes + planes]
                    own_sum[z] = own_sum[z] + weight * there[z + 1 + oz]
                    term = weight * own[z]
                    spot = z + 1 + oz
                    sums[spot] = term if sums[spot] is None else sums[spot] + term
            for z in range(ext):
                if sums[z] is not None:
                    target[x + 1 + ox, y + 1 + oy, z] = target[x + 1 + ox, y + 1 + oy, z] + sums[z]
        for z in range(SIDE):
            target[x + 1, y + 1, z + 1] = target[x + 1, y + 1, z + 1] + own_sum[z]

    def body(number, carry):
        if beside is not None:
            beside(number)
        for part in range(3):
            one_line(number * 3 + part)
        return carry

    lax.fori_loop(0, SIDE * SIDE // 3, body, 0)
    fold_ghosts(target)


def spread(block):
    return jnp.broadcast_to(block[:, None, :], (NBASIS, 16, chan)).reshape(128, chan)


def wide(left, right):
    left, right = spread(left), spread(right)
    line = jnp.concatenate([left, left, right, right], axis=1)
    return jnp.concatenate([line, line], axis=0)


def doubled(ref):
    return jnp.concatenate([ref[...], ref[...]], axis=1)


def box_kernel(
    all_ref,
    pos_ref,
    gain_ref,
    embed_ref,
    radial_one_ref,
    radial_two_ref,
    mix_one_ref,
    mix_two_ref,
    read_ref,
    bias_ref,
    energy_ref,
    energy_out,
    force_out,
    sep_ref,
    sites_ref,
    basis_ref,
    filters_ref,
    waves_ref,
    ring_ref,
    zero_ref,
    one_ref,
    sum_ref,
    packed_ref,
    own_ref,
    flat_ref,
    low_ref,
    saved_ref,
    radial_ref,
    shift_ref,
):
    home = [lax.axis_index(axis) for axis in ("gx", "gy", "gz")]
    pair_scale = 1.0 / math.sqrt(NEIGH)
    fall = jnp.exp(-gamma * jnp.square(step * iota((NBASIS, 1), 0).astype(f32)))
    rows = iota((pad, pad), 0)
    columns = iota((pad, pad), 1)
    kept = (rows // 128) == (columns % 128 // chan)
    radial_ref[...] = jnp.where(
        kept, wide(radial_one_ref[...] * fall, radial_two_ref[...] * fall), 0.0
    )
    table_rows = jnp.concatenate([embed_ref[...], jnp.zeros((2, chan), f32)], axis=0)
    table_high = table_rows.astype(bf16).astype(f32)
    species_rows = kept & (rows % 16 == half)
    embeds = jnp.where(species_rows, wide(table_high, table_rows - table_high), 0.0).astype(bf16)
    lives = jnp.where(species_rows[:, :128], 1.0, 0.0).astype(bf16)
    sites_ref[...] = jnp.zeros((4 * domains, pad), f32)
    flat_ref[...] = jnp.zeros(flat_ref.shape, f32)
    domain_width = SIDE * spacing
    offset_row = iota((4, slots), 0)
    for number in range(domains):
        spot = [
            lax.rem(home[axis] + part, grid_dims[axis])
            for axis, part in enumerate((number // 4, number // 2 % 2, number % 2))
        ]
        block = all_ref[(spot[0] * 2 + spot[1]) * 2 + spot[2]]
        sites_ref[number * 4 : number * 4 + 4, 0:slots] = block
        shifts = [part * domain_width for part in (number // 4, number // 2 % 2, number % 2)]
        moved = jnp.where(
            offset_row == 0, shifts[0], jnp.where(offset_row == 1, shifts[1], shifts[2])
        )
        start = number % 2 * span + number // 2 * slots
        flat_ref[0:4, start : start + slots] = block + moved
    sites = sites_ref[:, 0:slots]

    lane = iota((1, cells), 1)
    coords = [(lane // (ext * ext) + 1) % ext, lane // ext % ext, lane % ext]
    wrapped = [(value + SIDE - 1) % SIDE for value in coords]
    wrapped_site = (wrapped[0] * SIDE + wrapped[1]) * SIDE + wrapped[2]
    inside = coords[0] >= 0
    for value in coords:
        inside = inside & (value > 0) & (value < ext - 1)
    hot_all = iota((slots, cells), 0) == wrapped_site
    grown = exact(sites, hot_all.astype(f32).astype(bf16))
    picks = (hot_all & inside)[:, :inner_lanes].astype(f32).astype(bf16)

    back16 = jnp.concatenate([grown[48:], grown[:48]], axis=0)
    ahead16 = jnp.concatenate([grown[16:], grown[:16]], axis=0)
    grown = jnp.where(coords[0] == 0, back16, jnp.where(coords[0] == ext - 1, ahead16, grown))
    swapped = jnp.concatenate(
        [grown[8 * (part ^ 1) : 8 * (part ^ 1) + 8] for part in range(8)], axis=0
    )
    grown = jnp.where((coords[1] == 0) | (coords[1] == ext - 1), swapped, grown)
    swapped = pltpu.roll(grown.reshape(8, 8, cells), 4, 1).reshape(64, cells)
    grown = jnp.where((coords[2] == 0) | (coords[2] == ext - 1), swapped, grown)
    component = iota((64, cells), 0) % 4
    for axis in range(3):
        moved = jnp.where(
            coords[axis] == 0,
            -domain_width,
            jnp.where(coords[axis] == ext - 1, domain_width, 0.0),
        )
        grown = grown + jnp.where(component == axis, moved, 0.0)
    own_ext = grown[0:4]
    tiles = cells // 128

    def put_sep(number, value):
        for tile in range(tiles):
            sep_ref[tile, pl.ds(number, 64, stride=16), :] = value[:, tile * 128 : tile * 128 + 128]

    def get_sep(window, count=tiles):
        return jnp.concatenate([sep_ref[tile, window, :] for tile in range(count)], axis=1)

    for number, (ox, oy, oz) in enumerate(offsets):
        distance = (ox * ext + oy) * ext + oz
        put_sep(number, pltpu.roll(grown, cells - distance, 1) - grown)
    for number in range(half, 16):
        put_sep(number, grown)

    basis_unroll = 4
    row16 = iota((16, inner_lanes), 0)

    def basis_of(domain):
        first = pl.multiple_of(domain * 64, 64)
        sx, sy, sz, codes = [get_sep(pl.ds(first + 16 * part, 16), inner_lanes // 128) for part in range(4)]
        square = sx * sx + sy * sy + sz * sz
        near = jnp.minimum(jnp.sqrt(square), cutoff)
        base = jnp.maximum(1.0 - square * (1.0 / (cutoff * cutoff)), 0.0)
        value = jnp.exp(-gamma * jnp.minimum(square, cutoff * cutoff)) * base * base
        ratio = jnp.exp((2.0 * gamma * step) * near)
        out = []
        for number in range(NBASIS):
            hit = jnp.where(codes == number + 1.0, 1.0, 0.0)
            out.append(jnp.where(row16 == half, hit, value))
            value = value * ratio
        return jnp.concatenate(out, axis=0).astype(bf16)

    def basis_step(plane, carry):
        both = jnp.concatenate([basis_of(2 * plane), basis_of(2 * plane + 1)], axis=0)
        picked = dot(picks, both, nt)
        for tile in range(2):
            basis_ref[tile, pl.ds(plane, slots, stride=planes), :] = picked[
                :, tile * 128 : tile * 128 + 128
            ]
        return carry

    def basis_group(number, carry):
        for part in range(basis_unroll):
            basis_step(number * basis_unroll + part, carry)
        return carry

    lax.fori_loop(0, planes // basis_unroll, basis_group, 0)

    basis_low = jnp.concatenate([basis_ref[0], basis_ref[1]], axis=1).astype(bf16)
    low_ref[...] = basis_low

    def flat_tile(start):
        block = flat_ref[:, pl.ds(start, 128)]

        def store(index, value):
            waves_ref[index * 16 : index * 16 + 16, pl.ds(start, 128)] = value

        return wave_tile([block[axis : axis + 1] for axis in range(3)], store)

    def wave_step(number, carry):
        chosen = jnp.where(iota((pad, pad), 0) % 16 == number, radial_ref[...], 0.0)
        chosen = chosen.astype(bf16)
        levels = []
        for part in range(2):
            levels.append(flat_tile(pl.multiple_of(number * 256 + part * 128, 128)))
        rows_each = rows_all // 6
        for part in range(6):
            window = slice(part * rows_each, part * rows_each + rows_each)
            filters_ref[number, window] = dot(low_ref[window], chosen).astype(bf16)
            for _ in range(3):
                next(levels[part // 3])
        return carry

    lax.fori_loop(0, half, wave_step, 0)
    for tile in range(2 * half, 2 * span // 128):
        list(flat_tile(tile * 128))
    for tile in range(cells // 128):
        lanes = slice(tile * 128, tile * 128 + 128)

        def store(index, value):
            ring_ref[index * 16 : index * 16 + 16, lanes] = value

        list(wave_tile([own_ext[axis : axis + 1, lanes] for axis in range(3)], store))

    start_values = dot(low_ref[...], jnp.concatenate([embeds, lives], axis=1))
    rows_ref = basis_ref.at[0]
    live_ref = basis_ref.at[1]
    live_ref[...] = start_values[:, 256:384]
    set_inner(zero_ref, start_values[:, :128] + start_values[:, 128:256])
    fill_ghosts(zero_ref)
    convolve(filters_ref, 0, zero_ref, sum_ref)
    flat = (cells * planes, 128)
    own_cells = pl.ds(0, cells, stride=planes)

    def cells_of(ref):
        value = ref.reshape(flat)[own_cells, :]
        return jnp.concatenate([value[ext * ext :], value[: ext * ext]], axis=0)[:, :chan]

    saved_ref[0] = cells_of(zero_ref)
    mix_high, mix_low = split(twice(mix_one_ref[...] * pair_scale))
    for level in range(SIDE):
        window = level_rows(level)
        first_rows = inner_rows(zero_ref, level) + live_ref[window] * dot_split(
            inner_rows(sum_ref, level), mix_high, mix_low
        )
        set_level(one_ref, level, first_rows)
        rows_ref[window] = first_rows
    fill_ghosts(one_ref)
    saved_ref[1] = cells_of(one_ref)
    two_ref = zero_ref

    def structure():
        for plane in range(planes):
            packed_ref[plane * slots : plane * slots + slots] = rows_ref[
                pl.ds(plane, slots, stride=planes), :
            ]
        turned = packed_ref[...].T
        zeros = jnp.zeros((chan, span - rows_all), f32)
        turned = jnp.concatenate([turned[:chan], zeros, turned[chan:], zeros], axis=1)
        return dot(turned.astype(bf16), waves_ref[...], nt) * gain_ref[...]

    filtered = structure()
    own_ref[...] = jnp.zeros(own_ref.shape, f32)
    own_ref[0, 0:slots] = rows_ref[pl.ds(0, slots, stride=planes), :]
    convolve(filters_ref, 1, one_ref, sum_ref)
    long_rows = dot(filtered.astype(bf16), waves_ref[...]).T
    for plane in range(planes):
        first = long_rows[plane * slots : plane * slots + slots]
        second = long_rows[span + plane * slots : span + plane * slots + slots]
        rows_ref[pl.ds(plane, slots, stride=planes), :] = jnp.concatenate([first, second], axis=1)
    read = read_ref[...]
    both = dot_split(mix_two_ref[...] * pair_scale, *split(read))
    act_high, act_low = split(jnp.concatenate([twice(read), twice(both)], axis=0))
    grad_high, grad_low = split(jnp.concatenate([twice(read.T), twice(both.T)], axis=1))
    bias = doubled(bias_ref)
    energy = doubled(energy_ref)
    for level in range(SIDE):
        window = level_rows(level)
        joined = jnp.concatenate(
            [inner_rows(one_ref, level) + rows_ref[window], inner_rows(sum_ref, level)], axis=1
        )
        act = dot_split(joined, act_high, act_low) + bias
        sig = 1.0 / (1.0 + jnp.exp(-act))
        weighted = live_ref[window] * energy * sig
        packed_ref[window] = weighted * act
        grads = dot_split(weighted * (1.0 + act * (1.0 - sig)), grad_high, grad_low)
        rows_ref[window] = grads[:, :128]
        set_level(two_ref, level, grads[:, 128:])
    own_energy = packed_ref[pl.ds(0, slots, stride=planes), :]
    first_half = jnp.where(iota((8, 128), 1) < chan, 1.0, 0.0)
    energy_high, energy_low = split(own_energy)
    first_half = first_half.astype(bf16)
    site_energy = (dot(first_half, energy_high, nt) + dot(first_half, energy_low, nt))[0:1]
    fill_ghosts(two_ref)
    back = structure()
    own_ref[1, 0:slots] = rows_ref[pl.ds(0, slots, stride=planes), :]
    two_cells = cells_of(two_ref)
    convolve(filters_ref, 1, two_ref, sum_ref)
    back_rows = back.astype(bf16)
    for level in range(SIDE):
        window = level_rows(level)
        set_level(
            sum_ref, level, rows_ref[window] + live_ref[window] * inner_rows(sum_ref, level)
        )
    fill_ghosts(sum_ref)
    sum_cells = cells_of(sum_ref)
    live_cells = jnp.where(own_ext[3:4] > 0, 1.0, 0.0)
    ring_long = (dot(back_rows, ring_ref[...]) * live_cells).T
    grad_cells = dot_split(sum_cells + ring_long, *split(mix_one_ref[...].T * pair_scale))

    def crossed(value):
        value = value.T.reshape(waves // 8, 2, 8, chan)
        value = jnp.concatenate([value[:, 1:2], -value[:, 0:1]], axis=1).reshape(table, chan)
        return jnp.concatenate([value, jnp.zeros((table, chan), f32)], axis=1).astype(bf16)

    response = dot(crossed(filtered), own_ref[1].astype(bf16), nt) + dot(
        crossed(back), own_ref[0].astype(bf16), nt
    )
    turning_high, turning_low = split(waves_ref[:, 0:pad].astype(f32) * response)
    spot = iota((8, table), 1)
    wave = spot // 16 * 8 + spot % 8

    def signed(index):
        return jnp.where(index % 2 == 1, (index + 1) // 2, -(index // 2))

    row = iota((8, table), 0)
    number = jnp.where(
        row == 0,
        wave % 8 + 1,
        jnp.where(row == 1, signed(wave // 72), jnp.where(row == 2, signed(wave // 8 % 9), 0)),
    )
    number = number.astype(f32).astype(bf16)
    scale_row = iota((8, 1), 0)
    scales = jnp.where(
        scale_row == 0,
        two_pi / (grid_dims[0] * domain_width),
        two_pi / (grid_dims[1] * domain_width),
    )
    long_force = (dot(number, turning_high) + dot(number, turning_low))[:, :slots] * scales

    zero_cells = saved_ref[0]
    one_cells = saved_ref[1]
    left = [
        jnp.concatenate([two_cells, one_cells], axis=1),
        jnp.concatenate([grad_cells, zero_cells], axis=1),
    ]
    right = jnp.concatenate(
        [
            jnp.concatenate([one_cells, two_cells], axis=1),
            jnp.concatenate([zero_cells, grad_cells], axis=1),
        ],
        axis=1,
    )
    left = jnp.concatenate(left, axis=1)
    for shift in range(3):
        moved = right if shift == 1 else pltpu.roll(right, (1 - shift) % cells, 0)
        shift_ref[shift, 0:cells] = moved
        shift_ref[shift, cells:] = moved[:reach]
    one, two = radial_one_ref[...], radial_two_ref[...]
    pairs = jnp.concatenate([two, two, one, one], axis=1)
    pairs = jnp.broadcast_to(pairs[:, None, :], (NBASIS, 16, pad)).reshape(128, pad).T
    pair_column = iota((pad, 128), 1) % 16
    shares = jnp.zeros((cells, 128), f32)
    for number, (ox, oy, oz) in enumerate(offsets):
        distance = (ox * ext + oy) * ext
        products = left * shift_ref[oz + 1, distance : distance + cells]
        chosen = jnp.where(pair_column == number, pairs, 0.0).astype(bf16)
        shares = shares + dot(products.astype(bf16), chosen)
    shares = shares.T
    sep = [get_sep(slice(16 * part, 16 * part + 16)) for part in range(3)]
    square = sep[0] * sep[0] + sep[1] * sep[1] + sep[2] * sep[2]
    length = jnp.sqrt(square)
    base = jnp.maximum(1.0 - square * (1.0 / (cutoff * cutoff)), 0.0)
    inward = length * base * (-4.0 / (cutoff * cutoff))
    outward = (-2.0 * gamma) * base * base
    strength = jnp.zeros((16, cells), f32)
    for number in range(NBASIS):
        gap = length - step * number
        slope = jnp.exp(-gamma * gap * gap) * (inward + gap * outward)
        strength = strength + slope * shares[16 * number : 16 * number + 16]
    strength = strength / length
    totals = []
    for part in range(3):
        force = jnp.where(iota((16, cells), 0) < half, sep[part] * strength, 0.0)
        total = -jnp.sum(force, axis=0, keepdims=True)
        for number, (ox, oy, oz) in enumerate(offsets):
            distance = (ox * ext + oy) * ext + oz
            total = total + pltpu.roll(force[number : number + 1], distance, 1)
        totals.append(total)
    total = jnp.concatenate(totals + [jnp.zeros((5, cells), f32)], axis=0)
    site_total = exact(total[:, :inner_lanes], picks, nt)
    lines = jnp.concatenate([-(site_total[0:3] + long_force[0:3]), site_energy], axis=0)
    lines = jnp.concatenate([lines, jnp.zeros((4, slots), f32)], axis=0)
    hot = (iota((slots, slots), 0) == site_of(coords_of(pos_ref))).astype(f32).astype(bf16)
    lines = exact(lines, hot)
    for axis in range(3):
        force_out[0, 0, axis] = lines[axis : axis + 1]
    energy_out[0, 0] = lines[3:4]


def kernel_params():
    return pltpu.CompilerParams(vmem_limit_bytes=56 * 1024 * 1024)


def whole_box(
    species,
    counts,
    positions,
    ghost_rows,
    neighbours,
    kvec,
    embed,
    radial_one,
    radial_two,
    mix_one,
    mix_two,
    lr_filter,
    read_weight,
    read_bias,
    energy_weight,
):
    axes = ("gx", "gy", "gz")
    vmem = pl.BlockSpec(memory_space=pltpu.VMEM)
    smem = pl.BlockSpec(memory_space=pltpu.SMEM)
    placed = pl.pallas_call(
        place_kernel,
        out_shape=jax.ShapeDtypeStruct((domains, 4, slots), f32),
        in_specs=[smem, vmem, vmem],
        out_specs=vmem,
    )(counts, positions.transpose(0, 1, 3, 2, 4), species)
    shared = lax.all_to_all(placed, axes, 0, 0, tiled=True)
    gain = pl.pallas_call(
        gain_kernel,
        out_shape=jax.ShapeDtypeStruct((chan, table), f32),
        in_specs=[vmem] * 2,
        out_specs=vmem,
    )(kvec, lr_filter)
    tables = (
        gain,
        embed,
        radial_one,
        radial_two,
        mix_one,
        mix_two,
        read_weight,
        read_bias.reshape(1, chan),
        energy_weight.reshape(1, chan),
    )
    energies, forces = box_call(shared, positions.transpose(0, 1, 3, 2, 4), tables)
    return (energies, forces.transpose(0, 1, 3, 2, 4))


def box_call(shared, coords, tables):
    vmem = pl.BlockSpec(memory_space=pltpu.VMEM)
    grid_shape = (ext, ext, ext, planes, 128)
    return pl.pallas_call(
        box_kernel,
        out_shape=(
            jax.ShapeDtypeStruct((1, 1, 1, slots), f32),
            jax.ShapeDtypeStruct((1, 1, 3, 1, slots), f32),
        ),
        in_specs=[vmem] * 11,
        out_specs=(vmem, vmem),
        scratch_shapes=[
            pltpu.VMEM((cells // 128, 64 * 16, 128), f32),
            pltpu.VMEM((64, pad), f32),
            pltpu.VMEM((2, rows_all, 128), f32),
            pltpu.VMEM((half, rows_all, pad), bf16),
            pltpu.VMEM((table, 2 * span), bf16),
            pltpu.VMEM((table, cells), bf16),
            pltpu.VMEM(grid_shape, f32),
            pltpu.VMEM(grid_shape, f32),
            pltpu.VMEM(grid_shape, f32),
            pltpu.VMEM((rows_all, 128), f32),
            pltpu.VMEM((2, pad, 128), f32),
            pltpu.VMEM((8, 2 * span), f32),
            pltpu.VMEM((rows_all, pad), bf16),
            pltpu.VMEM((2, cells, chan), f32),
            pltpu.VMEM((pad, pad), f32),
            pltpu.VMEM((3, cells + reach, 256), f32),
        ],
        compiler_params=kernel_params(),
    )(shared, coords, *tables)


def solution(mesh):
    in_specs = (
        P(("group", "gx"), "gy", "gz", None),
        P(("group", "gx"), "gy", "gz"),
        P(("group", "gx"), "gy", "gz", None, None),
        P(("group", "gx"), "gy", "gz", None),
        P(("group", "gx"), "gy", "gz", None, None),
        P(),
        P(),
        P(),
        P(),
        P(),
        P(),
        P(),
        P(),
        P(),
        P(),
    )
    out_specs = (P(("group", "gx"), "gy", "gz", None), P(("group", "gx"), "gy", "gz", None, None))
    sizes = tuple(mesh.shape[axis] for axis in ("gx", "gy", "gz"))
    plan = whole_box if sizes == grid_dims else local
    return jax.shard_map(plan, mesh=mesh, in_specs=in_specs, out_specs=out_specs, check_vma=False)
```

```python
import math

import jax
import jax.numpy as jnp
import numpy as np
from jax import lax
from jax.experimental import pallas as pl
from jax.experimental.pallas import tpu as pltpu
from jax.sharding import PartitionSpec as P

SIDE = 6
KVEC = 4096
NBASIS = 8
NEIGH = 26


spacing = 2.5
cutoff = 5.0
two_pi = 6.283185307179586
highest = lax.Precision.HIGHEST


def passed_along(block, axis, distance):
    devices = range(lax.axis_size(axis))
    route = [((i - distance) % len(devices), i) for i in devices]
    return lax.ppermute(block, axis, route)


def extended(block, sides, width):
    for axis, dim in sides:
        count = lax.axis_size(axis)
        forward = [(i, i + 1) for i in range(count - 1)]
        forward.append((count - 1, 0))
        backward = [(target, source) for source, target in forward]
        low = lax.ppermute(
            lax.slice_in_dim(block, block.shape[dim] - width, None, axis=dim), axis, forward
        )
        high = lax.ppermute(lax.slice_in_dim(block, 0, width, axis=dim), axis, backward)
        block = jnp.concatenate([low, block, high], axis=dim)
    return block


def rows_per_block():
    return SIDE * SIDE


def boundary_list(side):
    site_ids = np.arange(side**3).reshape(side, side, side)
    inner = np.zeros((side, side, side), dtype=bool)
    inner[1 : side - 1, 1 : side - 1, 1 : side - 1] = True
    return site_ids[~inner].astype(np.int32)


def radial_terms(distance):
    centres = cutoff * jnp.arange(NBASIS).astype(jnp.float32) / (NBASIS - 1)
    sharpness = (NBASIS / cutoff) ** 2
    gap_value = distance[None] - centres[:, None, None]
    gaussian = jnp.exp(-sharpness * gap_value * gap_value)
    envelope_base = jnp.maximum(1.0 - distance * distance / (cutoff * cutoff), 0.0)
    envelope = envelope_base * envelope_base
    envelope_slope = -4.0 * distance * envelope_base / (cutoff * cutoff)
    radial_value = gaussian * envelope[None]
    radial_slope = gaussian * (envelope_slope[None] - 2.0 * sharpness * gap_value * envelope[None])
    return (radial_value, radial_slope)


def embed_codes(type_code, embed):
    species_ids = jnp.arange(1, embed.shape[0] + 1, dtype=jnp.int32).astype(type_code.dtype)
    one_hot = (type_code[None, :] == species_ids[:, None]).astype(jnp.float32)
    return jnp.dot(embed.T, one_hot, precision=highest, preferred_element_type=jnp.float32)


def cell_shift():
    ext_side = SIDE + 2
    cells = jnp.arange(ext_side**3, dtype=jnp.int32)
    coords = jnp.stack(
        [cells // (ext_side * ext_side), cells // ext_side % ext_side, cells % ext_side]
    )
    domain_width = SIDE * spacing
    return jnp.where(
        coords == 0, -domain_width, jnp.where(coords == ext_side - 1, domain_width, 0.0)
    ).astype(jnp.float32)


def pair_geometry(coords_own, pool_coords, pair_lists):
    separation = jnp.take(pool_coords, pair_lists, axis=1) - coords_own[:, None, :]
    distance = jnp.sqrt(jnp.sum(separation * separation, axis=0))
    return (separation, distance)


def message_forward(pool_values, pair_lists, radial_value, radial_weight):
    radial_filter = jnp.einsum("bc,bma->cma", radial_weight, radial_value, precision=highest)
    neighbour_value = jnp.take(pool_values, pair_lists, axis=1)
    return jnp.sum(radial_filter * neighbour_value, axis=1)


def message_backward(
    grad_message,
    pool_values,
    pair_lists,
    radial_value,
    radial_slope,
    radial_weight,
    separation,
    distance,
    pool_size,
    with_features,
):
    neighbour_value = jnp.take(pool_values, pair_lists, axis=1)
    contracted = jnp.einsum(
        "bc,cma->bma", radial_weight, grad_message[:, None, :] * neighbour_value, precision=highest
    )
    energy_slope = jnp.sum(radial_slope * contracted, axis=0)
    pair_force = separation * (energy_slope / distance)[None]
    flat_index = pair_lists.reshape(-1)
    grad_pool = (
        jnp.zeros((3, pool_size), jnp.float32).at[:, flat_index].add(pair_force.reshape(3, -1))
    )
    grad_own = -jnp.sum(pair_force, axis=1)
    if with_features:
        radial_filter = jnp.einsum("bc,bma->cma", radial_weight, radial_value, precision=highest)
        spread = (radial_filter * grad_message[:, None, :]).reshape(radial_filter.shape[0], -1)
        feature_pool = (
            jnp.zeros((radial_filter.shape[0], pool_size), jnp.float32)
            .at[:, flat_index]
            .add(spread)
        )
        return (grad_pool, grad_own, feature_pool)
    return (grad_pool, grad_own, grad_pool)


def phase_table(fraction, wave_numbers):
    phase_angle = two_pi * (
        fraction[0][:, None] * wave_numbers[0][None, :]
        + fraction[1][:, None] * wave_numbers[1][None, :]
        + fraction[2][:, None] * wave_numbers[2][None, :]
    )
    return (jnp.cos(phase_angle).astype(jnp.bfloat16), jnp.sin(phase_angle).astype(jnp.bfloat16))


def read_long(cosine_low, sine_low, filtered):
    dims = (((1,), (1,)), ((), ()))
    return lax.dot_general(
        filtered[0], cosine_low, dims, preferred_element_type=jnp.float32
    ) + lax.dot_general(filtered[1], sine_low, dims, preferred_element_type=jnp.float32)


def block_live(step_index, live_count):
    block_rows = rows_per_block()
    per_member = SIDE**3 // block_rows
    first_row = (step_index % per_member * block_rows).astype(jnp.float32)
    return first_row < live_count[step_index // per_member]


def lr_struct(fraction, row_values, live_count, wave_numbers):
    block_rows = rows_per_block()
    blocks = fraction.shape[1] // block_rows

    def step(step_index, running):

        def work(running):
            offset = step_index * block_rows
            frac_block = lax.dynamic_slice_in_dim(fraction, offset, block_rows, 1)
            feature_block = lax.dynamic_slice_in_dim(row_values, offset, block_rows, 1)
            cosine_low, sine_low = phase_table(frac_block, wave_numbers)
            term = jnp.stack(
                [
                    jnp.dot(feature_block, cosine_low, preferred_element_type=jnp.float32),
                    jnp.dot(feature_block, sine_low, preferred_element_type=jnp.float32),
                ]
            )
            return running + term

        return lax.cond(
            block_live(step_index, live_count), work, lambda unchanged: unchanged, running
        )

    initial = jnp.zeros((2, row_values.shape[0], wave_numbers.shape[1]), jnp.float32)
    return lax.fori_loop(0, blocks, step, initial)


def lr_read(fraction, live_count, wave_numbers, filtered):
    block_rows = rows_per_block()
    blocks = fraction.shape[1] // block_rows

    def step(step_index, result):

        def work(result):
            offset = step_index * block_rows
            cosine_low, sine_low = phase_table(
                lax.dynamic_slice_in_dim(fraction, offset, block_rows, 1), wave_numbers
            )
            return lax.dynamic_update_slice_in_dim(
                result, read_long(cosine_low, sine_low, filtered), offset, 1
            )

        return lax.cond(
            block_live(step_index, live_count), work, lambda unchanged: unchanged, result
        )

    initial = jnp.zeros((filtered.shape[1], fraction.shape[1]), jnp.float32)
    return lax.fori_loop(0, blocks, step, initial)


def lr_back(
    fraction,
    rounded_rows,
    grad_rows,
    occupied_rows,
    live_count,
    wave_numbers,
    wave_factors,
    filtered,
    back_filtered,
):
    block_rows = rows_per_block()
    blocks = fraction.shape[1] // block_rows
    dims = (((0,), (0,)), ((), ()))
    right_real = jnp.concatenate([filtered[0], back_filtered[0]], axis=0)
    right_imag = jnp.concatenate([filtered[1], back_filtered[1]], axis=0)

    def step(step_index, carried):

        def work(carried):
            grad_long, force_long = carried
            offset = step_index * block_rows
            cosine_low, sine_low = phase_table(
                lax.dynamic_slice_in_dim(fraction, offset, block_rows, 1), wave_numbers
            )
            mask_block = lax.dynamic_slice_in_dim(occupied_rows, offset, block_rows, 0)
            grad_block = mask_block[None] * read_long(cosine_low, sine_low, back_filtered)
            stacked_left = jnp.concatenate(
                [
                    lax.dynamic_slice_in_dim(grad_rows, offset, block_rows, 1),
                    lax.dynamic_slice_in_dim(rounded_rows, offset, block_rows, 1),
                ],
                axis=0,
            )
            real_part = lax.dot_general(
                stacked_left, right_real, dims, preferred_element_type=jnp.float32
            )
            imag_part = lax.dot_general(
                stacked_left, right_imag, dims, preferred_element_type=jnp.float32
            )
            turning = (
                cosine_low.astype(jnp.float32) * imag_part
                - sine_low.astype(jnp.float32) * real_part
            )
            force_block = lax.dot_general(
                wave_factors,
                turning,
                (((1,), (1,)), ((), ())),
                precision=highest,
                preferred_element_type=jnp.float32,
            )
            return (
                lax.dynamic_update_slice_in_dim(grad_long, grad_block, offset, 1),
                lax.dynamic_update_slice_in_dim(force_long, force_block, offset, 1),
            )

        return lax.cond(
            block_live(step_index, live_count), work, lambda unchanged: unchanged, carried
        )

    initial = (
        jnp.zeros((rounded_rows.shape[0], fraction.shape[1]), jnp.float32),
        jnp.zeros((3, fraction.shape[1]), jnp.float32),
    )
    return lax.fori_loop(0, blocks, step, initial)


def boundary_grid(values, ghost_slots, boundary):
    picked = jnp.take(values, ghost_slots, axis=1)
    site_grid = jnp.zeros((values.shape[0], SIDE**3), values.dtype).at[:, boundary].set(picked)
    return site_grid.reshape(values.shape[0], SIDE, SIDE, SIDE)


def fold_slab(site_grid, axis_number, from_left, from_right):
    inner_size = site_grid.shape[axis_number] - 2
    inner = lax.slice_in_dim(site_grid, 1, inner_size + 1, axis=axis_number)
    first_layer = lax.slice_in_dim(inner, 0, 1, axis=axis_number) + from_left
    last_layer = lax.slice_in_dim(inner, inner_size - 1, inner_size, axis=axis_number) + from_right
    middle = lax.slice_in_dim(inner, 1, inner_size - 1, axis=axis_number)
    return jnp.concatenate([first_layer, middle, last_layer], axis=axis_number)


def return_halo(site_grid):
    edge = site_grid.shape[3] - 1
    received = [
        passed_along(
            lax.slice_in_dim(site_grid, slab_start, slab_start + 1, axis=3), "gz", direction
        )
        for direction, slab_start in ((1, edge), (-1, 0))
    ]
    site_grid = fold_slab(site_grid, 3, received[0], received[1])
    edge = site_grid.shape[2] - 1
    received = [
        passed_along(
            lax.slice_in_dim(site_grid, slab_start, slab_start + 1, axis=2), "gy", direction
        )
        for direction, slab_start in ((1, edge), (-1, 0))
    ]
    site_grid = fold_slab(site_grid, 2, received[0], received[1])
    edge = site_grid.shape[1] - 1
    received = [
        passed_along(
            lax.slice_in_dim(site_grid, slab_start, slab_start + 1, axis=1), "gx", direction
        )
        for direction, slab_start in ((1, edge), (-1, 0))
    ]
    return fold_slab(site_grid, 1, received[0], received[1])


def ghost_to_rows(site_grid, ghost_slots, boundary):
    features = site_grid.shape[0]
    picked = site_grid.reshape(features, -1)[:, boundary]
    return jnp.zeros((features, SIDE**3), site_grid.dtype).at[:, ghost_slots].add(picked)


def local(
    species,
    counts,
    positions,
    ghost_rows,
    neighbours,
    kvec,
    embed,
    radial_one,
    radial_two,
    mix_one,
    mix_two,
    lr_filter,
    read_weight,
    read_bias,
    energy_weight,
):
    slot_count = SIDE**3
    ext_side = SIDE + 2
    pool_size = slot_count + ext_side**3
    pair_scale = 1.0 / math.sqrt(NEIGH)
    domain_width = SIDE * spacing
    mesh_sizes = (lax.axis_size("gx"), lax.axis_size("gy"), lax.axis_size("gz"))
    box_length = tuple((count_along * domain_width for count_along in mesh_sizes))
    wave_scale = 1.0 / math.sqrt(
        KVEC * (slot_count * mesh_sizes[0] * mesh_sizes[1] * mesh_sizes[2])
    )
    species_flat = species.reshape(slot_count)
    live_total = counts.reshape(())
    coords_own = positions.reshape(3, slot_count)
    ghost_slots = ghost_rows.reshape(-1)
    pair_lists = neighbours.reshape(NEIGH, slot_count)
    boundary = jnp.asarray(boundary_list(SIDE))
    cell_offset = cell_shift()
    occupied = (jnp.arange(slot_count, dtype=jnp.int32) < live_total).astype(jnp.float32)
    type_code = jnp.where(occupied > 0, species_flat + 1, 0).astype(jnp.float32)
    hidden_zero = embed_codes(species_flat + 1, embed)
    masked_zero = hidden_zero * occupied[None]
    packet = boundary_grid(
        jnp.concatenate([coords_own, type_code[None]], axis=0), ghost_slots, boundary
    )
    ext_atoms = extended(packet, (("gx", 1), ("gy", 2), ("gz", 3)), 1).reshape(4, -1)
    pool_coords = jnp.concatenate([coords_own, ext_atoms[:3] + cell_offset], axis=1)
    pool_zero = jnp.concatenate([masked_zero, embed_codes(ext_atoms[3], embed)], axis=1)
    separation, distance = pair_geometry(coords_own, pool_coords, pair_lists)
    radial_value, radial_slope = radial_terms(distance)
    message = message_forward(pool_zero, pair_lists, radial_value, radial_one)
    hidden_one = hidden_zero + pair_scale * jnp.dot(
        mix_one.T, message, precision=highest, preferred_element_type=jnp.float32
    )
    masked_one = hidden_one * occupied[None]
    rounded_one = masked_one.astype(jnp.bfloat16)
    domain_pos = (lax.axis_index("gx"), lax.axis_index("gy"), lax.axis_index("gz"))
    fraction = jnp.stack(
        [
            (domain_pos[axis_id].astype(jnp.float32) * domain_width + coords_own[axis_id])
            / box_length[axis_id]
            for axis_id in range(3)
        ]
    )
    wave_numbers = kvec.astype(jnp.float32)
    wave_factors = jnp.stack(
        [two_pi * wave_numbers[axis_id] / box_length[axis_id] for axis_id in range(3)]
    )
    own_count = jnp.sum(occupied)[None]
    share_size = KVEC // (mesh_sizes[0] * mesh_sizes[1] * mesh_sizes[2])
    share_start = lax.axis_index(("gx", "gy", "gz")) * share_size
    filter_share = lax.dynamic_slice_in_dim(lr_filter, share_start, share_size, 1)
    struct_part = lax.psum_scatter(
        lr_struct(fraction, rounded_one, own_count, wave_numbers),
        ("gx", "gy", "gz"),
        scatter_dimension=2,
        tiled=True,
    )
    filtered = lax.all_gather(
        (struct_part * filter_share[None] * wave_scale).astype(jnp.bfloat16),
        ("gx", "gy", "gz"),
        axis=2,
        tiled=True,
    )
    long_part = lr_read(fraction, own_count, wave_numbers, filtered)
    masked_ext = extended(
        boundary_grid(masked_one, ghost_slots, boundary).astype(jnp.bfloat16),
        (("gx", 1), ("gy", 2), ("gz", 3)),
        1,
    ).astype(jnp.float32)
    pool_one = jnp.concatenate([masked_one, masked_ext.reshape(masked_one.shape[0], -1)], axis=1)
    message_two = message_forward(pool_one, pair_lists, radial_value, radial_two)
    hidden_two = (
        hidden_one
        + pair_scale
        * jnp.dot(mix_two.T, message_two, precision=highest, preferred_element_type=jnp.float32)
        + long_part
    )
    activation = (
        jnp.dot(read_weight.T, hidden_two, precision=highest, preferred_element_type=jnp.float32)
        + read_bias[:, None]
    )
    gating = jax.nn.sigmoid(activation)
    energies = occupied * jnp.sum(activation * gating * energy_weight[:, None], axis=0)
    grad_act = (
        occupied[None] * energy_weight[:, None] * gating * (1.0 + activation * (1.0 - gating))
    )
    grad_two = jnp.dot(read_weight, grad_act, precision=highest, preferred_element_type=jnp.float32)
    grad_low = grad_two.astype(jnp.bfloat16)
    grad_part = lax.psum_scatter(
        lr_struct(fraction, grad_low, own_count, wave_numbers),
        ("gx", "gy", "gz"),
        scatter_dimension=2,
        tiled=True,
    )
    back_filtered = lax.all_gather(
        (grad_part * filter_share[None] * wave_scale).astype(jnp.bfloat16),
        ("gx", "gy", "gz"),
        axis=2,
        tiled=True,
    )
    grad_long, force_long = lr_back(
        fraction,
        rounded_one,
        grad_low,
        occupied,
        own_count,
        wave_numbers,
        wave_factors,
        filtered,
        back_filtered,
    )
    grad_message = pair_scale * jnp.dot(
        mix_two, grad_two, precision=highest, preferred_element_type=jnp.float32
    )
    grad_pool, grad_own_two, feature_pool = message_backward(
        grad_message,
        pool_one,
        pair_lists,
        radial_value,
        radial_slope,
        radial_two,
        separation,
        distance,
        pool_size,
        True,
    )
    combined = jnp.concatenate([feature_pool, grad_pool], axis=0)
    features = combined.shape[0]
    returned_two = ghost_to_rows(
        return_halo(combined[:, slot_count:].reshape(features, ext_side, ext_side, ext_side)),
        ghost_slots,
        boundary,
    )
    own_two = combined[:, :slot_count]
    channels = masked_one.shape[0]
    grad_one = (
        grad_two + grad_long + occupied[None] * (own_two[:channels] + returned_two[:channels])
    )
    grad_message_one = pair_scale * jnp.dot(
        mix_one, grad_one, precision=highest, preferred_element_type=jnp.float32
    )
    grad_pool_one, grad_own_one, unused = message_backward(
        grad_message_one,
        pool_zero,
        pair_lists,
        radial_value,
        radial_slope,
        radial_one,
        separation,
        distance,
        pool_size,
        False,
    )
    layer_one_grad = grad_own_one + grad_pool_one[:, :slot_count]
    returned_one = ghost_to_rows(
        return_halo(grad_pool_one[:, slot_count:].reshape(3, ext_side, ext_side, ext_side)),
        ghost_slots,
        boundary,
    )
    total_grad = (
        layer_one_grad
        + returned_one
        + force_long
        + grad_own_two
        + own_two[channels:]
        + returned_two[channels:]
    )
    forces = -total_grad
    return (energies.reshape(1, 1, 1, slot_count), forces.reshape(1, 1, 1, 3, slot_count))


offsets = tuple(
    (ox, oy, oz)
    for ox in (0, 1)
    for oy in (-1, 0, 1)
    for oz in (-1, 0, 1)
    if (ox, oy, oz) > (0, 0, 0)
)
half = len(offsets)
slots = SIDE**3
ext = SIDE + 2
cells = ext**3
inner_lanes = SIDE * ext * ext
reach = ext * ext + 2 * ext
chan = 64
grid_dims = (4, 2, 2)
domains = 16
planes = 8
rows_all = slots * planes
waves = 648
table = 2 * waves
pad = 256
span = -(-rows_all // 128) * 128
gamma = (NBASIS / cutoff) ** 2
step = cutoff / (NBASIS - 1)
nt = (((1,), (1,)), ((), ()))
nn = (((1,), (0,)), ((), ()))
f32 = jnp.float32
bf16 = jnp.bfloat16


def dot(left, right, dims=nn, precision=None):
    return lax.dot_general(left, right, dims, precision=precision, preferred_element_type=f32)


def split(value):
    high = value.astype(bf16)
    return high, (value - high.astype(f32)).astype(bf16)


def dot_split(left, high, low):
    left_high, left_low = split(left)
    return dot(left_high, high) + dot(left_low, high) + dot(left_high, low)


def exact(left, hot, dims=nn):
    high = left.astype(bf16).astype(f32)
    rest = left - high
    middle = rest.astype(bf16).astype(f32)
    count = left.shape[0]
    stacked = jnp.concatenate([high, middle, rest - middle], axis=0).astype(bf16)
    parts = dot(stacked, hot, dims)
    return parts[:count] + parts[count : 2 * count] + parts[2 * count :]


def coords_of(ref):
    return jnp.concatenate([ref[0, 0, axis] for axis in range(3)], axis=0)


def site_of(coords):
    where = (coords * (1.0 / spacing)).astype(jnp.int32)
    return (where[0:1] * SIDE + where[1:2]) * SIDE + where[2:3]


def iota(shape, dim):
    return lax.broadcasted_iota(jnp.int32, shape, dim)


def place_kernel(count_ref, pos_ref, species_ref, out_ref):
    coords = coords_of(pos_ref)
    live = iota((1, slots), 1) < count_ref[0, 0, 0]
    code = jnp.where(live, species_ref[0, 0] + 1, 0).astype(f32)
    data = jnp.concatenate([coords, code, jnp.zeros((4, slots), f32)], axis=0)
    hot = (iota((slots, slots), 0) == site_of(coords)).astype(f32).astype(bf16)
    placed = exact(data, hot, nt)[0:4]
    for number in range(domains):
        out_ref[number] = placed


def twice(block):
    zero = jnp.zeros_like(block)
    return jnp.concatenate(
        [jnp.concatenate([block, zero], axis=1), jnp.concatenate([zero, block], axis=1)], axis=0
    )


def gain_kernel(kvec_ref, filter_ref, gain_ref):
    wave_scale = 1.0 / math.sqrt(KVEC * slots * domains)
    waves_in = kvec_ref[...]

    def folded(row):
        return jnp.where(row > 0, 2 * row - 1, -2 * row)

    index = (folded(waves_in[1:2]) * 9 + folded(waves_in[2:3])) * 8 + waves_in[0:1] - 1
    filter_high, filter_low = split(filter_ref[...] * wave_scale)
    parts = jnp.concatenate([filter_high, filter_low], axis=0)
    gain = jnp.zeros((waves, 2 * chan), f32)
    width = 1024
    for start in range(0, KVEC, width):
        hot = (iota((waves, width), 0) == index[:, start : start + width]).astype(f32).astype(bf16)
        gain = gain + dot(hot, parts[:, start : start + width], nt)
    gain = (gain[:, :chan] + gain[:, chan:]).reshape(waves // 8, 8, chan)
    gain_ref[...] = jnp.concatenate([gain, gain], axis=1).reshape(table, chan).T


def turn(fraction):
    rest = fraction - jnp.floor(fraction + 0.5)
    angle = rest * (0.5 * two_pi)
    square = angle * angle
    sine = angle * (
        1.0
        + square
        * (
            -1.0 / 6
            + square
            * (
                1.0 / 120
                + square * (-1.0 / 5040 + square * (1.0 / 362880 - square * (1.0 / 39916800)))
            )
        )
    )
    cosine = 1.0 + square * (
        -0.5
        + square
        * (
            1.0 / 24
            + square
            * (
                -1.0 / 720
                + square
                * (1.0 / 40320 + square * (-1.0 / 3628800 + square * (1.0 / 479001600)))
            )
        )
    )
    return 1.0 - 2.0 * sine * sine, 2.0 * sine * cosine


def fan(base, step_pairs):
    real, imag = base
    out = [(real, imag)]
    for cosine, sine in step_pairs:
        a, b, c, d = real * cosine, imag * sine, real * sine, imag * cosine
        out.append((a - b, c + d))
        out.append((a + b, d - c))
    return out


def wave_tile(coords, store):
    frac = [coords[axis] / (grid_dims[axis] * SIDE * spacing) for axis in range(3)]
    row = iota((8, 128), 0)
    base = turn(frac[0] * (row + 1).astype(f32))
    rest = turn(jnp.where(row < 4, frac[1], frac[2]) * (row % 4 + 1).astype(f32))

    def line(index):
        return tuple(jnp.broadcast_to(part[index : index + 1], (8, 128)) for part in rest)

    y_lines = [line(index) for index in range(4)]
    z_lines = [line(index + 4) for index in range(4)]
    index = 0
    for level in fan(base, y_lines):
        for real, imag in fan(level, z_lines):
            store(index, jnp.concatenate([real, imag], axis=0).astype(bf16))
            index += 1
        yield index


def swap_lanes(value):
    return pltpu.roll(value, chan, value.ndim - 1)


def swap_planes(value):
    up = pltpu.roll(value, 1, 1)
    down = pltpu.roll(value, planes - 1, 1)
    return jnp.where(iota(value.shape, 1) % 2 == 0, down, up)


def as_three(value):
    return value.reshape((-1,) + value.shape[-2:])


def fill_ghosts(ref):
    inner = slice(1, SIDE + 1)
    for ghost, source, shift in ((0, SIDE, 2), (SIDE + 1, 1, planes - 2)):
        value = ref[source, inner, inner]
        ref[ghost, inner, inner] = pltpu.roll(as_three(value), shift, 1).reshape(value.shape)
    for ghost, source in ((0, SIDE), (SIDE + 1, 1)):
        value = ref[:, source, inner]
        ref[:, ghost, inner] = swap_planes(as_three(value)).reshape(value.shape)
    for ghost, source in ((0, SIDE), (SIDE + 1, 1)):
        value = ref[:, :, source]
        ref[:, :, ghost] = swap_lanes(as_three(value)).reshape(value.shape)


def fold_ghosts(ref):
    inner = slice(1, SIDE + 1)
    for ghost, target in ((SIDE + 1, 1), (0, SIDE)):
        value = ref[:, :, ghost]
        ref[:, :, target] = ref[:, :, target] + swap_lanes(as_three(value)).reshape(value.shape)
    for ghost, target in ((SIDE + 1, 1), (0, SIDE)):
        value = ref[:, ghost, inner]
        ref[:, target, inner] = ref[:, target, inner] + swap_planes(as_three(value)).reshape(
            value.shape
        )
    for ghost, target, shift in ((SIDE + 1, 1, 2), (0, SIDE, planes - 2)):
        value = ref[ghost, inner, inner]
        ref[target, inner, inner] = ref[target, inner, inner] + pltpu.roll(
            as_three(value), shift, 1
        ).reshape(value.shape)


def inner_rows(ref, level):
    inner = slice(1, SIDE + 1)
    return ref[level + 1, inner, inner].reshape(rows_all // SIDE, 128)


def set_level(ref, level, value):
    inner = slice(1, SIDE + 1)
    ref[level + 1, inner, inner] = value.reshape(SIDE, SIDE, planes, 128)


def level_rows(level):
    return slice(level * (rows_all // SIDE), (level + 1) * (rows_all // SIDE))


def set_inner(ref, value):
    inner = slice(1, SIDE + 1)
    ref[inner, inner, inner] = value.reshape(SIDE, SIDE, SIDE, planes, 128)


def convolve(filters, layer, source, target, beside=None):
    target[...] = jnp.zeros(target.shape, f32)
    lanes = slice(layer * 128, layer * 128 + 128)
    groups = {}
    for number, (ox, oy, oz) in enumerate(offsets):
        groups.setdefault((ox, oy), []).append((number, oz))

    def one_line(line):
        x = line // SIDE
        y = line % SIDE
        own = [source[x + 1, y + 1, z + 1] for z in range(SIDE)]
        own_sum = [jnp.zeros((planes, 128), f32)] * SIDE
        for (ox, oy), members in groups.items():
            there = [source[x + 1 + ox, y + 1 + oy, z] for z in range(ext)]
            sums = [None] * ext
            first = pl.multiple_of(line * (SIDE * planes), SIDE * planes)
            weights = [
                filters[number, pl.ds(first, SIDE * planes), lanes].astype(f32)
                for number, _ in members
            ]
            for z in range(SIDE):
                for block, (_, oz) in zip(weights, members):
                    weight = block[z * planes : z * planes + planes]
                    own_sum[z] = own_sum[z] + weight * there[z + 1 + oz]
                    term = weight * own[z]
                    spot = z + 1 + oz
                    sums[spot] = term if sums[spot] is None else sums[spot] + term
            for z in range(ext):
                if sums[z] is not None:
                    target[x + 1 + ox, y + 1 + oy, z] = target[x + 1 + ox, y + 1 + oy, z] + sums[z]
        for z in range(SIDE):
            target[x + 1, y + 1, z + 1] = target[x + 1, y + 1, z + 1] + own_sum[z]

    def body(number, carry):
        one_line(number * 3)
        if beside is not None:
            beside(number)
        one_line(number * 3 + 1)
        one_line(number * 3 + 2)
        return carry

    lax.fori_loop(0, SIDE * SIDE // 3, body, 0)
    fold_ghosts(target)


def spread(block):
    return jnp.broadcast_to(block[:, None, :], (NBASIS, 16, chan)).reshape(128, chan)


def wide(left, right):
    left, right = spread(left), spread(right)
    line = jnp.concatenate([left, left, right, right], axis=1)
    return jnp.concatenate([line, line], axis=0)


def doubled(ref):
    return jnp.concatenate([ref[...], ref[...]], axis=1)


def box_kernel(
    all_ref,
    pos_ref,
    gain_ref,
    embed_ref,
    radial_one_ref,
    radial_two_ref,
    mix_one_ref,
    mix_two_ref,
    read_ref,
    bias_ref,
    energy_ref,
    energy_out,
    force_out,
    sep_ref,
    sites_ref,
    basis_ref,
    filters_ref,
    waves_ref,
    ring_ref,
    zero_ref,
    one_ref,
    sum_ref,
    packed_ref,
    own_ref,
    flat_ref,
    low_ref,
    saved_ref,
    radial_ref,
    shift_ref,
    turned_ref,
    parts_ref,
):
    home = [lax.axis_index(axis) for axis in ("gx", "gy", "gz")]
    pair_scale = 1.0 / math.sqrt(NEIGH)
    fall = jnp.exp(-gamma * jnp.square(step * iota((NBASIS, 1), 0).astype(f32)))
    rows = iota((pad, pad), 0)
    columns = iota((pad, pad), 1)
    kept = (rows // 128) == (columns % 128 // chan)
    radial_ref[...] = jnp.where(
        kept, wide(radial_one_ref[...] * fall, radial_two_ref[...] * fall), 0.0
    )
    table_rows = jnp.concatenate([embed_ref[...], jnp.zeros((2, chan), f32)], axis=0)
    table_high = table_rows.astype(bf16).astype(f32)
    species_rows = kept & (rows % 16 == half)
    embeds = jnp.where(species_rows, wide(table_high, table_rows - table_high), 0.0).astype(bf16)
    lives = jnp.where(species_rows[:, :128], 1.0, 0.0).astype(bf16)
    sites_ref[...] = jnp.zeros((4 * domains, pad), f32)
    flat_ref[...] = jnp.zeros(flat_ref.shape, f32)
    domain_width = SIDE * spacing
    offset_row = iota((4, slots), 0)
    for number in range(domains):
        spot = [
            lax.rem(home[axis] + part, grid_dims[axis])
            for axis, part in enumerate((number // 4, number // 2 % 2, number % 2))
        ]
        block = all_ref[(spot[0] * 2 + spot[1]) * 2 + spot[2]]
        sites_ref[number * 4 : number * 4 + 4, 0:slots] = block
        shifts = [part * domain_width for part in (number // 4, number // 2 % 2, number % 2)]
        moved = jnp.where(
            offset_row == 0, shifts[0], jnp.where(offset_row == 1, shifts[1], shifts[2])
        )
        start = number % 2 * span + number // 2 * slots
        flat_ref[0:4, start : start + slots] = block + moved
    sites = sites_ref[:, 0:slots]

    lane = iota((1, cells), 1)
    coords = [(lane // (ext * ext) + 1) % ext, lane // ext % ext, lane % ext]
    wrapped = [(value + SIDE - 1) % SIDE for value in coords]
    wrapped_site = (wrapped[0] * SIDE + wrapped[1]) * SIDE + wrapped[2]
    inside = coords[0] >= 0
    for value in coords:
        inside = inside & (value > 0) & (value < ext - 1)
    hot_all = iota((slots, cells), 0) == wrapped_site
    grown = exact(sites, hot_all.astype(f32).astype(bf16))
    picks = (hot_all & inside)[:, :inner_lanes].astype(f32).astype(bf16)

    back16 = jnp.concatenate([grown[48:], grown[:48]], axis=0)
    ahead16 = jnp.concatenate([grown[16:], grown[:16]], axis=0)
    grown = jnp.where(coords[0] == 0, back16, jnp.where(coords[0] == ext - 1, ahead16, grown))
    swapped = jnp.concatenate(
        [grown[8 * (part ^ 1) : 8 * (part ^ 1) + 8] for part in range(8)], axis=0
    )
    grown = jnp.where((coords[1] == 0) | (coords[1] == ext - 1), swapped, grown)
    swapped = pltpu.roll(grown.reshape(8, 8, cells), 4, 1).reshape(64, cells)
    grown = jnp.where((coords[2] == 0) | (coords[2] == ext - 1), swapped, grown)
    component = iota((64, cells), 0) % 4
    for axis in range(3):
        moved = jnp.where(
            coords[axis] == 0,
            -domain_width,
            jnp.where(coords[axis] == ext - 1, domain_width, 0.0),
        )
        grown = grown + jnp.where(component == axis, moved, 0.0)
    own_ext = grown[0:4]
    tiles = cells // 128

    def put_sep(number, value):
        for tile in range(tiles):
            sep_ref[tile, pl.ds(number, 64, stride=16), :] = value[:, tile * 128 : tile * 128 + 128]

    def get_sep(window, count=tiles):
        return jnp.concatenate([sep_ref[tile, window, :] for tile in range(count)], axis=1)

    for number, (ox, oy, oz) in enumerate(offsets):
        distance = (ox * ext + oy) * ext + oz
        put_sep(number, pltpu.roll(grown, cells - distance, 1) - grown)
    for number in range(half, 16):
        put_sep(number, grown)

    basis_unroll = 8
    row16 = iota((16, inner_lanes), 0)

    def basis_of(domain):
        first = pl.multiple_of(domain * 64, 64)
        sx, sy, sz, codes = [get_sep(pl.ds(first + 16 * part, 16), inner_lanes // 128) for part in range(4)]
        square = sx * sx + sy * sy + sz * sz
        near = jnp.minimum(jnp.sqrt(square), cutoff)
        base = jnp.maximum(1.0 - square * (1.0 / (cutoff * cutoff)), 0.0)
        value = jnp.exp(-gamma * jnp.minimum(square, cutoff * cutoff)) * base * base
        ratio = jnp.exp((2.0 * gamma * step) * near)
        out = []
        for number in range(NBASIS):
            hit = jnp.where(codes == number + 1.0, 1.0, 0.0)
            out.append(jnp.where(row16 == half, hit, value))
            value = value * ratio
        return jnp.concatenate(out, axis=0).astype(bf16)

    def basis_step(plane, carry):
        both = jnp.concatenate([basis_of(2 * plane), basis_of(2 * plane + 1)], axis=0)
        picked = dot(picks, both, nt)
        for tile in range(2):
            basis_ref[tile, pl.ds(plane, slots, stride=planes), :] = picked[
                :, tile * 128 : tile * 128 + 128
            ]
        return carry

    def basis_group(number, carry):
        for part in range(basis_unroll):
            basis_step(number * basis_unroll + part, carry)
        return carry

    lax.fori_loop(0, planes // basis_unroll, basis_group, 0)

    basis_low = jnp.concatenate([basis_ref[0], basis_ref[1]], axis=1).astype(bf16)
    low_ref[...] = basis_low

    def flat_tile(start):
        block = flat_ref[:, pl.ds(start, 128)]

        def store(index, value):
            waves_ref[index * 16 : index * 16 + 16, pl.ds(start, 128)] = value

        return wave_tile([block[axis : axis + 1] for axis in range(3)], store)

    def wave_step(number, carry):
        chosen = jnp.where(iota((pad, pad), 0) % 16 == number, radial_ref[...], 0.0)
        chosen = chosen.astype(bf16)
        levels = []
        for part in range(2):
            levels.append(flat_tile(pl.multiple_of(number * 256 + part * 128, 128)))
        rows_each = rows_all // 6
        for part in range(6):
            window = slice(part * rows_each, part * rows_each + rows_each)
            filters_ref[number, window] = dot(low_ref[window], chosen).astype(bf16)
            for _ in range(3):
                next(levels[part // 3])
        return carry

    lax.fori_loop(0, half, wave_step, 0)
    for tile in range(2 * half, 2 * span // 128):
        list(flat_tile(tile * 128))
    for tile in range(cells // 128):
        lanes = slice(tile * 128, tile * 128 + 128)

        def store(index, value):
            ring_ref[index * 16 : index * 16 + 16, lanes] = value

        list(wave_tile([own_ext[axis : axis + 1, lanes] for axis in range(3)], store))

    start_values = dot(low_ref[...], jnp.concatenate([embeds, lives], axis=1))
    rows_ref = basis_ref.at[0]
    live_ref = basis_ref.at[1]
    live_ref[...] = start_values[:, 256:384]
    set_inner(zero_ref, start_values[:, :128] + start_values[:, 128:256])
    fill_ghosts(zero_ref)
    convolve(filters_ref, 0, zero_ref, sum_ref)
    flat = (cells * planes, 128)
    own_cells = pl.ds(0, cells, stride=planes)

    def cells_of(ref):
        value = ref.reshape(flat)[own_cells, :]
        return jnp.concatenate([value[ext * ext :], value[: ext * ext]], axis=0)[:, :chan]

    saved_ref[0] = cells_of(zero_ref)
    mix_high, mix_low = split(twice(mix_one_ref[...] * pair_scale))
    for level in range(SIDE):
        window = level_rows(level)
        first_rows = inner_rows(zero_ref, level) + live_ref[window] * dot_split(
            inner_rows(sum_ref, level), mix_high, mix_low
        )
        set_level(one_ref, level, first_rows)
        rows_ref[window] = first_rows
    fill_ghosts(one_ref)
    saved_ref[1] = cells_of(one_ref)
    two_ref = zero_ref

    def start_structure():
        for plane in range(planes):
            packed_ref[plane * slots : plane * slots + slots] = rows_ref[
                pl.ds(plane, slots, stride=planes), :
            ]
        turned = packed_ref[...].T
        zeros = jnp.zeros((chan, span - rows_all), f32)
        turned = jnp.concatenate([turned[:chan], zeros, turned[chan:], zeros], axis=1)
        turned_ref[...] = turned.astype(bf16)
        tail = 12 * pad
        parts_ref[...] = dot(turned_ref[:, tail:], waves_ref[:, tail:], nt)

    def step_structure(number):
        start = pl.multiple_of(number * pad, pad)
        parts_ref[...] = parts_ref[...] + dot(
            turned_ref[:, pl.ds(start, pad)], waves_ref[:, pl.ds(start, pad)], nt
        )

    start_structure()
    own_ref[...] = jnp.zeros(own_ref.shape, f32)
    own_ref[0, 0:slots] = rows_ref[pl.ds(0, slots, stride=planes), :]
    convolve(filters_ref, 1, one_ref, sum_ref, step_structure)
    filtered = parts_ref[...] * gain_ref[...]
    long_rows = dot(filtered.astype(bf16), waves_ref[...]).T
    for plane in range(planes):
        first = long_rows[plane * slots : plane * slots + slots]
        second = long_rows[span + plane * slots : span + plane * slots + slots]
        rows_ref[pl.ds(plane, slots, stride=planes), :] = jnp.concatenate([first, second], axis=1)
    read = read_ref[...]
    both = dot_split(mix_two_ref[...] * pair_scale, *split(read))
    act_high, act_low = split(jnp.concatenate([twice(read), twice(both)], axis=0))
    grad_high, grad_low = split(jnp.concatenate([twice(read.T), twice(both.T)], axis=1))
    bias = doubled(bias_ref)
    energy = doubled(energy_ref)
    for level in range(SIDE):
        window = level_rows(level)
        joined = jnp.concatenate(
            [inner_rows(one_ref, level) + rows_ref[window], inner_rows(sum_ref, level)], axis=1
        )
        act = dot_split(joined, act_high, act_low) + bias
        sig = 1.0 / (1.0 + jnp.exp(-act))
        weighted = live_ref[window] * energy * sig
        packed_ref[window] = weighted * act
        grads = dot_split(weighted * (1.0 + act * (1.0 - sig)), grad_high, grad_low)
        rows_ref[window] = grads[:, :128]
        set_level(two_ref, level, grads[:, 128:])
    own_energy = packed_ref[pl.ds(0, slots, stride=planes), :]
    first_half = jnp.where(iota((8, 128), 1) < chan, 1.0, 0.0)
    energy_high, energy_low = split(own_energy)
    first_half = first_half.astype(bf16)
    site_energy = (dot(first_half, energy_high, nt) + dot(first_half, energy_low, nt))[0:1]
    fill_ghosts(two_ref)
    start_structure()
    own_ref[1, 0:slots] = rows_ref[pl.ds(0, slots, stride=planes), :]
    two_cells = cells_of(two_ref)
    convolve(filters_ref, 1, two_ref, sum_ref, step_structure)
    back = parts_ref[...] * gain_ref[...]
    back_rows = back.astype(bf16)
    for level in range(SIDE):
        window = level_rows(level)
        set_level(
            sum_ref, level, rows_ref[window] + live_ref[window] * inner_rows(sum_ref, level)
        )
    fill_ghosts(sum_ref)
    sum_cells = cells_of(sum_ref)
    live_cells = jnp.where(own_ext[3:4] > 0, 1.0, 0.0)
    ring_long = (dot(back_rows, ring_ref[...]) * live_cells).T
    grad_cells = dot_split(sum_cells + ring_long, *split(mix_one_ref[...].T * pair_scale))

    def crossed(value):
        value = value.T.reshape(waves // 8, 2, 8, chan)
        value = jnp.concatenate([value[:, 1:2], -value[:, 0:1]], axis=1).reshape(table, chan)
        return jnp.concatenate([value, jnp.zeros((table, chan), f32)], axis=1).astype(bf16)

    response = dot(crossed(filtered), own_ref[1].astype(bf16), nt) + dot(
        crossed(back), own_ref[0].astype(bf16), nt
    )
    turning_high, turning_low = split(waves_ref[:, 0:pad].astype(f32) * response)
    spot = iota((8, table), 1)
    wave = spot // 16 * 8 + spot % 8

    def signed(index):
        return jnp.where(index % 2 == 1, (index + 1) // 2, -(index // 2))

    row = iota((8, table), 0)
    number = jnp.where(
        row == 0,
        wave % 8 + 1,
        jnp.where(row == 1, signed(wave // 72), jnp.where(row == 2, signed(wave // 8 % 9), 0)),
    )
    number = number.astype(f32).astype(bf16)
    scale_row = iota((8, 1), 0)
    scales = jnp.where(
        scale_row == 0,
        two_pi / (grid_dims[0] * domain_width),
        two_pi / (grid_dims[1] * domain_width),
    )
    long_force = (dot(number, turning_high) + dot(number, turning_low))[:, :slots] * scales

    zero_cells = saved_ref[0]
    one_cells = saved_ref[1]
    left = [
        jnp.concatenate([two_cells, one_cells], axis=1),
        jnp.concatenate([grad_cells, zero_cells], axis=1),
    ]
    right = jnp.concatenate(
        [
            jnp.concatenate([one_cells, two_cells], axis=1),
            jnp.concatenate([zero_cells, grad_cells], axis=1),
        ],
        axis=1,
    )
    left = jnp.concatenate(left, axis=1)
    for shift in range(3):
        moved = right if shift == 1 else pltpu.roll(right, (1 - shift) % cells, 0)
        shift_ref[shift, 0:cells] = moved
        shift_ref[shift, cells:] = moved[:reach]
    one, two = radial_one_ref[...], radial_two_ref[...]
    pairs = jnp.concatenate([two, two, one, one], axis=1)
    pairs = jnp.broadcast_to(pairs[:, None, :], (NBASIS, 16, pad)).reshape(128, pad).T
    pair_column = iota((pad, 128), 1) % 16
    shares = jnp.zeros((cells, 128), f32)
    for number, (ox, oy, oz) in enumerate(offsets):
        distance = (ox * ext + oy) * ext
        products = left * shift_ref[oz + 1, distance : distance + cells]
        chosen = jnp.where(pair_column == number, pairs, 0.0).astype(bf16)
        shares = shares + dot(products.astype(bf16), chosen)
    shares = shares.T
    sep = [get_sep(slice(16 * part, 16 * part + 16)) for part in range(3)]
    square = sep[0] * sep[0] + sep[1] * sep[1] + sep[2] * sep[2]
    length = jnp.sqrt(square)
    base = jnp.maximum(1.0 - square * (1.0 / (cutoff * cutoff)), 0.0)
    inward = length * base * (-4.0 / (cutoff * cutoff))
    outward = (-2.0 * gamma) * base * base
    strength = jnp.zeros((16, cells), f32)
    for number in range(NBASIS):
        gap = length - step * number
        slope = jnp.exp(-gamma * gap * gap) * (inward + gap * outward)
        strength = strength + slope * shares[16 * number : 16 * number + 16]
    strength = strength / length
    totals = []
    for part in range(3):
        force = jnp.where(iota((16, cells), 0) < half, sep[part] * strength, 0.0)
        total = -jnp.sum(force, axis=0, keepdims=True)
        for number, (ox, oy, oz) in enumerate(offsets):
            distance = (ox * ext + oy) * ext + oz
            total = total + pltpu.roll(force[number : number + 1], distance, 1)
        totals.append(total)
    total = jnp.concatenate(totals + [jnp.zeros((5, cells), f32)], axis=0)
    site_total = exact(total[:, :inner_lanes], picks, nt)
    lines = jnp.concatenate([-(site_total[0:3] + long_force[0:3]), site_energy], axis=0)
    lines = jnp.concatenate([lines, jnp.zeros((4, slots), f32)], axis=0)
    hot = (iota((slots, slots), 0) == site_of(coords_of(pos_ref))).astype(f32).astype(bf16)
    lines = exact(lines, hot)
    for axis in range(3):
        force_out[0, 0, axis] = lines[axis : axis + 1]
    energy_out[0, 0] = lines[3:4]


def kernel_params():
    return pltpu.CompilerParams(vmem_limit_bytes=56 * 1024 * 1024)


def whole_box(
    species,
    counts,
    positions,
    ghost_rows,
    neighbours,
    kvec,
    embed,
    radial_one,
    radial_two,
    mix_one,
    mix_two,
    lr_filter,
    read_weight,
    read_bias,
    energy_weight,
):
    axes = ("gx", "gy", "gz")
    vmem = pl.BlockSpec(memory_space=pltpu.VMEM)
    smem = pl.BlockSpec(memory_space=pltpu.SMEM)
    placed = pl.pallas_call(
        place_kernel,
        out_shape=jax.ShapeDtypeStruct((domains, 4, slots), f32),
        in_specs=[smem, vmem, vmem],
        out_specs=vmem,
    )(counts, positions.transpose(0, 1, 3, 2, 4), species)
    shared = lax.all_to_all(placed, axes, 0, 0, tiled=True)
    gain = pl.pallas_call(
        gain_kernel,
        out_shape=jax.ShapeDtypeStruct((chan, table), f32),
        in_specs=[vmem] * 2,
        out_specs=vmem,
    )(kvec, lr_filter)
    tables = (
        gain,
        embed,
        radial_one,
        radial_two,
        mix_one,
        mix_two,
        read_weight,
        read_bias.reshape(1, chan),
        energy_weight.reshape(1, chan),
    )
    energies, forces = box_call(shared, positions.transpose(0, 1, 3, 2, 4), tables)
    return (energies, forces.transpose(0, 1, 3, 2, 4))


def box_call(shared, coords, tables):
    vmem = pl.BlockSpec(memory_space=pltpu.VMEM)
    grid_shape = (ext, ext, ext, planes, 128)
    return pl.pallas_call(
        box_kernel,
        out_shape=(
            jax.ShapeDtypeStruct((1, 1, 1, slots), f32),
            jax.ShapeDtypeStruct((1, 1, 3, 1, slots), f32),
        ),
        in_specs=[vmem] * 11,
        out_specs=(vmem, vmem),
        scratch_shapes=[
            pltpu.VMEM((cells // 128, 64 * 16, 128), f32),
            pltpu.VMEM((64, pad), f32),
            pltpu.VMEM((2, rows_all, 128), f32),
            pltpu.VMEM((half, rows_all, pad), bf16),
            pltpu.VMEM((table, 2 * span), bf16),
            pltpu.VMEM((table, cells), bf16),
            pltpu.VMEM(grid_shape, f32),
            pltpu.VMEM(grid_shape, f32),
            pltpu.VMEM(grid_shape, f32),
            pltpu.VMEM((rows_all, 128), f32),
            pltpu.VMEM((2, pad, 128), f32),
            pltpu.VMEM((8, 2 * span), f32),
            pltpu.VMEM((rows_all, pad), bf16),
            pltpu.VMEM((2, cells, chan), f32),
            pltpu.VMEM((pad, pad), f32),
            pltpu.VMEM((3, cells + reach, 256), f32),
            pltpu.VMEM((chan, 2 * span), bf16),
            pltpu.VMEM((chan, table), f32),
        ],
        compiler_params=kernel_params(),
    )(shared, coords, *tables)


def solution(mesh):
    in_specs = (
        P(("group", "gx"), "gy", "gz", None),
        P(("group", "gx"), "gy", "gz"),
        P(("group", "gx"), "gy", "gz", None, None),
        P(("group", "gx"), "gy", "gz", None),
        P(("group", "gx"), "gy", "gz", None, None),
        P(),
        P(),
        P(),
        P(),
        P(),
        P(),
        P(),
        P(),
        P(),
        P(),
    )
    out_specs = (P(("group", "gx"), "gy", "gz", None), P(("group", "gx"), "gy", "gz", None, None))
    sizes = tuple(mesh.shape[axis] for axis in ("gx", "gy", "gz"))
    plan = whole_box if sizes == grid_dims else local
    return jax.shard_map(plan, mesh=mesh, in_specs=in_specs, out_specs=out_specs, check_vma=False)
```

```python
import math

import jax
import jax.numpy as jnp
import numpy as np
from jax import lax
from jax.experimental import pallas as pl
from jax.experimental.pallas import tpu as pltpu
from jax.sharding import PartitionSpec as P

SIDE = 6
KVEC = 4096
NBASIS = 8
NEIGH = 26


spacing = 2.5
cutoff = 5.0
two_pi = 6.283185307179586
highest = lax.Precision.HIGHEST


def passed_along(block, axis, distance):
    devices = range(lax.axis_size(axis))
    route = [((i - distance) % len(devices), i) for i in devices]
    return lax.ppermute(block, axis, route)


def extended(block, sides, width):
    for axis, dim in sides:
        count = lax.axis_size(axis)
        forward = [(i, i + 1) for i in range(count - 1)]
        forward.append((count - 1, 0))
        backward = [(target, source) for source, target in forward]
        low = lax.ppermute(
            lax.slice_in_dim(block, block.shape[dim] - width, None, axis=dim), axis, forward
        )
        high = lax.ppermute(lax.slice_in_dim(block, 0, width, axis=dim), axis, backward)
        block = jnp.concatenate([low, block, high], axis=dim)
    return block


def rows_per_block():
    return SIDE * SIDE


def boundary_list(side):
    site_ids = np.arange(side**3).reshape(side, side, side)
    inner = np.zeros((side, side, side), dtype=bool)
    inner[1 : side - 1, 1 : side - 1, 1 : side - 1] = True
    return site_ids[~inner].astype(np.int32)


def radial_terms(distance):
    centres = cutoff * jnp.arange(NBASIS).astype(jnp.float32) / (NBASIS - 1)
    sharpness = (NBASIS / cutoff) ** 2
    gap_value = distance[None] - centres[:, None, None]
    gaussian = jnp.exp(-sharpness * gap_value * gap_value)
    envelope_base = jnp.maximum(1.0 - distance * distance / (cutoff * cutoff), 0.0)
    envelope = envelope_base * envelope_base
    envelope_slope = -4.0 * distance * envelope_base / (cutoff * cutoff)
    radial_value = gaussian * envelope[None]
    radial_slope = gaussian * (envelope_slope[None] - 2.0 * sharpness * gap_value * envelope[None])
    return (radial_value, radial_slope)


def embed_codes(type_code, embed):
    species_ids = jnp.arange(1, embed.shape[0] + 1, dtype=jnp.int32).astype(type_code.dtype)
    one_hot = (type_code[None, :] == species_ids[:, None]).astype(jnp.float32)
    return jnp.dot(embed.T, one_hot, precision=highest, preferred_element_type=jnp.float32)


def cell_shift():
    ext_side = SIDE + 2
    cells = jnp.arange(ext_side**3, dtype=jnp.int32)
    coords = jnp.stack(
        [cells // (ext_side * ext_side), cells // ext_side % ext_side, cells % ext_side]
    )
    domain_width = SIDE * spacing
    return jnp.where(
        coords == 0, -domain_width, jnp.where(coords == ext_side - 1, domain_width, 0.0)
    ).astype(jnp.float32)


def pair_geometry(coords_own, pool_coords, pair_lists):
    separation = jnp.take(pool_coords, pair_lists, axis=1) - coords_own[:, None, :]
    distance = jnp.sqrt(jnp.sum(separation * separation, axis=0))
    return (separation, distance)


def message_forward(pool_values, pair_lists, radial_value, radial_weight):
    radial_filter = jnp.einsum("bc,bma->cma", radial_weight, radial_value, precision=highest)
    neighbour_value = jnp.take(pool_values, pair_lists, axis=1)
    return jnp.sum(radial_filter * neighbour_value, axis=1)


def message_backward(
    grad_message,
    pool_values,
    pair_lists,
    radial_value,
    radial_slope,
    radial_weight,
    separation,
    distance,
    pool_size,
    with_features,
):
    neighbour_value = jnp.take(pool_values, pair_lists, axis=1)
    contracted = jnp.einsum(
        "bc,cma->bma", radial_weight, grad_message[:, None, :] * neighbour_value, precision=highest
    )
    energy_slope = jnp.sum(radial_slope * contracted, axis=0)
    pair_force = separation * (energy_slope / distance)[None]
    flat_index = pair_lists.reshape(-1)
    grad_pool = (
        jnp.zeros((3, pool_size), jnp.float32).at[:, flat_index].add(pair_force.reshape(3, -1))
    )
    grad_own = -jnp.sum(pair_force, axis=1)
    if with_features:
        radial_filter = jnp.einsum("bc,bma->cma", radial_weight, radial_value, precision=highest)
        spread = (radial_filter * grad_message[:, None, :]).reshape(radial_filter.shape[0], -1)
        feature_pool = (
            jnp.zeros((radial_filter.shape[0], pool_size), jnp.float32)
            .at[:, flat_index]
            .add(spread)
        )
        return (grad_pool, grad_own, feature_pool)
    return (grad_pool, grad_own, grad_pool)


def phase_table(fraction, wave_numbers):
    phase_angle = two_pi * (
        fraction[0][:, None] * wave_numbers[0][None, :]
        + fraction[1][:, None] * wave_numbers[1][None, :]
        + fraction[2][:, None] * wave_numbers[2][None, :]
    )
    return (jnp.cos(phase_angle).astype(jnp.bfloat16), jnp.sin(phase_angle).astype(jnp.bfloat16))


def read_long(cosine_low, sine_low, filtered):
    dims = (((1,), (1,)), ((), ()))
    return lax.dot_general(
        filtered[0], cosine_low, dims, preferred_element_type=jnp.float32
    ) + lax.dot_general(filtered[1], sine_low, dims, preferred_element_type=jnp.float32)


def block_live(step_index, live_count):
    block_rows = rows_per_block()
    per_member = SIDE**3 // block_rows
    first_row = (step_index % per_member * block_rows).astype(jnp.float32)
    return first_row < live_count[step_index // per_member]


def lr_struct(fraction, row_values, live_count, wave_numbers):
    block_rows = rows_per_block()
    blocks = fraction.shape[1] // block_rows

    def step(step_index, running):

        def work(running):
            offset = step_index * block_rows
            frac_block = lax.dynamic_slice_in_dim(fraction, offset, block_rows, 1)
            feature_block = lax.dynamic_slice_in_dim(row_values, offset, block_rows, 1)
            cosine_low, sine_low = phase_table(frac_block, wave_numbers)
            term = jnp.stack(
                [
                    jnp.dot(feature_block, cosine_low, preferred_element_type=jnp.float32),
                    jnp.dot(feature_block, sine_low, preferred_element_type=jnp.float32),
                ]
            )
            return running + term

        return lax.cond(
            block_live(step_index, live_count), work, lambda unchanged: unchanged, running
        )

    initial = jnp.zeros((2, row_values.shape[0], wave_numbers.shape[1]), jnp.float32)
    return lax.fori_loop(0, blocks, step, initial)


def lr_read(fraction, live_count, wave_numbers, filtered):
    block_rows = rows_per_block()
    blocks = fraction.shape[1] // block_rows

    def step(step_index, result):

        def work(result):
            offset = step_index * block_rows
            cosine_low, sine_low = phase_table(
                lax.dynamic_slice_in_dim(fraction, offset, block_rows, 1), wave_numbers
            )
            return lax.dynamic_update_slice_in_dim(
                result, read_long(cosine_low, sine_low, filtered), offset, 1
            )

        return lax.cond(
            block_live(step_index, live_count), work, lambda unchanged: unchanged, result
        )

    initial = jnp.zeros((filtered.shape[1], fraction.shape[1]), jnp.float32)
    return lax.fori_loop(0, blocks, step, initial)


def lr_back(
    fraction,
    rounded_rows,
    grad_rows,
    occupied_rows,
    live_count,
    wave_numbers,
    wave_factors,
    filtered,
    back_filtered,
):
    block_rows = rows_per_block()
    blocks = fraction.shape[1] // block_rows
    dims = (((0,), (0,)), ((), ()))
    right_real = jnp.concatenate([filtered[0], back_filtered[0]], axis=0)
    right_imag = jnp.concatenate([filtered[1], back_filtered[1]], axis=0)

    def step(step_index, carried):

        def work(carried):
            grad_long, force_long = carried
            offset = step_index * block_rows
            cosine_low, sine_low = phase_table(
                lax.dynamic_slice_in_dim(fraction, offset, block_rows, 1), wave_numbers
            )
            mask_block = lax.dynamic_slice_in_dim(occupied_rows, offset, block_rows, 0)
            grad_block = mask_block[None] * read_long(cosine_low, sine_low, back_filtered)
            stacked_left = jnp.concatenate(
                [
                    lax.dynamic_slice_in_dim(grad_rows, offset, block_rows, 1),
                    lax.dynamic_slice_in_dim(rounded_rows, offset, block_rows, 1),
                ],
                axis=0,
            )
            real_part = lax.dot_general(
                stacked_left, right_real, dims, preferred_element_type=jnp.float32
            )
            imag_part = lax.dot_general(
                stacked_left, right_imag, dims, preferred_element_type=jnp.float32
            )
            turning = (
                cosine_low.astype(jnp.float32) * imag_part
                - sine_low.astype(jnp.float32) * real_part
            )
            force_block = lax.dot_general(
                wave_factors,
                turning,
                (((1,), (1,)), ((), ())),
                precision=highest,
                preferred_element_type=jnp.float32,
            )
            return (
                lax.dynamic_update_slice_in_dim(grad_long, grad_block, offset, 1),
                lax.dynamic_update_slice_in_dim(force_long, force_block, offset, 1),
            )

        return lax.cond(
            block_live(step_index, live_count), work, lambda unchanged: unchanged, carried
        )

    initial = (
        jnp.zeros((rounded_rows.shape[0], fraction.shape[1]), jnp.float32),
        jnp.zeros((3, fraction.shape[1]), jnp.float32),
    )
    return lax.fori_loop(0, blocks, step, initial)


def boundary_grid(values, ghost_slots, boundary):
    picked = jnp.take(values, ghost_slots, axis=1)
    site_grid = jnp.zeros((values.shape[0], SIDE**3), values.dtype).at[:, boundary].set(picked)
    return site_grid.reshape(values.shape[0], SIDE, SIDE, SIDE)


def fold_slab(site_grid, axis_number, from_left, from_right):
    inner_size = site_grid.shape[axis_number] - 2
    inner = lax.slice_in_dim(site_grid, 1, inner_size + 1, axis=axis_number)
    first_layer = lax.slice_in_dim(inner, 0, 1, axis=axis_number) + from_left
    last_layer = lax.slice_in_dim(inner, inner_size - 1, inner_size, axis=axis_number) + from_right
    middle = lax.slice_in_dim(inner, 1, inner_size - 1, axis=axis_number)
    return jnp.concatenate([first_layer, middle, last_layer], axis=axis_number)


def return_halo(site_grid):
    edge = site_grid.shape[3] - 1
    received = [
        passed_along(
            lax.slice_in_dim(site_grid, slab_start, slab_start + 1, axis=3), "gz", direction
        )
        for direction, slab_start in ((1, edge), (-1, 0))
    ]
    site_grid = fold_slab(site_grid, 3, received[0], received[1])
    edge = site_grid.shape[2] - 1
    received = [
        passed_along(
            lax.slice_in_dim(site_grid, slab_start, slab_start + 1, axis=2), "gy", direction
        )
        for direction, slab_start in ((1, edge), (-1, 0))
    ]
    site_grid = fold_slab(site_grid, 2, received[0], received[1])
    edge = site_grid.shape[1] - 1
    received = [
        passed_along(
            lax.slice_in_dim(site_grid, slab_start, slab_start + 1, axis=1), "gx", direction
        )
        for direction, slab_start in ((1, edge), (-1, 0))
    ]
    return fold_slab(site_grid, 1, received[0], received[1])


def ghost_to_rows(site_grid, ghost_slots, boundary):
    features = site_grid.shape[0]
    picked = site_grid.reshape(features, -1)[:, boundary]
    return jnp.zeros((features, SIDE**3), site_grid.dtype).at[:, ghost_slots].add(picked)


def local(
    species,
    counts,
    positions,
    ghost_rows,
    neighbours,
    kvec,
    embed,
    radial_one,
    radial_two,
    mix_one,
    mix_two,
    lr_filter,
    read_weight,
    read_bias,
    energy_weight,
):
    slot_count = SIDE**3
    ext_side = SIDE + 2
    pool_size = slot_count + ext_side**3
    pair_scale = 1.0 / math.sqrt(NEIGH)
    domain_width = SIDE * spacing
    mesh_sizes = (lax.axis_size("gx"), lax.axis_size("gy"), lax.axis_size("gz"))
    box_length = tuple((count_along * domain_width for count_along in mesh_sizes))
    wave_scale = 1.0 / math.sqrt(
        KVEC * (slot_count * mesh_sizes[0] * mesh_sizes[1] * mesh_sizes[2])
    )
    species_flat = species.reshape(slot_count)
    live_total = counts.reshape(())
    coords_own = positions.reshape(3, slot_count)
    ghost_slots = ghost_rows.reshape(-1)
    pair_lists = neighbours.reshape(NEIGH, slot_count)
    boundary = jnp.asarray(boundary_list(SIDE))
    cell_offset = cell_shift()
    occupied = (jnp.arange(slot_count, dtype=jnp.int32) < live_total).astype(jnp.float32)
    type_code = jnp.where(occupied > 0, species_flat + 1, 0).astype(jnp.float32)
    hidden_zero = embed_codes(species_flat + 1, embed)
    masked_zero = hidden_zero * occupied[None]
    packet = boundary_grid(
        jnp.concatenate([coords_own, type_code[None]], axis=0), ghost_slots, boundary
    )
    ext_atoms = extended(packet, (("gx", 1), ("gy", 2), ("gz", 3)), 1).reshape(4, -1)
    pool_coords = jnp.concatenate([coords_own, ext_atoms[:3] + cell_offset], axis=1)
    pool_zero = jnp.concatenate([masked_zero, embed_codes(ext_atoms[3], embed)], axis=1)
    separation, distance = pair_geometry(coords_own, pool_coords, pair_lists)
    radial_value, radial_slope = radial_terms(distance)
    message = message_forward(pool_zero, pair_lists, radial_value, radial_one)
    hidden_one = hidden_zero + pair_scale * jnp.dot(
        mix_one.T, message, precision=highest, preferred_element_type=jnp.float32
    )
    masked_one = hidden_one * occupied[None]
    rounded_one = masked_one.astype(jnp.bfloat16)
    domain_pos = (lax.axis_index("gx"), lax.axis_index("gy"), lax.axis_index("gz"))
    fraction = jnp.stack(
        [
            (domain_pos[axis_id].astype(jnp.float32) * domain_width + coords_own[axis_id])
            / box_length[axis_id]
            for axis_id in range(3)
        ]
    )
    wave_numbers = kvec.astype(jnp.float32)
    wave_factors = jnp.stack(
        [two_pi * wave_numbers[axis_id] / box_length[axis_id] for axis_id in range(3)]
    )
    own_count = jnp.sum(occupied)[None]
    share_size = KVEC // (mesh_sizes[0] * mesh_sizes[1] * mesh_sizes[2])
    share_start = lax.axis_index(("gx", "gy", "gz")) * share_size
    filter_share = lax.dynamic_slice_in_dim(lr_filter, share_start, share_size, 1)
    struct_part = lax.psum_scatter(
        lr_struct(fraction, rounded_one, own_count, wave_numbers),
        ("gx", "gy", "gz"),
        scatter_dimension=2,
        tiled=True,
    )
    filtered = lax.all_gather(
        (struct_part * filter_share[None] * wave_scale).astype(jnp.bfloat16),
        ("gx", "gy", "gz"),
        axis=2,
        tiled=True,
    )
    long_part = lr_read(fraction, own_count, wave_numbers, filtered)
    masked_ext = extended(
        boundary_grid(masked_one, ghost_slots, boundary).astype(jnp.bfloat16),
        (("gx", 1), ("gy", 2), ("gz", 3)),
        1,
    ).astype(jnp.float32)
    pool_one = jnp.concatenate([masked_one, masked_ext.reshape(masked_one.shape[0], -1)], axis=1)
    message_two = message_forward(pool_one, pair_lists, radial_value, radial_two)
    hidden_two = (
        hidden_one
        + pair_scale
        * jnp.dot(mix_two.T, message_two, precision=highest, preferred_element_type=jnp.float32)
        + long_part
    )
    activation = (
        jnp.dot(read_weight.T, hidden_two, precision=highest, preferred_element_type=jnp.float32)
        + read_bias[:, None]
    )
    gating = jax.nn.sigmoid(activation)
    energies = occupied * jnp.sum(activation * gating * energy_weight[:, None], axis=0)
    grad_act = (
        occupied[None] * energy_weight[:, None] * gating * (1.0 + activation * (1.0 - gating))
    )
    grad_two = jnp.dot(read_weight, grad_act, precision=highest, preferred_element_type=jnp.float32)
    grad_low = grad_two.astype(jnp.bfloat16)
    grad_part = lax.psum_scatter(
        lr_struct(fraction, grad_low, own_count, wave_numbers),
        ("gx", "gy", "gz"),
        scatter_dimension=2,
        tiled=True,
    )
    back_filtered = lax.all_gather(
        (grad_part * filter_share[None] * wave_scale).astype(jnp.bfloat16),
        ("gx", "gy", "gz"),
        axis=2,
        tiled=True,
    )
    grad_long, force_long = lr_back(
        fraction,
        rounded_one,
        grad_low,
        occupied,
        own_count,
        wave_numbers,
        wave_factors,
        filtered,
        back_filtered,
    )
    grad_message = pair_scale * jnp.dot(
        mix_two, grad_two, precision=highest, preferred_element_type=jnp.float32
    )
    grad_pool, grad_own_two, feature_pool = message_backward(
        grad_message,
        pool_one,
        pair_lists,
        radial_value,
        radial_slope,
        radial_two,
        separation,
        distance,
        pool_size,
        True,
    )
    combined = jnp.concatenate([feature_pool, grad_pool], axis=0)
    features = combined.shape[0]
    returned_two = ghost_to_rows(
        return_halo(combined[:, slot_count:].reshape(features, ext_side, ext_side, ext_side)),
        ghost_slots,
        boundary,
    )
    own_two = combined[:, :slot_count]
    channels = masked_one.shape[0]
    grad_one = (
        grad_two + grad_long + occupied[None] * (own_two[:channels] + returned_two[:channels])
    )
    grad_message_one = pair_scale * jnp.dot(
        mix_one, grad_one, precision=highest, preferred_element_type=jnp.float32
    )
    grad_pool_one, grad_own_one, unused = message_backward(
        grad_message_one,
        pool_zero,
        pair_lists,
        radial_value,
        radial_slope,
        radial_one,
        separation,
        distance,
        pool_size,
        False,
    )
    layer_one_grad = grad_own_one + grad_pool_one[:, :slot_count]
    returned_one = ghost_to_rows(
        return_halo(grad_pool_one[:, slot_count:].reshape(3, ext_side, ext_side, ext_side)),
        ghost_slots,
        boundary,
    )
    total_grad = (
        layer_one_grad
        + returned_one
        + force_long
        + grad_own_two
        + own_two[channels:]
        + returned_two[channels:]
    )
    forces = -total_grad
    return (energies.reshape(1, 1, 1, slot_count), forces.reshape(1, 1, 1, 3, slot_count))


offsets = tuple(
    (ox, oy, oz)
    for ox in (0, 1)
    for oy in (-1, 0, 1)
    for oz in (-1, 0, 1)
    if (ox, oy, oz) > (0, 0, 0)
)
half = len(offsets)
slots = SIDE**3
ext = SIDE + 2
cells = ext**3
inner_lanes = SIDE * ext * ext
reach = ext * ext + 2 * ext
chan = 64
grid_dims = (4, 2, 2)
domains = 16
planes = 8
rows_all = slots * planes
waves = 648
table = 2 * waves
pad = 256
span = -(-rows_all // 128) * 128
gamma = (NBASIS / cutoff) ** 2
step = cutoff / (NBASIS - 1)
nt = (((1,), (1,)), ((), ()))
nn = (((1,), (0,)), ((), ()))
f32 = jnp.float32
bf16 = jnp.bfloat16


def dot(left, right, dims=nn, precision=None):
    return lax.dot_general(left, right, dims, precision=precision, preferred_element_type=f32)


def split(value):
    high = value.astype(bf16)
    return high, (value - high.astype(f32)).astype(bf16)


def dot_split(left, high, low):
    left_high, left_low = split(left)
    return dot(left_high, high) + dot(left_low, high) + dot(left_high, low)


def exact(left, hot, dims=nn):
    high = left.astype(bf16).astype(f32)
    rest = left - high
    middle = rest.astype(bf16).astype(f32)
    count = left.shape[0]
    stacked = jnp.concatenate([high, middle, rest - middle], axis=0).astype(bf16)
    parts = dot(stacked, hot, dims)
    return parts[:count] + parts[count : 2 * count] + parts[2 * count :]


def coords_of(ref):
    return jnp.concatenate([ref[0, 0, axis] for axis in range(3)], axis=0)


def site_of(coords):
    where = (coords * (1.0 / spacing)).astype(jnp.int32)
    return (where[0:1] * SIDE + where[1:2]) * SIDE + where[2:3]


def iota(shape, dim):
    return lax.broadcasted_iota(jnp.int32, shape, dim)


def place_kernel(count_ref, pos_ref, species_ref, out_ref):
    coords = coords_of(pos_ref)
    live = iota((1, slots), 1) < count_ref[0, 0, 0]
    code = jnp.where(live, species_ref[0, 0] + 1, 0).astype(f32)
    data = jnp.concatenate([coords, code, jnp.zeros((4, slots), f32)], axis=0)
    hot = (iota((slots, slots), 0) == site_of(coords)).astype(f32).astype(bf16)
    placed = exact(data, hot, nt)[0:4]
    for number in range(domains):
        out_ref[number] = placed


def twice(block):
    zero = jnp.zeros_like(block)
    return jnp.concatenate(
        [jnp.concatenate([block, zero], axis=1), jnp.concatenate([zero, block], axis=1)], axis=0
    )


def gain_kernel(kvec_ref, filter_ref, gain_ref):
    wave_scale = 1.0 / math.sqrt(KVEC * slots * domains)
    waves_in = kvec_ref[...]

    def folded(row):
        return jnp.where(row > 0, 2 * row - 1, -2 * row)

    index = (folded(waves_in[1:2]) * 9 + folded(waves_in[2:3])) * 8 + waves_in[0:1] - 1
    filter_high, filter_low = split(filter_ref[...] * wave_scale)
    parts = jnp.concatenate([filter_high, filter_low], axis=0)
    gain = jnp.zeros((waves, 2 * chan), f32)
    width = 1024
    for start in range(0, KVEC, width):
        hot = (iota((waves, width), 0) == index[:, start : start + width]).astype(f32).astype(bf16)
        gain = gain + dot(hot, parts[:, start : start + width], nt)
    gain = (gain[:, :chan] + gain[:, chan:]).reshape(waves // 8, 8, chan)
    gain_ref[...] = jnp.concatenate([gain, gain], axis=1).reshape(table, chan).T


def turn(fraction):
    rest = fraction - jnp.floor(fraction + 0.5)
    angle = rest * (0.5 * two_pi)
    square = angle * angle
    sine = angle * (
        1.0
        + square
        * (
            -1.0 / 6
            + square
            * (
                1.0 / 120
                + square * (-1.0 / 5040 + square * (1.0 / 362880 - square * (1.0 / 39916800)))
            )
        )
    )
    cosine = 1.0 + square * (
        -0.5
        + square
        * (
            1.0 / 24
            + square
            * (
                -1.0 / 720
                + square
                * (1.0 / 40320 + square * (-1.0 / 3628800 + square * (1.0 / 479001600)))
            )
        )
    )
    return 1.0 - 2.0 * sine * sine, 2.0 * sine * cosine


def fan(base, step_pairs):
    real, imag = base
    out = [(real, imag)]
    for cosine, sine in step_pairs:
        a, b, c, d = real * cosine, imag * sine, real * sine, imag * cosine
        out.append((a - b, c + d))
        out.append((a + b, d - c))
    return out


def wave_tile(coords, store):
    frac = [coords[axis] / (grid_dims[axis] * SIDE * spacing) for axis in range(3)]
    row = iota((8, 128), 0)
    base = turn(frac[0] * (row + 1).astype(f32))
    rest = turn(jnp.where(row < 4, frac[1], frac[2]) * (row % 4 + 1).astype(f32))

    def line(index):
        return tuple(jnp.broadcast_to(part[index : index + 1], (8, 128)) for part in rest)

    y_lines = [line(index) for index in range(4)]
    z_lines = [line(index + 4) for index in range(4)]
    index = 0
    for level in fan(base, y_lines):
        for real, imag in fan(level, z_lines):
            store(index, jnp.concatenate([real, imag], axis=0).astype(bf16))
            index += 1
        yield index


def swap_lanes(value):
    return pltpu.roll(value, chan, value.ndim - 1)


def swap_planes(value):
    up = pltpu.roll(value, 1, 1)
    down = pltpu.roll(value, planes - 1, 1)
    return jnp.where(iota(value.shape, 1) % 2 == 0, down, up)


def as_three(value):
    return value.reshape((-1,) + value.shape[-2:])


def fill_ghosts(ref):
    inner = slice(1, SIDE + 1)
    for ghost, source, shift in ((0, SIDE, 2), (SIDE + 1, 1, planes - 2)):
        value = ref[source, inner, inner]
        ref[ghost, inner, inner] = pltpu.roll(as_three(value), shift, 1).reshape(value.shape)
    for ghost, source in ((0, SIDE), (SIDE + 1, 1)):
        value = ref[:, source, inner]
        ref[:, ghost, inner] = swap_planes(as_three(value)).reshape(value.shape)
    for ghost, source in ((0, SIDE), (SIDE + 1, 1)):
        value = ref[:, :, source]
        ref[:, :, ghost] = swap_lanes(as_three(value)).reshape(value.shape)


def fold_ghosts(ref):
    inner = slice(1, SIDE + 1)
    for ghost, target in ((SIDE + 1, 1), (0, SIDE)):
        value = ref[:, :, ghost]
        ref[:, :, target] = ref[:, :, target] + swap_lanes(as_three(value)).reshape(value.shape)
    for ghost, target in ((SIDE + 1, 1), (0, SIDE)):
        value = ref[:, ghost, inner]
        ref[:, target, inner] = ref[:, target, inner] + swap_planes(as_three(value)).reshape(
            value.shape
        )
    for ghost, target, shift in ((SIDE + 1, 1, 2), (0, SIDE, planes - 2)):
        value = ref[ghost, inner, inner]
        ref[target, inner, inner] = ref[target, inner, inner] + pltpu.roll(
            as_three(value), shift, 1
        ).reshape(value.shape)


def inner_rows(ref, level):
    inner = slice(1, SIDE + 1)
    return ref[level + 1, inner, inner].reshape(rows_all // SIDE, 128)


def set_level(ref, level, value):
    inner = slice(1, SIDE + 1)
    ref[level + 1, inner, inner] = value.reshape(SIDE, SIDE, planes, 128)


def level_rows(level):
    return slice(level * (rows_all // SIDE), (level + 1) * (rows_all // SIDE))


def set_inner(ref, value):
    inner = slice(1, SIDE + 1)
    ref[inner, inner, inner] = value.reshape(SIDE, SIDE, SIDE, planes, 128)


def convolve(filters, layer, source, target, beside=None):
    target[...] = jnp.zeros(target.shape, f32)
    lanes = slice(layer * 128, layer * 128 + 128)
    groups = {}
    for number, (ox, oy, oz) in enumerate(offsets):
        groups.setdefault((ox, oy), []).append((number, oz))

    def one_line(line):
        x = line // SIDE
        y = line % SIDE
        own = [source[x + 1, y + 1, z + 1] for z in range(SIDE)]
        own_sum = [jnp.zeros((planes, 128), f32)] * SIDE
        for (ox, oy), members in groups.items():
            there = [source[x + 1 + ox, y + 1 + oy, z] for z in range(ext)]
            sums = [None] * ext
            first = pl.multiple_of(line * (SIDE * planes), SIDE * planes)
            weights = [
                filters[number, pl.ds(first, SIDE * planes), lanes].astype(f32)
                for number, _ in members
            ]
            for z in range(SIDE):
                for block, (_, oz) in zip(weights, members):
                    weight = block[z * planes : z * planes + planes]
                    own_sum[z] = own_sum[z] + weight * there[z + 1 + oz]
                    term = weight * own[z]
                    spot = z + 1 + oz
                    sums[spot] = term if sums[spot] is None else sums[spot] + term
            for z in range(ext):
                if sums[z] is not None:
                    target[x + 1 + ox, y + 1 + oy, z] = target[x + 1 + ox, y + 1 + oy, z] + sums[z]
        for z in range(SIDE):
            target[x + 1, y + 1, z + 1] = target[x + 1, y + 1, z + 1] + own_sum[z]

    def body(number, carry):
        for part in range(6):
            one_line(number * 6 + part)
            if beside is not None and part % 3 == 0:
                beside(number * 2 + part // 3)
        return carry

    lax.fori_loop(0, SIDE, body, 0)
    fold_ghosts(target)


def spread(block):
    return jnp.broadcast_to(block[:, None, :], (NBASIS, 16, chan)).reshape(128, chan)


def wide(left, right):
    left, right = spread(left), spread(right)
    line = jnp.concatenate([left, left, right, right], axis=1)
    return jnp.concatenate([line, line], axis=0)


def doubled(ref):
    return jnp.concatenate([ref[...], ref[...]], axis=1)


def box_kernel(
    all_ref,
    pos_ref,
    gain_ref,
    embed_ref,
    radial_one_ref,
    radial_two_ref,
    mix_one_ref,
    mix_two_ref,
    read_ref,
    bias_ref,
    energy_ref,
    energy_out,
    force_out,
    sep_ref,
    sites_ref,
    basis_ref,
    filters_ref,
    waves_ref,
    ring_ref,
    zero_ref,
    one_ref,
    sum_ref,
    packed_ref,
    own_ref,
    flat_ref,
    low_ref,
    saved_ref,
    radial_ref,
    shift_ref,
    turned_ref,
    parts_ref,
):
    home = [lax.axis_index(axis) for axis in ("gx", "gy", "gz")]
    pair_scale = 1.0 / math.sqrt(NEIGH)
    fall = jnp.exp(-gamma * jnp.square(step * iota((NBASIS, 1), 0).astype(f32)))
    rows = iota((pad, pad), 0)
    columns = iota((pad, pad), 1)
    kept = (rows // 128) == (columns % 128 // chan)
    radial_ref[...] = jnp.where(
        kept, wide(radial_one_ref[...] * fall, radial_two_ref[...] * fall), 0.0
    )
    table_rows = jnp.concatenate([embed_ref[...], jnp.zeros((2, chan), f32)], axis=0)
    table_high = table_rows.astype(bf16).astype(f32)
    species_rows = kept & (rows % 16 == half)
    embeds = jnp.where(species_rows, wide(table_high, table_rows - table_high), 0.0).astype(bf16)
    lives = jnp.where(species_rows[:, :128], 1.0, 0.0).astype(bf16)
    sites_ref[...] = jnp.zeros((4 * domains, pad), f32)
    flat_ref[...] = jnp.zeros(flat_ref.shape, f32)
    domain_width = SIDE * spacing
    offset_row = iota((4, slots), 0)
    for number in range(domains):
        spot = [
            lax.rem(home[axis] + part, grid_dims[axis])
            for axis, part in enumerate((number // 4, number // 2 % 2, number % 2))
        ]
        block = all_ref[(spot[0] * 2 + spot[1]) * 2 + spot[2]]
        sites_ref[number * 4 : number * 4 + 4, 0:slots] = block
        shifts = [part * domain_width for part in (number // 4, number // 2 % 2, number % 2)]
        moved = jnp.where(
            offset_row == 0, shifts[0], jnp.where(offset_row == 1, shifts[1], shifts[2])
        )
        start = number % 2 * span + number // 2 * slots
        flat_ref[0:4, start : start + slots] = block + moved
    sites = sites_ref[:, 0:slots]

    lane = iota((1, cells), 1)
    coords = [(lane // (ext * ext) + 1) % ext, lane // ext % ext, lane % ext]
    wrapped = [(value + SIDE - 1) % SIDE for value in coords]
    wrapped_site = (wrapped[0] * SIDE + wrapped[1]) * SIDE + wrapped[2]
    inside = coords[0] >= 0
    for value in coords:
        inside = inside & (value > 0) & (value < ext - 1)
    hot_all = iota((slots, cells), 0) == wrapped_site
    grown = exact(sites, hot_all.astype(f32).astype(bf16))
    picks = (hot_all & inside)[:, :inner_lanes].astype(f32).astype(bf16)

    back16 = jnp.concatenate([grown[48:], grown[:48]], axis=0)
    ahead16 = jnp.concatenate([grown[16:], grown[:16]], axis=0)
    grown = jnp.where(coords[0] == 0, back16, jnp.where(coords[0] == ext - 1, ahead16, grown))
    swapped = jnp.concatenate(
        [grown[8 * (part ^ 1) : 8 * (part ^ 1) + 8] for part in range(8)], axis=0
    )
    grown = jnp.where((coords[1] == 0) | (coords[1] == ext - 1), swapped, grown)
    swapped = pltpu.roll(grown.reshape(8, 8, cells), 4, 1).reshape(64, cells)
    grown = jnp.where((coords[2] == 0) | (coords[2] == ext - 1), swapped, grown)
    component = iota((64, cells), 0) % 4
    for axis in range(3):
        moved = jnp.where(
            coords[axis] == 0,
            -domain_width,
            jnp.where(coords[axis] == ext - 1, domain_width, 0.0),
        )
        grown = grown + jnp.where(component == axis, moved, 0.0)
    own_ext = grown[0:4]
    tiles = cells // 128

    def put_sep(number, value):
        for tile in range(tiles):
            sep_ref[tile, pl.ds(number, 64, stride=16), :] = value[:, tile * 128 : tile * 128 + 128]

    def get_sep(window, count=tiles):
        return jnp.concatenate([sep_ref[tile, window, :] for tile in range(count)], axis=1)

    for number, (ox, oy, oz) in enumerate(offsets):
        distance = (ox * ext + oy) * ext + oz
        put_sep(number, pltpu.roll(grown, cells - distance, 1) - grown)
    for number in range(half, 16):
        put_sep(number, grown)

    basis_unroll = 8
    row16 = iota((16, inner_lanes), 0)

    def basis_of(domain):
        first = pl.multiple_of(domain * 64, 64)
        sx, sy, sz, codes = [get_sep(pl.ds(first + 16 * part, 16), inner_lanes // 128) for part in range(4)]
        square = sx * sx + sy * sy + sz * sz
        near = jnp.minimum(jnp.sqrt(square), cutoff)
        base = jnp.maximum(1.0 - square * (1.0 / (cutoff * cutoff)), 0.0)
        value = jnp.exp(-gamma * jnp.minimum(square, cutoff * cutoff)) * base * base
        ratio = jnp.exp((2.0 * gamma * step) * near)
        out = []
        for number in range(NBASIS):
            hit = jnp.where(codes == number + 1.0, 1.0, 0.0)
            out.append(jnp.where(row16 == half, hit, value))
            value = value * ratio
        return jnp.concatenate(out, axis=0).astype(bf16)

    def basis_step(plane, carry):
        both = jnp.concatenate([basis_of(2 * plane), basis_of(2 * plane + 1)], axis=0)
        picked = dot(picks, both, nt)
        for tile in range(2):
            basis_ref[tile, pl.ds(plane, slots, stride=planes), :] = picked[
                :, tile * 128 : tile * 128 + 128
            ]
        return carry

    def basis_group(number, carry):
        for part in range(basis_unroll):
            basis_step(number * basis_unroll + part, carry)
        return carry

    lax.fori_loop(0, planes // basis_unroll, basis_group, 0)

    basis_low = jnp.concatenate([basis_ref[0], basis_ref[1]], axis=1).astype(bf16)
    low_ref[...] = basis_low

    def flat_tile(start):
        block = flat_ref[:, pl.ds(start, 128)]

        def store(index, value):
            waves_ref[index * 16 : index * 16 + 16, pl.ds(start, 128)] = value

        return wave_tile([block[axis : axis + 1] for axis in range(3)], store)

    def wave_step(number, carry):
        chosen = jnp.where(iota((pad, pad), 0) % 16 == number, radial_ref[...], 0.0)
        chosen = chosen.astype(bf16)
        levels = []
        for part in range(2):
            levels.append(flat_tile(pl.multiple_of(number * 256 + part * 128, 128)))
        rows_each = rows_all // 6
        for part in range(6):
            window = slice(part * rows_each, part * rows_each + rows_each)
            filters_ref[number, window] = dot(low_ref[window], chosen).astype(bf16)
            for _ in range(3):
                next(levels[part // 3])
        return carry

    lax.fori_loop(0, half, wave_step, 0)
    for tile in range(2 * half, 2 * span // 128):
        list(flat_tile(tile * 128))
    for tile in range(cells // 128):
        lanes = slice(tile * 128, tile * 128 + 128)

        def store(index, value):
            ring_ref[index * 16 : index * 16 + 16, lanes] = value

        list(wave_tile([own_ext[axis : axis + 1, lanes] for axis in range(3)], store))

    start_values = dot(low_ref[...], jnp.concatenate([embeds, lives], axis=1))
    rows_ref = basis_ref.at[0]
    live_ref = basis_ref.at[1]
    live_ref[...] = start_values[:, 256:384]
    set_inner(zero_ref, start_values[:, :128] + start_values[:, 128:256])
    fill_ghosts(zero_ref)
    convolve(filters_ref, 0, zero_ref, sum_ref)
    flat = (cells * planes, 128)
    own_cells = pl.ds(0, cells, stride=planes)

    def cells_of(ref):
        value = ref.reshape(flat)[own_cells, :]
        return jnp.concatenate([value[ext * ext :], value[: ext * ext]], axis=0)[:, :chan]

    saved_ref[0] = cells_of(zero_ref)
    mix_high, mix_low = split(twice(mix_one_ref[...] * pair_scale))
    for level in range(SIDE):
        window = level_rows(level)
        first_rows = inner_rows(zero_ref, level) + live_ref[window] * dot_split(
            inner_rows(sum_ref, level), mix_high, mix_low
        )
        set_level(one_ref, level, first_rows)
        rows_ref[window] = first_rows
    fill_ghosts(one_ref)
    saved_ref[1] = cells_of(one_ref)
    two_ref = zero_ref

    def start_structure():
        for plane in range(planes):
            packed_ref[plane * slots : plane * slots + slots] = rows_ref[
                pl.ds(plane, slots, stride=planes), :
            ]
        turned = packed_ref[...].T
        zeros = jnp.zeros((chan, span - rows_all), f32)
        turned = jnp.concatenate([turned[:chan], zeros, turned[chan:], zeros], axis=1)
        turned_ref[...] = turned.astype(bf16)
        tail = 12 * pad
        parts_ref[...] = dot(turned_ref[:, tail:], waves_ref[:, tail:], nt)

    def step_structure(number):
        start = pl.multiple_of(number * pad, pad)
        parts_ref[...] = parts_ref[...] + dot(
            turned_ref[:, pl.ds(start, pad)], waves_ref[:, pl.ds(start, pad)], nt
        )

    start_structure()
    own_ref[...] = jnp.zeros(own_ref.shape, f32)
    own_ref[0, 0:slots] = rows_ref[pl.ds(0, slots, stride=planes), :]
    convolve(filters_ref, 1, one_ref, sum_ref, step_structure)
    filtered = parts_ref[...] * gain_ref[...]
    long_rows = dot(filtered.astype(bf16), waves_ref[...]).T
    for plane in range(planes):
        first = long_rows[plane * slots : plane * slots + slots]
        second = long_rows[span + plane * slots : span + plane * slots + slots]
        rows_ref[pl.ds(plane, slots, stride=planes), :] = jnp.concatenate([first, second], axis=1)
    read = read_ref[...]
    both = dot_split(mix_two_ref[...] * pair_scale, *split(read))
    act_high, act_low = split(jnp.concatenate([twice(read), twice(both)], axis=0))
    grad_high, grad_low = split(jnp.concatenate([twice(read.T), twice(both.T)], axis=1))
    bias = doubled(bias_ref)
    energy = doubled(energy_ref)
    for level in range(SIDE):
        window = level_rows(level)
        joined = jnp.concatenate(
            [inner_rows(one_ref, level) + rows_ref[window], inner_rows(sum_ref, level)], axis=1
        )
        act = dot_split(joined, act_high, act_low) + bias
        sig = 1.0 / (1.0 + jnp.exp(-act))
        weighted = live_ref[window] * energy * sig
        packed_ref[window] = weighted * act
        grads = dot_split(weighted * (1.0 + act * (1.0 - sig)), grad_high, grad_low)
        rows_ref[window] = grads[:, :128]
        set_level(two_ref, level, grads[:, 128:])
    own_energy = packed_ref[pl.ds(0, slots, stride=planes), :]
    first_half = jnp.where(iota((8, 128), 1) < chan, 1.0, 0.0)
    energy_high, energy_low = split(own_energy)
    first_half = first_half.astype(bf16)
    site_energy = (dot(first_half, energy_high, nt) + dot(first_half, energy_low, nt))[0:1]
    fill_ghosts(two_ref)
    start_structure()
    own_ref[1, 0:slots] = rows_ref[pl.ds(0, slots, stride=planes), :]
    two_cells = cells_of(two_ref)
    convolve(filters_ref, 1, two_ref, sum_ref, step_structure)
    back = parts_ref[...] * gain_ref[...]
    back_rows = back.astype(bf16)
    for level in range(SIDE):
        window = level_rows(level)
        set_level(
            sum_ref, level, rows_ref[window] + live_ref[window] * inner_rows(sum_ref, level)
        )
    fill_ghosts(sum_ref)
    sum_cells = cells_of(sum_ref)
    live_cells = jnp.where(own_ext[3:4] > 0, 1.0, 0.0)
    ring_long = (dot(back_rows, ring_ref[...]) * live_cells).T
    grad_cells = dot_split(sum_cells + ring_long, *split(mix_one_ref[...].T * pair_scale))

    def crossed(value):
        value = value.T.reshape(waves // 8, 2, 8, chan)
        value = jnp.concatenate([value[:, 1:2], -value[:, 0:1]], axis=1).reshape(table, chan)
        return jnp.concatenate([value, jnp.zeros((table, chan), f32)], axis=1).astype(bf16)

    response = dot(crossed(filtered), own_ref[1].astype(bf16), nt) + dot(
        crossed(back), own_ref[0].astype(bf16), nt
    )
    turning_high, turning_low = split(waves_ref[:, 0:pad].astype(f32) * response)
    spot = iota((8, table), 1)
    wave = spot // 16 * 8 + spot % 8

    def signed(index):
        return jnp.where(index % 2 == 1, (index + 1) // 2, -(index // 2))

    row = iota((8, table), 0)
    number = jnp.where(
        row == 0,
        wave % 8 + 1,
        jnp.where(row == 1, signed(wave // 72), jnp.where(row == 2, signed(wave // 8 % 9), 0)),
    )
    number = number.astype(f32).astype(bf16)
    scale_row = iota((8, 1), 0)
    scales = jnp.where(
        scale_row == 0,
        two_pi / (grid_dims[0] * domain_width),
        two_pi / (grid_dims[1] * domain_width),
    )
    long_force = (dot(number, turning_high) + dot(number, turning_low))[:, :slots] * scales

    zero_cells = saved_ref[0]
    one_cells = saved_ref[1]
    left = [
        jnp.concatenate([two_cells, one_cells], axis=1),
        jnp.concatenate([grad_cells, zero_cells], axis=1),
    ]
    right = jnp.concatenate(
        [
            jnp.concatenate([one_cells, two_cells], axis=1),
            jnp.concatenate([zero_cells, grad_cells], axis=1),
        ],
        axis=1,
    )
    left = jnp.concatenate(left, axis=1)
    for shift in range(3):
        moved = right if shift == 1 else pltpu.roll(right, (1 - shift) % cells, 0)
        shift_ref[shift, 0:cells] = moved
        shift_ref[shift, cells:] = moved[:reach]
    one, two = radial_one_ref[...], radial_two_ref[...]
    pairs = jnp.concatenate([two, two, one, one], axis=1)
    pairs = jnp.broadcast_to(pairs[:, None, :], (NBASIS, 16, pad)).reshape(128, pad).T
    pair_column = iota((pad, 128), 1) % 16
    shares = jnp.zeros((cells, 128), f32)
    for number, (ox, oy, oz) in enumerate(offsets):
        distance = (ox * ext + oy) * ext
        products = left * shift_ref[oz + 1, distance : distance + cells]
        chosen = jnp.where(pair_column == number, pairs, 0.0).astype(bf16)
        shares = shares + dot(products.astype(bf16), chosen)
    shares = shares.T
    sep = [get_sep(slice(16 * part, 16 * part + 16)) for part in range(3)]
    square = sep[0] * sep[0] + sep[1] * sep[1] + sep[2] * sep[2]
    length = jnp.sqrt(square)
    base = jnp.maximum(1.0 - square * (1.0 / (cutoff * cutoff)), 0.0)
    inward = length * base * (-4.0 / (cutoff * cutoff))
    outward = (-2.0 * gamma) * base * base
    strength = jnp.zeros((16, cells), f32)
    for number in range(NBASIS):
        gap = length - step * number
        slope = jnp.exp(-gamma * gap * gap) * (inward + gap * outward)
        strength = strength + slope * shares[16 * number : 16 * number + 16]
    strength = strength / length
    totals = []
    for part in range(3):
        force = jnp.where(iota((16, cells), 0) < half, sep[part] * strength, 0.0)
        total = -jnp.sum(force, axis=0, keepdims=True)
        for number, (ox, oy, oz) in enumerate(offsets):
            distance = (ox * ext + oy) * ext + oz
            total = total + pltpu.roll(force[number : number + 1], distance, 1)
        totals.append(total)
    total = jnp.concatenate(totals + [jnp.zeros((5, cells), f32)], axis=0)
    site_total = exact(total[:, :inner_lanes], picks, nt)
    lines = jnp.concatenate([-(site_total[0:3] + long_force[0:3]), site_energy], axis=0)
    lines = jnp.concatenate([lines, jnp.zeros((4, slots), f32)], axis=0)
    hot = (iota((slots, slots), 0) == site_of(coords_of(pos_ref))).astype(f32).astype(bf16)
    lines = exact(lines, hot)
    for axis in range(3):
        force_out[0, 0, axis] = lines[axis : axis + 1]
    energy_out[0, 0] = lines[3:4]


def kernel_params():
    return pltpu.CompilerParams(vmem_limit_bytes=56 * 1024 * 1024)


def whole_box(
    species,
    counts,
    positions,
    ghost_rows,
    neighbours,
    kvec,
    embed,
    radial_one,
    radial_two,
    mix_one,
    mix_two,
    lr_filter,
    read_weight,
    read_bias,
    energy_weight,
):
    axes = ("gx", "gy", "gz")
    vmem = pl.BlockSpec(memory_space=pltpu.VMEM)
    smem = pl.BlockSpec(memory_space=pltpu.SMEM)
    placed = pl.pallas_call(
        place_kernel,
        out_shape=jax.ShapeDtypeStruct((domains, 4, slots), f32),
        in_specs=[smem, vmem, vmem],
        out_specs=vmem,
    )(counts, positions.transpose(0, 1, 3, 2, 4), species)
    shared = lax.all_to_all(placed, axes, 0, 0, tiled=True)
    gain = pl.pallas_call(
        gain_kernel,
        out_shape=jax.ShapeDtypeStruct((chan, table), f32),
        in_specs=[vmem] * 2,
        out_specs=vmem,
    )(kvec, lr_filter)
    tables = (
        gain,
        embed,
        radial_one,
        radial_two,
        mix_one,
        mix_two,
        read_weight,
        read_bias.reshape(1, chan),
        energy_weight.reshape(1, chan),
    )
    energies, forces = box_call(shared, positions.transpose(0, 1, 3, 2, 4), tables)
    return (energies, forces.transpose(0, 1, 3, 2, 4))


def box_call(shared, coords, tables):
    vmem = pl.BlockSpec(memory_space=pltpu.VMEM)
    grid_shape = (ext, ext, ext, planes, 128)
    return pl.pallas_call(
        box_kernel,
        out_shape=(
            jax.ShapeDtypeStruct((1, 1, 1, slots), f32),
            jax.ShapeDtypeStruct((1, 1, 3, 1, slots), f32),
        ),
        in_specs=[vmem] * 11,
        out_specs=(vmem, vmem),
        scratch_shapes=[
            pltpu.VMEM((cells // 128, 64 * 16, 128), f32),
            pltpu.VMEM((64, pad), f32),
            pltpu.VMEM((2, rows_all, 128), f32),
            pltpu.VMEM((half, rows_all, pad), bf16),
            pltpu.VMEM((table, 2 * span), bf16),
            pltpu.VMEM((table, cells), bf16),
            pltpu.VMEM(grid_shape, f32),
            pltpu.VMEM(grid_shape, f32),
            pltpu.VMEM(grid_shape, f32),
            pltpu.VMEM((rows_all, 128), f32),
            pltpu.VMEM((2, pad, 128), f32),
            pltpu.VMEM((8, 2 * span), f32),
            pltpu.VMEM((rows_all, pad), bf16),
            pltpu.VMEM((2, cells, chan), f32),
            pltpu.VMEM((pad, pad), f32),
            pltpu.VMEM((3, cells + reach, 256), f32),
            pltpu.VMEM((chan, 2 * span), bf16),
            pltpu.VMEM((chan, table), f32),
        ],
        compiler_params=kernel_params(),
    )(shared, coords, *tables)


def solution(mesh):
    in_specs = (
        P(("group", "gx"), "gy", "gz", None),
        P(("group", "gx"), "gy", "gz"),
        P(("group", "gx"), "gy", "gz", None, None),
        P(("group", "gx"), "gy", "gz", None),
        P(("group", "gx"), "gy", "gz", None, None),
        P(),
        P(),
        P(),
        P(),
        P(),
        P(),
        P(),
        P(),
        P(),
        P(),
    )
    out_specs = (P(("group", "gx"), "gy", "gz", None), P(("group", "gx"), "gy", "gz", None, None))
    sizes = tuple(mesh.shape[axis] for axis in ("gx", "gy", "gz"))
    plan = whole_box if sizes == grid_dims else local
    return jax.shard_map(plan, mesh=mesh, in_specs=in_specs, out_specs=out_specs, check_vma=False)
```

```python
import math

import jax
import jax.numpy as jnp
import numpy as np
from jax import lax
from jax.experimental import pallas as pl
from jax.experimental.pallas import tpu as pltpu
from jax.sharding import PartitionSpec as P

SIDE = 6
KVEC = 4096
NBASIS = 8
NEIGH = 26


spacing = 2.5
cutoff = 5.0
two_pi = 6.283185307179586
highest = lax.Precision.HIGHEST


def passed_along(block, axis, distance):
    devices = range(lax.axis_size(axis))
    route = [((i - distance) % len(devices), i) for i in devices]
    return lax.ppermute(block, axis, route)


def extended(block, sides, width):
    for axis, dim in sides:
        count = lax.axis_size(axis)
        forward = [(i, i + 1) for i in range(count - 1)]
        forward.append((count - 1, 0))
        backward = [(target, source) for source, target in forward]
        low = lax.ppermute(
            lax.slice_in_dim(block, block.shape[dim] - width, None, axis=dim), axis, forward
        )
        high = lax.ppermute(lax.slice_in_dim(block, 0, width, axis=dim), axis, backward)
        block = jnp.concatenate([low, block, high], axis=dim)
    return block


def rows_per_block():
    return SIDE * SIDE


def boundary_list(side):
    site_ids = np.arange(side**3).reshape(side, side, side)
    inner = np.zeros((side, side, side), dtype=bool)
    inner[1 : side - 1, 1 : side - 1, 1 : side - 1] = True
    return site_ids[~inner].astype(np.int32)


def radial_terms(distance):
    centres = cutoff * jnp.arange(NBASIS).astype(jnp.float32) / (NBASIS - 1)
    sharpness = (NBASIS / cutoff) ** 2
    gap_value = distance[None] - centres[:, None, None]
    gaussian = jnp.exp(-sharpness * gap_value * gap_value)
    envelope_base = jnp.maximum(1.0 - distance * distance / (cutoff * cutoff), 0.0)
    envelope = envelope_base * envelope_base
    envelope_slope = -4.0 * distance * envelope_base / (cutoff * cutoff)
    radial_value = gaussian * envelope[None]
    radial_slope = gaussian * (envelope_slope[None] - 2.0 * sharpness * gap_value * envelope[None])
    return (radial_value, radial_slope)


def embed_codes(type_code, embed):
    species_ids = jnp.arange(1, embed.shape[0] + 1, dtype=jnp.int32).astype(type_code.dtype)
    one_hot = (type_code[None, :] == species_ids[:, None]).astype(jnp.float32)
    return jnp.dot(embed.T, one_hot, precision=highest, preferred_element_type=jnp.float32)


def cell_shift():
    ext_side = SIDE + 2
    cells = jnp.arange(ext_side**3, dtype=jnp.int32)
    coords = jnp.stack(
        [cells // (ext_side * ext_side), cells // ext_side % ext_side, cells % ext_side]
    )
    domain_width = SIDE * spacing
    return jnp.where(
        coords == 0, -domain_width, jnp.where(coords == ext_side - 1, domain_width, 0.0)
    ).astype(jnp.float32)


def pair_geometry(coords_own, pool_coords, pair_lists):
    separation = jnp.take(pool_coords, pair_lists, axis=1) - coords_own[:, None, :]
    distance = jnp.sqrt(jnp.sum(separation * separation, axis=0))
    return (separation, distance)


def message_forward(pool_values, pair_lists, radial_value, radial_weight):
    radial_filter = jnp.einsum("bc,bma->cma", radial_weight, radial_value, precision=highest)
    neighbour_value = jnp.take(pool_values, pair_lists, axis=1)
    return jnp.sum(radial_filter * neighbour_value, axis=1)


def message_backward(
    grad_message,
    pool_values,
    pair_lists,
    radial_value,
    radial_slope,
    radial_weight,
    separation,
    distance,
    pool_size,
    with_features,
):
    neighbour_value = jnp.take(pool_values, pair_lists, axis=1)
    contracted = jnp.einsum(
        "bc,cma->bma", radial_weight, grad_message[:, None, :] * neighbour_value, precision=highest
    )
    energy_slope = jnp.sum(radial_slope * contracted, axis=0)
    pair_force = separation * (energy_slope / distance)[None]
    flat_index = pair_lists.reshape(-1)
    grad_pool = (
        jnp.zeros((3, pool_size), jnp.float32).at[:, flat_index].add(pair_force.reshape(3, -1))
    )
    grad_own = -jnp.sum(pair_force, axis=1)
    if with_features:
        radial_filter = jnp.einsum("bc,bma->cma", radial_weight, radial_value, precision=highest)
        spread = (radial_filter * grad_message[:, None, :]).reshape(radial_filter.shape[0], -1)
        feature_pool = (
            jnp.zeros((radial_filter.shape[0], pool_size), jnp.float32)
            .at[:, flat_index]
            .add(spread)
        )
        return (grad_pool, grad_own, feature_pool)
    return (grad_pool, grad_own, grad_pool)


def phase_table(fraction, wave_numbers):
    phase_angle = two_pi * (
        fraction[0][:, None] * wave_numbers[0][None, :]
        + fraction[1][:, None] * wave_numbers[1][None, :]
        + fraction[2][:, None] * wave_numbers[2][None, :]
    )
    return (jnp.cos(phase_angle).astype(jnp.bfloat16), jnp.sin(phase_angle).astype(jnp.bfloat16))


def read_long(cosine_low, sine_low, filtered):
    dims = (((1,), (1,)), ((), ()))
    return lax.dot_general(
        filtered[0], cosine_low, dims, preferred_element_type=jnp.float32
    ) + lax.dot_general(filtered[1], sine_low, dims, preferred_element_type=jnp.float32)


def block_live(step_index, live_count):
    block_rows = rows_per_block()
    per_member = SIDE**3 // block_rows
    first_row = (step_index % per_member * block_rows).astype(jnp.float32)
    return first_row < live_count[step_index // per_member]


def lr_struct(fraction, row_values, live_count, wave_numbers):
    block_rows = rows_per_block()
    blocks = fraction.shape[1] // block_rows

    def step(step_index, running):

        def work(running):
            offset = step_index * block_rows
            frac_block = lax.dynamic_slice_in_dim(fraction, offset, block_rows, 1)
            feature_block = lax.dynamic_slice_in_dim(row_values, offset, block_rows, 1)
            cosine_low, sine_low = phase_table(frac_block, wave_numbers)
            term = jnp.stack(
                [
                    jnp.dot(feature_block, cosine_low, preferred_element_type=jnp.float32),
                    jnp.dot(feature_block, sine_low, preferred_element_type=jnp.float32),
                ]
            )
            return running + term

        return lax.cond(
            block_live(step_index, live_count), work, lambda unchanged: unchanged, running
        )

    initial = jnp.zeros((2, row_values.shape[0], wave_numbers.shape[1]), jnp.float32)
    return lax.fori_loop(0, blocks, step, initial)


def lr_read(fraction, live_count, wave_numbers, filtered):
    block_rows = rows_per_block()
    blocks = fraction.shape[1] // block_rows

    def step(step_index, result):

        def work(result):
            offset = step_index * block_rows
            cosine_low, sine_low = phase_table(
                lax.dynamic_slice_in_dim(fraction, offset, block_rows, 1), wave_numbers
            )
            return lax.dynamic_update_slice_in_dim(
                result, read_long(cosine_low, sine_low, filtered), offset, 1
            )

        return lax.cond(
            block_live(step_index, live_count), work, lambda unchanged: unchanged, result
        )

    initial = jnp.zeros((filtered.shape[1], fraction.shape[1]), jnp.float32)
    return lax.fori_loop(0, blocks, step, initial)


def lr_back(
    fraction,
    rounded_rows,
    grad_rows,
    occupied_rows,
    live_count,
    wave_numbers,
    wave_factors,
    filtered,
    back_filtered,
):
    block_rows = rows_per_block()
    blocks = fraction.shape[1] // block_rows
    dims = (((0,), (0,)), ((), ()))
    right_real = jnp.concatenate([filtered[0], back_filtered[0]], axis=0)
    right_imag = jnp.concatenate([filtered[1], back_filtered[1]], axis=0)

    def step(step_index, carried):

        def work(carried):
            grad_long, force_long = carried
            offset = step_index * block_rows
            cosine_low, sine_low = phase_table(
                lax.dynamic_slice_in_dim(fraction, offset, block_rows, 1), wave_numbers
            )
            mask_block = lax.dynamic_slice_in_dim(occupied_rows, offset, block_rows, 0)
            grad_block = mask_block[None] * read_long(cosine_low, sine_low, back_filtered)
            stacked_left = jnp.concatenate(
                [
                    lax.dynamic_slice_in_dim(grad_rows, offset, block_rows, 1),
                    lax.dynamic_slice_in_dim(rounded_rows, offset, block_rows, 1),
                ],
                axis=0,
            )
            real_part = lax.dot_general(
                stacked_left, right_real, dims, preferred_element_type=jnp.float32
            )
            imag_part = lax.dot_general(
                stacked_left, right_imag, dims, preferred_element_type=jnp.float32
            )
            turning = (
                cosine_low.astype(jnp.float32) * imag_part
                - sine_low.astype(jnp.float32) * real_part
            )
            force_block = lax.dot_general(
                wave_factors,
                turning,
                (((1,), (1,)), ((), ())),
                precision=highest,
                preferred_element_type=jnp.float32,
            )
            return (
                lax.dynamic_update_slice_in_dim(grad_long, grad_block, offset, 1),
                lax.dynamic_update_slice_in_dim(force_long, force_block, offset, 1),
            )

        return lax.cond(
            block_live(step_index, live_count), work, lambda unchanged: unchanged, carried
        )

    initial = (
        jnp.zeros((rounded_rows.shape[0], fraction.shape[1]), jnp.float32),
        jnp.zeros((3, fraction.shape[1]), jnp.float32),
    )
    return lax.fori_loop(0, blocks, step, initial)


def boundary_grid(values, ghost_slots, boundary):
    picked = jnp.take(values, ghost_slots, axis=1)
    site_grid = jnp.zeros((values.shape[0], SIDE**3), values.dtype).at[:, boundary].set(picked)
    return site_grid.reshape(values.shape[0], SIDE, SIDE, SIDE)


def fold_slab(site_grid, axis_number, from_left, from_right):
    inner_size = site_grid.shape[axis_number] - 2
    inner = lax.slice_in_dim(site_grid, 1, inner_size + 1, axis=axis_number)
    first_layer = lax.slice_in_dim(inner, 0, 1, axis=axis_number) + from_left
    last_layer = lax.slice_in_dim(inner, inner_size - 1, inner_size, axis=axis_number) + from_right
    middle = lax.slice_in_dim(inner, 1, inner_size - 1, axis=axis_number)
    return jnp.concatenate([first_layer, middle, last_layer], axis=axis_number)


def return_halo(site_grid):
    edge = site_grid.shape[3] - 1
    received = [
        passed_along(
            lax.slice_in_dim(site_grid, slab_start, slab_start + 1, axis=3), "gz", direction
        )
        for direction, slab_start in ((1, edge), (-1, 0))
    ]
    site_grid = fold_slab(site_grid, 3, received[0], received[1])
    edge = site_grid.shape[2] - 1
    received = [
        passed_along(
            lax.slice_in_dim(site_grid, slab_start, slab_start + 1, axis=2), "gy", direction
        )
        for direction, slab_start in ((1, edge), (-1, 0))
    ]
    site_grid = fold_slab(site_grid, 2, received[0], received[1])
    edge = site_grid.shape[1] - 1
    received = [
        passed_along(
            lax.slice_in_dim(site_grid, slab_start, slab_start + 1, axis=1), "gx", direction
        )
        for direction, slab_start in ((1, edge), (-1, 0))
    ]
    return fold_slab(site_grid, 1, received[0], received[1])


def ghost_to_rows(site_grid, ghost_slots, boundary):
    features = site_grid.shape[0]
    picked = site_grid.reshape(features, -1)[:, boundary]
    return jnp.zeros((features, SIDE**3), site_grid.dtype).at[:, ghost_slots].add(picked)


def local(
    species,
    counts,
    positions,
    ghost_rows,
    neighbours,
    kvec,
    embed,
    radial_one,
    radial_two,
    mix_one,
    mix_two,
    lr_filter,
    read_weight,
    read_bias,
    energy_weight,
):
    slot_count = SIDE**3
    ext_side = SIDE + 2
    pool_size = slot_count + ext_side**3
    pair_scale = 1.0 / math.sqrt(NEIGH)
    domain_width = SIDE * spacing
    mesh_sizes = (lax.axis_size("gx"), lax.axis_size("gy"), lax.axis_size("gz"))
    box_length = tuple((count_along * domain_width for count_along in mesh_sizes))
    wave_scale = 1.0 / math.sqrt(
        KVEC * (slot_count * mesh_sizes[0] * mesh_sizes[1] * mesh_sizes[2])
    )
    species_flat = species.reshape(slot_count)
    live_total = counts.reshape(())
    coords_own = positions.reshape(3, slot_count)
    ghost_slots = ghost_rows.reshape(-1)
    pair_lists = neighbours.reshape(NEIGH, slot_count)
    boundary = jnp.asarray(boundary_list(SIDE))
    cell_offset = cell_shift()
    occupied = (jnp.arange(slot_count, dtype=jnp.int32) < live_total).astype(jnp.float32)
    type_code = jnp.where(occupied > 0, species_flat + 1, 0).astype(jnp.float32)
    hidden_zero = embed_codes(species_flat + 1, embed)
    masked_zero = hidden_zero * occupied[None]
    packet = boundary_grid(
        jnp.concatenate([coords_own, type_code[None]], axis=0), ghost_slots, boundary
    )
    ext_atoms = extended(packet, (("gx", 1), ("gy", 2), ("gz", 3)), 1).reshape(4, -1)
    pool_coords = jnp.concatenate([coords_own, ext_atoms[:3] + cell_offset], axis=1)
    pool_zero = jnp.concatenate([masked_zero, embed_codes(ext_atoms[3], embed)], axis=1)
    separation, distance = pair_geometry(coords_own, pool_coords, pair_lists)
    radial_value, radial_slope = radial_terms(distance)
    message = message_forward(pool_zero, pair_lists, radial_value, radial_one)
    hidden_one = hidden_zero + pair_scale * jnp.dot(
        mix_one.T, message, precision=highest, preferred_element_type=jnp.float32
    )
    masked_one = hidden_one * occupied[None]
    rounded_one = masked_one.astype(jnp.bfloat16)
    domain_pos = (lax.axis_index("gx"), lax.axis_index("gy"), lax.axis_index("gz"))
    fraction = jnp.stack(
        [
            (domain_pos[axis_id].astype(jnp.float32) * domain_width + coords_own[axis_id])
            / box_length[axis_id]
            for axis_id in range(3)
        ]
    )
    wave_numbers = kvec.astype(jnp.float32)
    wave_factors = jnp.stack(
        [two_pi * wave_numbers[axis_id] / box_length[axis_id] for axis_id in range(3)]
    )
    own_count = jnp.sum(occupied)[None]
    share_size = KVEC // (mesh_sizes[0] * mesh_sizes[1] * mesh_sizes[2])
    share_start = lax.axis_index(("gx", "gy", "gz")) * share_size
    filter_share = lax.dynamic_slice_in_dim(lr_filter, share_start, share_size, 1)
    struct_part = lax.psum_scatter(
        lr_struct(fraction, rounded_one, own_count, wave_numbers),
        ("gx", "gy", "gz"),
        scatter_dimension=2,
        tiled=True,
    )
    filtered = lax.all_gather(
        (struct_part * filter_share[None] * wave_scale).astype(jnp.bfloat16),
        ("gx", "gy", "gz"),
        axis=2,
        tiled=True,
    )
    long_part = lr_read(fraction, own_count, wave_numbers, filtered)
    masked_ext = extended(
        boundary_grid(masked_one, ghost_slots, boundary).astype(jnp.bfloat16),
        (("gx", 1), ("gy", 2), ("gz", 3)),
        1,
    ).astype(jnp.float32)
    pool_one = jnp.concatenate([masked_one, masked_ext.reshape(masked_one.shape[0], -1)], axis=1)
    message_two = message_forward(pool_one, pair_lists, radial_value, radial_two)
    hidden_two = (
        hidden_one
        + pair_scale
        * jnp.dot(mix_two.T, message_two, precision=highest, preferred_element_type=jnp.float32)
        + long_part
    )
    activation = (
        jnp.dot(read_weight.T, hidden_two, precision=highest, preferred_element_type=jnp.float32)
        + read_bias[:, None]
    )
    gating = jax.nn.sigmoid(activation)
    energies = occupied * jnp.sum(activation * gating * energy_weight[:, None], axis=0)
    grad_act = (
        occupied[None] * energy_weight[:, None] * gating * (1.0 + activation * (1.0 - gating))
    )
    grad_two = jnp.dot(read_weight, grad_act, precision=highest, preferred_element_type=jnp.float32)
    grad_low = grad_two.astype(jnp.bfloat16)
    grad_part = lax.psum_scatter(
        lr_struct(fraction, grad_low, own_count, wave_numbers),
        ("gx", "gy", "gz"),
        scatter_dimension=2,
        tiled=True,
    )
    back_filtered = lax.all_gather(
        (grad_part * filter_share[None] * wave_scale).astype(jnp.bfloat16),
        ("gx", "gy", "gz"),
        axis=2,
        tiled=True,
    )
    grad_long, force_long = lr_back(
        fraction,
        rounded_one,
        grad_low,
        occupied,
        own_count,
        wave_numbers,
        wave_factors,
        filtered,
        back_filtered,
    )
    grad_message = pair_scale * jnp.dot(
        mix_two, grad_two, precision=highest, preferred_element_type=jnp.float32
    )
    grad_pool, grad_own_two, feature_pool = message_backward(
        grad_message,
        pool_one,
        pair_lists,
        radial_value,
        radial_slope,
        radial_two,
        separation,
        distance,
        pool_size,
        True,
    )
    combined = jnp.concatenate([feature_pool, grad_pool], axis=0)
    features = combined.shape[0]
    returned_two = ghost_to_rows(
        return_halo(combined[:, slot_count:].reshape(features, ext_side, ext_side, ext_side)),
        ghost_slots,
        boundary,
    )
    own_two = combined[:, :slot_count]
    channels = masked_one.shape[0]
    grad_one = (
        grad_two + grad_long + occupied[None] * (own_two[:channels] + returned_two[:channels])
    )
    grad_message_one = pair_scale * jnp.dot(
        mix_one, grad_one, precision=highest, preferred_element_type=jnp.float32
    )
    grad_pool_one, grad_own_one, unused = message_backward(
        grad_message_one,
        pool_zero,
        pair_lists,
        radial_value,
        radial_slope,
        radial_one,
        separation,
        distance,
        pool_size,
        False,
    )
    layer_one_grad = grad_own_one + grad_pool_one[:, :slot_count]
    returned_one = ghost_to_rows(
        return_halo(grad_pool_one[:, slot_count:].reshape(3, ext_side, ext_side, ext_side)),
        ghost_slots,
        boundary,
    )
    total_grad = (
        layer_one_grad
        + returned_one
        + force_long
        + grad_own_two
        + own_two[channels:]
        + returned_two[channels:]
    )
    forces = -total_grad
    return (energies.reshape(1, 1, 1, slot_count), forces.reshape(1, 1, 1, 3, slot_count))


offsets = tuple(
    (ox, oy, oz)
    for ox in (0, 1)
    for oy in (-1, 0, 1)
    for oz in (-1, 0, 1)
    if (ox, oy, oz) > (0, 0, 0)
)
half = len(offsets)
slots = SIDE**3
ext = SIDE + 2
cells = ext**3
inner_lanes = SIDE * ext * ext
reach = ext * ext + 2 * ext
chan = 64
grid_dims = (4, 2, 2)
domains = 16
planes = 8
rows_all = slots * planes
waves = 648
table = 2 * waves
pad = 256
span = -(-rows_all // 128) * 128
gamma = (NBASIS / cutoff) ** 2
step = cutoff / (NBASIS - 1)
nt = (((1,), (1,)), ((), ()))
nn = (((1,), (0,)), ((), ()))
f32 = jnp.float32
bf16 = jnp.bfloat16


def dot(left, right, dims=nn, precision=None):
    return lax.dot_general(left, right, dims, precision=precision, preferred_element_type=f32)


def split(value):
    high = value.astype(bf16)
    return high, (value - high.astype(f32)).astype(bf16)


def dot_split(left, high, low):
    left_high, left_low = split(left)
    return dot(left_high, high) + dot(left_low, high) + dot(left_high, low)


def exact(left, hot, dims=nn):
    high = left.astype(bf16).astype(f32)
    rest = left - high
    middle = rest.astype(bf16).astype(f32)
    count = left.shape[0]
    stacked = jnp.concatenate([high, middle, rest - middle], axis=0).astype(bf16)
    parts = dot(stacked, hot, dims)
    return parts[:count] + parts[count : 2 * count] + parts[2 * count :]


def coords_of(ref):
    return jnp.concatenate([ref[0, 0, axis] for axis in range(3)], axis=0)


def site_of(coords):
    where = (coords * (1.0 / spacing)).astype(jnp.int32)
    return (where[0:1] * SIDE + where[1:2]) * SIDE + where[2:3]


def iota(shape, dim):
    return lax.broadcasted_iota(jnp.int32, shape, dim)


def place_kernel(count_ref, pos_ref, species_ref, out_ref):
    coords = coords_of(pos_ref)
    live = iota((1, slots), 1) < count_ref[0, 0, 0]
    code = jnp.where(live, species_ref[0, 0] + 1, 0).astype(f32)
    data = jnp.concatenate([coords, code, jnp.zeros((4, slots), f32)], axis=0)
    hot = (iota((slots, slots), 0) == site_of(coords)).astype(f32).astype(bf16)
    placed = exact(data, hot, nt)[0:4]
    for number in range(domains):
        out_ref[number] = placed


def twice(block):
    zero = jnp.zeros_like(block)
    return jnp.concatenate(
        [jnp.concatenate([block, zero], axis=1), jnp.concatenate([zero, block], axis=1)], axis=0
    )


def gain_kernel(kvec_ref, filter_ref, gain_ref):
    wave_scale = 1.0 / math.sqrt(KVEC * slots * domains)
    waves_in = kvec_ref[...]

    def folded(row):
        return jnp.where(row > 0, 2 * row - 1, -2 * row)

    index = (folded(waves_in[1:2]) * 9 + folded(waves_in[2:3])) * 8 + waves_in[0:1] - 1
    filter_high, filter_low = split(filter_ref[...] * wave_scale)
    parts = jnp.concatenate([filter_high, filter_low], axis=0)
    gain = jnp.zeros((waves, 2 * chan), f32)
    width = 1024
    for start in range(0, KVEC, width):
        hot = (iota((waves, width), 0) == index[:, start : start + width]).astype(f32).astype(bf16)
        gain = gain + dot(hot, parts[:, start : start + width], nt)
    gain = (gain[:, :chan] + gain[:, chan:]).reshape(waves // 8, 8, chan)
    gain_ref[...] = jnp.concatenate([gain, gain], axis=1).reshape(table, chan).T


def turn(fraction):
    rest = fraction - jnp.floor(fraction + 0.5)
    angle = rest * (0.5 * two_pi)
    square = angle * angle
    sine = angle * (
        1.0
        + square
        * (
            -1.0 / 6
            + square
            * (
                1.0 / 120
                + square * (-1.0 / 5040 + square * (1.0 / 362880 - square * (1.0 / 39916800)))
            )
        )
    )
    cosine = 1.0 + square * (
        -0.5
        + square
        * (
            1.0 / 24
            + square
            * (
                -1.0 / 720
                + square
                * (1.0 / 40320 + square * (-1.0 / 3628800 + square * (1.0 / 479001600)))
            )
        )
    )
    return 1.0 - 2.0 * sine * sine, 2.0 * sine * cosine


def fan(base, step_pairs):
    real, imag = base
    out = [(real, imag)]
    for cosine, sine in step_pairs:
        a, b, c, d = real * cosine, imag * sine, real * sine, imag * cosine
        out.append((a - b, c + d))
        out.append((a + b, d - c))
    return out


def wave_tile(coords, store):
    frac = [coords[axis] / (grid_dims[axis] * SIDE * spacing) for axis in range(3)]
    row = iota((8, 128), 0)
    base = turn(frac[0] * (row + 1).astype(f32))
    rest = turn(jnp.where(row < 4, frac[1], frac[2]) * (row % 4 + 1).astype(f32))

    def line(index):
        return tuple(jnp.broadcast_to(part[index : index + 1], (8, 128)) for part in rest)

    y_lines = [line(index) for index in range(4)]
    z_lines = [line(index + 4) for index in range(4)]
    index = 0
    for level in fan(base, y_lines):
        for real, imag in fan(level, z_lines):
            store(index, jnp.concatenate([real, imag], axis=0).astype(bf16))
            index += 1
        yield index


def swap_lanes(value):
    return pltpu.roll(value, chan, value.ndim - 1)


def swap_planes(value):
    up = pltpu.roll(value, 1, 1)
    down = pltpu.roll(value, planes - 1, 1)
    return jnp.where(iota(value.shape, 1) % 2 == 0, down, up)


def as_three(value):
    return value.reshape((-1,) + value.shape[-2:])


def fill_ghosts(ref):
    inner = slice(1, SIDE + 1)
    for ghost, source, shift in ((0, SIDE, 2), (SIDE + 1, 1, planes - 2)):
        value = ref[source, inner, inner]
        ref[ghost, inner, inner] = pltpu.roll(as_three(value), shift, 1).reshape(value.shape)
    for ghost, source in ((0, SIDE), (SIDE + 1, 1)):
        value = ref[:, source, inner]
        ref[:, ghost, inner] = swap_planes(as_three(value)).reshape(value.shape)
    for ghost, source in ((0, SIDE), (SIDE + 1, 1)):
        value = ref[:, :, source]
        ref[:, :, ghost] = swap_lanes(as_three(value)).reshape(value.shape)


def fold_ghosts(ref):
    inner = slice(1, SIDE + 1)
    for ghost, target in ((SIDE + 1, 1), (0, SIDE)):
        value = ref[:, :, ghost]
        ref[:, :, target] = ref[:, :, target] + swap_lanes(as_three(value)).reshape(value.shape)
    for ghost, target in ((SIDE + 1, 1), (0, SIDE)):
        value = ref[:, ghost, inner]
        ref[:, target, inner] = ref[:, target, inner] + swap_planes(as_three(value)).reshape(
            value.shape
        )
    for ghost, target, shift in ((SIDE + 1, 1, 2), (0, SIDE, planes - 2)):
        value = ref[ghost, inner, inner]
        ref[target, inner, inner] = ref[target, inner, inner] + pltpu.roll(
            as_three(value), shift, 1
        ).reshape(value.shape)


def inner_rows(ref, level):
    inner = slice(1, SIDE + 1)
    return ref[level + 1, inner, inner].reshape(rows_all // SIDE, 128)


def set_level(ref, level, value):
    inner = slice(1, SIDE + 1)
    ref[level + 1, inner, inner] = value.reshape(SIDE, SIDE, planes, 128)


def level_rows(level):
    return slice(level * (rows_all // SIDE), (level + 1) * (rows_all // SIDE))


def set_inner(ref, value):
    inner = slice(1, SIDE + 1)
    ref[inner, inner, inner] = value.reshape(SIDE, SIDE, SIDE, planes, 128)


def convolve(filters, layer, source, target, beside=None):
    target[...] = jnp.zeros(target.shape, f32)
    lanes = slice(layer * 128, layer * 128 + 128)
    groups = {}
    for number, (ox, oy, oz) in enumerate(offsets):
        groups.setdefault((ox, oy), []).append((number, oz))

    def one_line(line):
        x = line // SIDE
        y = line % SIDE
        own = [source[x + 1, y + 1, z + 1] for z in range(SIDE)]
        own_sum = [jnp.zeros((planes, 128), f32)] * SIDE
        for (ox, oy), members in groups.items():
            there = [source[x + 1 + ox, y + 1 + oy, z] for z in range(ext)]
            sums = [None] * ext
            first = pl.multiple_of(line * (SIDE * planes), SIDE * planes)
            weights = [
                filters[number, pl.ds(first, SIDE * planes), lanes].astype(f32)
                for number, _ in members
            ]
            for z in range(SIDE):
                for block, (_, oz) in zip(weights, members):
                    weight = block[z * planes : z * planes + planes]
                    own_sum[z] = own_sum[z] + weight * there[z + 1 + oz]
                    term = weight * own[z]
                    spot = z + 1 + oz
                    sums[spot] = term if sums[spot] is None else sums[spot] + term
            for z in range(ext):
                if sums[z] is not None:
                    target[x + 1 + ox, y + 1 + oy, z] = target[x + 1 + ox, y + 1 + oy, z] + sums[z]
        for z in range(SIDE):
            target[x + 1, y + 1, z + 1] = target[x + 1, y + 1, z + 1] + own_sum[z]

    def body(number, carry):
        for part in range(6):
            one_line(number * 6 + part)
            if beside is not None and part % 3 == 0:
                beside(number * 2 + part // 3)
        return carry

    lax.fori_loop(0, SIDE * SIDE // 6, body, 0)
    fold_ghosts(target)


def spread(block):
    return jnp.broadcast_to(block[:, None, :], (NBASIS, 16, chan)).reshape(128, chan)


def wide(left, right):
    left, right = spread(left), spread(right)
    line = jnp.concatenate([left, left, right, right], axis=1)
    return jnp.concatenate([line, line], axis=0)


def doubled(ref):
    return jnp.concatenate([ref[...], ref[...]], axis=1)


def box_kernel(
    all_ref,
    pos_ref,
    gain_ref,
    embed_ref,
    radial_one_ref,
    radial_two_ref,
    mix_one_ref,
    mix_two_ref,
    read_ref,
    bias_ref,
    energy_ref,
    energy_out,
    force_out,
    sep_ref,
    sites_ref,
    basis_ref,
    filters_ref,
    waves_ref,
    ring_ref,
    zero_ref,
    one_ref,
    sum_ref,
    packed_ref,
    own_ref,
    flat_ref,
    low_ref,
    saved_ref,
    radial_ref,
    shift_ref,
    turned_ref,
    parts_ref,
):
    home = [lax.axis_index(axis) for axis in ("gx", "gy", "gz")]
    pair_scale = 1.0 / math.sqrt(NEIGH)
    fall = jnp.exp(-gamma * jnp.square(step * iota((NBASIS, 1), 0).astype(f32)))
    rows = iota((pad, pad), 0)
    columns = iota((pad, pad), 1)
    kept = (rows // 128) == (columns % 128 // chan)
    radial_ref[...] = jnp.where(
        kept, wide(radial_one_ref[...] * fall, radial_two_ref[...] * fall), 0.0
    )
    table_rows = jnp.concatenate([embed_ref[...], jnp.zeros((2, chan), f32)], axis=0)
    table_high = table_rows.astype(bf16).astype(f32)
    species_rows = kept & (rows % 16 == half)
    embeds = jnp.where(species_rows, wide(table_high, table_rows - table_high), 0.0).astype(bf16)
    lives = jnp.where(species_rows[:, :128], 1.0, 0.0).astype(bf16)
    sites_ref[...] = jnp.zeros((4 * domains, pad), f32)
    flat_ref[...] = jnp.zeros(flat_ref.shape, f32)
    domain_width = SIDE * spacing
    offset_row = iota((4, slots), 0)
    for number in range(domains):
        spot = [
            lax.rem(home[axis] + part, grid_dims[axis])
            for axis, part in enumerate((number // 4, number // 2 % 2, number % 2))
        ]
        block = all_ref[(spot[0] * 2 + spot[1]) * 2 + spot[2]]
        sites_ref[number * 4 : number * 4 + 4, 0:slots] = block
        shifts = [part * domain_width for part in (number // 4, number // 2 % 2, number % 2)]
        moved = jnp.where(
            offset_row == 0, shifts[0], jnp.where(offset_row == 1, shifts[1], shifts[2])
        )
        start = number % 2 * span + number // 2 * slots
        flat_ref[0:4, start : start + slots] = block + moved
    sites = sites_ref[:, 0:slots]

    lane = iota((1, cells), 1)
    coords = [(lane // (ext * ext) + 1) % ext, lane // ext % ext, lane % ext]
    wrapped = [(value + SIDE - 1) % SIDE for value in coords]
    wrapped_site = (wrapped[0] * SIDE + wrapped[1]) * SIDE + wrapped[2]
    inside = coords[0] >= 0
    for value in coords:
        inside = inside & (value > 0) & (value < ext - 1)
    hot_all = iota((slots, cells), 0) == wrapped_site
    grown = exact(sites, hot_all.astype(f32).astype(bf16))
    picks = (hot_all & inside)[:, :inner_lanes].astype(f32).astype(bf16)

    back16 = jnp.concatenate([grown[48:], grown[:48]], axis=0)
    ahead16 = jnp.concatenate([grown[16:], grown[:16]], axis=0)
    grown = jnp.where(coords[0] == 0, back16, jnp.where(coords[0] == ext - 1, ahead16, grown))
    swapped = jnp.concatenate(
        [grown[8 * (part ^ 1) : 8 * (part ^ 1) + 8] for part in range(8)], axis=0
    )
    grown = jnp.where((coords[1] == 0) | (coords[1] == ext - 1), swapped, grown)
    swapped = pltpu.roll(grown.reshape(8, 8, cells), 4, 1).reshape(64, cells)
    grown = jnp.where((coords[2] == 0) | (coords[2] == ext - 1), swapped, grown)
    component = iota((64, cells), 0) % 4
    for axis in range(3):
        moved = jnp.where(
            coords[axis] == 0,
            -domain_width,
            jnp.where(coords[axis] == ext - 1, domain_width, 0.0),
        )
        grown = grown + jnp.where(component == axis, moved, 0.0)
    own_ext = grown[0:4]
    tiles = cells // 128

    def put_sep(number, value):
        for tile in range(tiles):
            sep_ref[tile, pl.ds(number, 64, stride=16), :] = value[:, tile * 128 : tile * 128 + 128]

    def get_sep(window, count=tiles):
        return jnp.concatenate([sep_ref[tile, window, :] for tile in range(count)], axis=1)

    for number, (ox, oy, oz) in enumerate(offsets):
        distance = (ox * ext + oy) * ext + oz
        put_sep(number, pltpu.roll(grown, cells - distance, 1) - grown)
    for number in range(half, 16):
        put_sep(number, grown)

    basis_unroll = 8
    row16 = iota((16, inner_lanes), 0)

    def basis_of(domain):
        first = pl.multiple_of(domain * 64, 64)
        sx, sy, sz, codes = [get_sep(pl.ds(first + 16 * part, 16), inner_lanes // 128) for part in range(4)]
        square = sx * sx + sy * sy + sz * sz
        near = jnp.minimum(jnp.sqrt(square), cutoff)
        base = jnp.maximum(1.0 - square * (1.0 / (cutoff * cutoff)), 0.0)
        value = jnp.exp(-gamma * jnp.minimum(square, cutoff * cutoff)) * base * base
        ratio = jnp.exp((2.0 * gamma * step) * near)
        out = []
        for number in range(NBASIS):
            hit = jnp.where(codes == number + 1.0, 1.0, 0.0)
            out.append(jnp.where(row16 == half, hit, value))
            value = value * ratio
        return jnp.concatenate(out, axis=0).astype(bf16)

    def basis_step(plane, carry):
        both = jnp.concatenate([basis_of(2 * plane), basis_of(2 * plane + 1)], axis=0)
        picked = dot(picks, both, nt)
        for tile in range(2):
            basis_ref[tile, pl.ds(plane, slots, stride=planes), :] = picked[
                :, tile * 128 : tile * 128 + 128
            ]
        return carry

    def basis_group(number, carry):
        for part in range(basis_unroll):
            basis_step(number * basis_unroll + part, carry)
        return carry

    lax.fori_loop(0, planes // basis_unroll, basis_group, 0)

    basis_low = jnp.concatenate([basis_ref[0], basis_ref[1]], axis=1).astype(bf16)
    low_ref[...] = basis_low

    def flat_tile(start):
        block = flat_ref[:, pl.ds(start, 128)]

        def store(index, value):
            waves_ref[index * 16 : index * 16 + 16, pl.ds(start, 128)] = value

        return wave_tile([block[axis : axis + 1] for axis in range(3)], store)

    def wave_step(number, carry):
        chosen = jnp.where(iota((pad, pad), 0) % 16 == number, radial_ref[...], 0.0)
        chosen = chosen.astype(bf16)
        levels = []
        for part in range(2):
            levels.append(flat_tile(pl.multiple_of(number * 256 + part * 128, 128)))
        rows_each = rows_all // 3
        for part in range(3):
            window = slice(part * rows_each, part * rows_each + rows_each)
            filters_ref[number, window] = dot(low_ref[window], chosen).astype(bf16)
            for turn_number in range(6):
                next(levels[(part * 6 + turn_number) // 9])
        return carry

    lax.fori_loop(0, half, wave_step, 0)
    for tile in range(2 * half, 2 * span // 128):
        list(flat_tile(tile * 128))
    for tile in range(cells // 128):
        lanes = slice(tile * 128, tile * 128 + 128)

        def store(index, value):
            ring_ref[index * 16 : index * 16 + 16, lanes] = value

        list(wave_tile([own_ext[axis : axis + 1, lanes] for axis in range(3)], store))

    start_values = dot(low_ref[...], jnp.concatenate([embeds, lives], axis=1))
    rows_ref = basis_ref.at[0]
    live_ref = basis_ref.at[1]
    live_ref[...] = start_values[:, 256:384]
    set_inner(zero_ref, start_values[:, :128] + start_values[:, 128:256])
    fill_ghosts(zero_ref)
    convolve(filters_ref, 0, zero_ref, sum_ref)
    flat = (cells * planes, 128)
    own_cells = pl.ds(0, cells, stride=planes)

    def cells_of(ref):
        value = ref.reshape(flat)[own_cells, :]
        return jnp.concatenate([value[ext * ext :], value[: ext * ext]], axis=0)[:, :chan]

    saved_ref[0] = cells_of(zero_ref)
    mix_high, mix_low = split(twice(mix_one_ref[...] * pair_scale))
    for level in range(SIDE):
        window = level_rows(level)
        first_rows = inner_rows(zero_ref, level) + live_ref[window] * dot_split(
            inner_rows(sum_ref, level), mix_high, mix_low
        )
        set_level(one_ref, level, first_rows)
        rows_ref[window] = first_rows
    fill_ghosts(one_ref)
    saved_ref[1] = cells_of(one_ref)
    two_ref = zero_ref

    def start_structure():
        for plane in range(planes):
            packed_ref[plane * slots : plane * slots + slots] = rows_ref[
                pl.ds(plane, slots, stride=planes), :
            ]
        turned = packed_ref[...].T
        zeros = jnp.zeros((chan, span - rows_all), f32)
        turned = jnp.concatenate([turned[:chan], zeros, turned[chan:], zeros], axis=1)
        turned_ref[...] = turned.astype(bf16)
        tail = 12 * pad
        parts_ref[...] = dot(turned_ref[:, tail:], waves_ref[:, tail:], nt)

    def step_structure(number):
        start = pl.multiple_of(number * pad, pad)
        parts_ref[...] = parts_ref[...] + dot(
            turned_ref[:, pl.ds(start, pad)], waves_ref[:, pl.ds(start, pad)], nt
        )

    start_structure()
    own_ref[...] = jnp.zeros(own_ref.shape, f32)
    own_ref[0, 0:slots] = rows_ref[pl.ds(0, slots, stride=planes), :]
    convolve(filters_ref, 1, one_ref, sum_ref, step_structure)
    filtered = parts_ref[...] * gain_ref[...]
    long_rows = dot(filtered.astype(bf16), waves_ref[...]).T
    for plane in range(planes):
        first = long_rows[plane * slots : plane * slots + slots]
        second = long_rows[span + plane * slots : span + plane * slots + slots]
        rows_ref[pl.ds(plane, slots, stride=planes), :] = jnp.concatenate([first, second], axis=1)
    read = read_ref[...]
    both = dot_split(mix_two_ref[...] * pair_scale, *split(read))
    act_high, act_low = split(jnp.concatenate([twice(read), twice(both)], axis=0))
    grad_high, grad_low = split(jnp.concatenate([twice(read.T), twice(both.T)], axis=1))
    bias = doubled(bias_ref)
    energy = doubled(energy_ref)
    for level in range(SIDE):
        window = level_rows(level)
        joined = jnp.concatenate(
            [inner_rows(one_ref, level) + rows_ref[window], inner_rows(sum_ref, level)], axis=1
        )
        act = dot_split(joined, act_high, act_low) + bias
        sig = 1.0 / (1.0 + jnp.exp(-act))
        weighted = live_ref[window] * energy * sig
        packed_ref[window] = weighted * act
        grads = dot_split(weighted * (1.0 + act * (1.0 - sig)), grad_high, grad_low)
        rows_ref[window] = grads[:, :128]
        set_level(two_ref, level, grads[:, 128:])
    own_energy = packed_ref[pl.ds(0, slots, stride=planes), :]
    first_half = jnp.where(iota((8, 128), 1) < chan, 1.0, 0.0)
    energy_high, energy_low = split(own_energy)
    first_half = first_half.astype(bf16)
    site_energy = (dot(first_half, energy_high, nt) + dot(first_half, energy_low, nt))[0:1]
    fill_ghosts(two_ref)
    start_structure()
    own_ref[1, 0:slots] = rows_ref[pl.ds(0, slots, stride=planes), :]
    two_cells = cells_of(two_ref)
    convolve(filters_ref, 1, two_ref, sum_ref, step_structure)
    back = parts_ref[...] * gain_ref[...]
    back_rows = back.astype(bf16)
    for level in range(SIDE):
        window = level_rows(level)
        set_level(
            sum_ref, level, rows_ref[window] + live_ref[window] * inner_rows(sum_ref, level)
        )
    fill_ghosts(sum_ref)
    sum_cells = cells_of(sum_ref)
    live_cells = jnp.where(own_ext[3:4] > 0, 1.0, 0.0)
    ring_long = (dot(back_rows, ring_ref[...]) * live_cells).T
    grad_cells = dot_split(sum_cells + ring_long, *split(mix_one_ref[...].T * pair_scale))

    def crossed(value):
        value = value.T.reshape(waves // 8, 2, 8, chan)
        value = jnp.concatenate([value[:, 1:2], -value[:, 0:1]], axis=1).reshape(table, chan)
        return jnp.concatenate([value, jnp.zeros((table, chan), f32)], axis=1).astype(bf16)

    response = dot(crossed(filtered), own_ref[1].astype(bf16), nt) + dot(
        crossed(back), own_ref[0].astype(bf16), nt
    )
    turning_high, turning_low = split(waves_ref[:, 0:pad].astype(f32) * response)
    spot = iota((8, table), 1)
    wave = spot // 16 * 8 + spot % 8

    def signed(index):
        return jnp.where(index % 2 == 1, (index + 1) // 2, -(index // 2))

    row = iota((8, table), 0)
    number = jnp.where(
        row == 0,
        wave % 8 + 1,
        jnp.where(row == 1, signed(wave // 72), jnp.where(row == 2, signed(wave // 8 % 9), 0)),
    )
    number = number.astype(f32).astype(bf16)
    scale_row = iota((8, 1), 0)
    scales = jnp.where(
        scale_row == 0,
        two_pi / (grid_dims[0] * domain_width),
        two_pi / (grid_dims[1] * domain_width),
    )
    long_force = (dot(number, turning_high) + dot(number, turning_low))[:, :slots] * scales

    zero_cells = saved_ref[0]
    one_cells = saved_ref[1]
    left = [
        jnp.concatenate([two_cells, one_cells], axis=1),
        jnp.concatenate([grad_cells, zero_cells], axis=1),
    ]
    right = jnp.concatenate(
        [
            jnp.concatenate([one_cells, two_cells], axis=1),
            jnp.concatenate([zero_cells, grad_cells], axis=1),
        ],
        axis=1,
    )
    left = jnp.concatenate(left, axis=1)
    for shift in range(3):
        moved = right if shift == 1 else pltpu.roll(right, (1 - shift) % cells, 0)
        shift_ref[shift, 0:cells] = moved
        shift_ref[shift, cells:] = moved[:reach]
    one, two = radial_one_ref[...], radial_two_ref[...]
    pairs = jnp.concatenate([two, two, one, one], axis=1)
    pairs = jnp.broadcast_to(pairs[:, None, :], (NBASIS, 16, pad)).reshape(128, pad).T
    pair_column = iota((pad, 128), 1) % 16
    shares = jnp.zeros((cells, 128), f32)
    for number, (ox, oy, oz) in enumerate(offsets):
        distance = (ox * ext + oy) * ext
        products = left * shift_ref[oz + 1, distance : distance + cells]
        chosen = jnp.where(pair_column == number, pairs, 0.0).astype(bf16)
        shares = shares + dot(products.astype(bf16), chosen)
    shares = shares.T
    sep = [get_sep(slice(16 * part, 16 * part + 16)) for part in range(3)]
    square = sep[0] * sep[0] + sep[1] * sep[1] + sep[2] * sep[2]
    length = jnp.sqrt(square)
    base = jnp.maximum(1.0 - square * (1.0 / (cutoff * cutoff)), 0.0)
    inward = length * base * (-4.0 / (cutoff * cutoff))
    outward = (-2.0 * gamma) * base * base
    strength = jnp.zeros((16, cells), f32)
    for number in range(NBASIS):
        gap = length - step * number
        slope = jnp.exp(-gamma * gap * gap) * (inward + gap * outward)
        strength = strength + slope * shares[16 * number : 16 * number + 16]
    strength = strength / length
    totals = []
    for part in range(3):
        force = jnp.where(iota((16, cells), 0) < half, sep[part] * strength, 0.0)
        total = -jnp.sum(force, axis=0, keepdims=True)
        for number, (ox, oy, oz) in enumerate(offsets):
            distance = (ox * ext + oy) * ext + oz
            total = total + pltpu.roll(force[number : number + 1], distance, 1)
        totals.append(total)
    total = jnp.concatenate(totals + [jnp.zeros((5, cells), f32)], axis=0)
    site_total = exact(total[:, :inner_lanes], picks, nt)
    lines = jnp.concatenate([-(site_total[0:3] + long_force[0:3]), site_energy], axis=0)
    lines = jnp.concatenate([lines, jnp.zeros((4, slots), f32)], axis=0)
    hot = (iota((slots, slots), 0) == site_of(coords_of(pos_ref))).astype(f32).astype(bf16)
    lines = exact(lines, hot)
    for axis in range(3):
        force_out[0, 0, axis] = lines[axis : axis + 1]
    energy_out[0, 0] = lines[3:4]


def kernel_params():
    return pltpu.CompilerParams(vmem_limit_bytes=56 * 1024 * 1024)


def whole_box(
    species,
    counts,
    positions,
    ghost_rows,
    neighbours,
    kvec,
    embed,
    radial_one,
    radial_two,
    mix_one,
    mix_two,
    lr_filter,
    read_weight,
    read_bias,
    energy_weight,
):
    axes = ("gx", "gy", "gz")
    vmem = pl.BlockSpec(memory_space=pltpu.VMEM)
    smem = pl.BlockSpec(memory_space=pltpu.SMEM)
    placed = pl.pallas_call(
        place_kernel,
        out_shape=jax.ShapeDtypeStruct((domains, 4, slots), f32),
        in_specs=[smem, vmem, vmem],
        out_specs=vmem,
    )(counts, positions.transpose(0, 1, 3, 2, 4), species)
    shared = lax.all_to_all(placed, axes, 0, 0, tiled=True)
    gain = pl.pallas_call(
        gain_kernel,
        out_shape=jax.ShapeDtypeStruct((chan, table), f32),
        in_specs=[vmem] * 2,
        out_specs=vmem,
    )(kvec, lr_filter)
    tables = (
        gain,
        embed,
        radial_one,
        radial_two,
        mix_one,
        mix_two,
        read_weight,
        read_bias.reshape(1, chan),
        energy_weight.reshape(1, chan),
    )
    energies, forces = box_call(shared, positions.transpose(0, 1, 3, 2, 4), tables)
    return (energies, forces.transpose(0, 1, 3, 2, 4))


def box_call(shared, coords, tables):
    vmem = pl.BlockSpec(memory_space=pltpu.VMEM)
    grid_shape = (ext, ext, ext, planes, 128)
    return pl.pallas_call(
        box_kernel,
        out_shape=(
            jax.ShapeDtypeStruct((1, 1, 1, slots), f32),
            jax.ShapeDtypeStruct((1, 1, 3, 1, slots), f32),
        ),
        in_specs=[vmem] * 11,
        out_specs=(vmem, vmem),
        scratch_shapes=[
            pltpu.VMEM((cells // 128, 64 * 16, 128), f32),
            pltpu.VMEM((64, pad), f32),
            pltpu.VMEM((2, rows_all, 128), f32),
            pltpu.VMEM((half, rows_all, pad), bf16),
            pltpu.VMEM((table, 2 * span), bf16),
            pltpu.VMEM((table, cells), bf16),
            pltpu.VMEM(grid_shape, f32),
            pltpu.VMEM(grid_shape, f32),
            pltpu.VMEM(grid_shape, f32),
            pltpu.VMEM((rows_all, 128), f32),
            pltpu.VMEM((2, pad, 128), f32),
            pltpu.VMEM((8, 2 * span), f32),
            pltpu.VMEM((rows_all, pad), bf16),
            pltpu.VMEM((2, cells, chan), f32),
            pltpu.VMEM((pad, pad), f32),
            pltpu.VMEM((3, cells + reach, 256), f32),
            pltpu.VMEM((chan, 2 * span), bf16),
            pltpu.VMEM((chan, table), f32),
        ],
        compiler_params=kernel_params(),
    )(shared, coords, *tables)


def solution(mesh):
    in_specs = (
        P(("group", "gx"), "gy", "gz", None),
        P(("group", "gx"), "gy", "gz"),
        P(("group", "gx"), "gy", "gz", None, None),
        P(("group", "gx"), "gy", "gz", None),
        P(("group", "gx"), "gy", "gz", None, None),
        P(),
        P(),
        P(),
        P(),
        P(),
        P(),
        P(),
        P(),
        P(),
        P(),
    )
    out_specs = (P(("group", "gx"), "gy", "gz", None), P(("group", "gx"), "gy", "gz", None, None))
    sizes = tuple(mesh.shape[axis] for axis in ("gx", "gy", "gz"))
    plan = whole_box if sizes == grid_dims else local
    return jax.shard_map(plan, mesh=mesh, in_specs=in_specs, out_specs=out_specs, check_vma=False)
```
